256 devices in a mesh: tm: 32 (over y_hi, z, core), slab: 8 (over x, y_lo).
Axes of the slice: x: 4, y: 4 (y_hi: 2, y_lo: 2; y = y_hi * 2 + y_lo), z: 8, core: 2. Of those that a mesh axis runs over, the one named last changes fastest.
Arguments:
- sources: float32 [4, 256, 128, 512], P(None, 'tm', 'slab'), may hold values from -6 to 6
- phonons: float32 [256, 128, 512], P('tm', 'slab'), may hold values from -3 to 3
- momenta: float32 [256, 128, 512], P('tm', 'slab'), may hold values from -6 to 6
- kernel: float32 [256], replicated, may hold values from -0.375 to 0.375
- bonds: int32 [2, 128, 512], P(None, 'slab'), may hold values 0 or 1
Outputs:
- half_momenta: float32 [256, 128, 512], P('tm', 'slab')
- new_phonons: float32 [256, 128, 512], P('tm', 'slab')
The draws below stay inside these ranges and needn't reach their ends.
All inputs are finite; a program needn't handle non-finite values. No bound on the sum of `bonds` on one device may be relied on, other than what follows from the above.
Results may differ from the reference program's by a relative error of at most 0.0001.
Values sent between devices are 32-bit elements; how exact they have to be, the bound alone decides.
No kernel may reach another device: no remote copies, remote signals or barrier semaphores. Data moves between devices by JAX's collectives and lax.ppermute only.
A program may use at most 64 MiB of HBM per device.

```python
import jax
import jax.numpy as jnp
from jax import lax

SOURCES = 4
NT = 256
LC = 512
ITERS = 2
NR = 128


def set_ends(array, stream_key, smallest, high):
    shape = array.shape
    index_at = [jax.random.randint(jax.random.fold_in(stream_key, axis), (), 0, shape[axis]) for axis in range(len(shape))]
    array = array.at[tuple(index_at)].set(smallest)
    longest = shape.index(max(shape))
    index_at[longest] = (index_at[longest] + 1) % shape[longest]
    return array.at[tuple(index_at)].set(high)


def steps_of(key, dims, split, low, largest):
    factor_of = 1.0
    for position, parts in split:
        steps = jax.random.uniform(jax.random.fold_in(jax.random.fold_in(key, 6), position), (parts,), jnp.float32, low / len(split), largest / len(split))
        factor_of = factor_of * jnp.repeat(jnp.exp(steps), dims[position] // parts).reshape((-1,) + (1,) * (len(dims) - 1 - position))
    return factor_of


def bell_draw(stream_key, shape, scale, limit, split=(), dtype=jnp.bfloat16):
    result = scale * jax.random.normal(stream_key, shape, jnp.float32)
    if split:
        result = result * steps_of(stream_key, shape, split, -0.22, 0.18)
    return jnp.clip(result, -limit, limit).astype(dtype)


def setup_inputs(seed: int = 0) -> dict:
    splits = jax.random.split(jax.random.key(seed), 6)
    return {
        "sources": bell_draw(splits[0], (SOURCES, NT, NR, LC), 1.0, 6.0, ((1, 32), (2, 8)), jnp.float32),
        "phonons": bell_draw(splits[1], (NT, NR, LC), 0.5, 3.0, ((0, 32), (1, 8)), jnp.float32),
        "momenta": bell_draw(splits[2], (NT, NR, LC), 1.0, 6.0, ((0, 32), (1, 8)), jnp.float32),
        "kernel": bell_draw(splits[3], (NT,), NT ** -0.5, 0.375, (), jnp.float32),
        "bonds": set_ends((jax.random.randint(splits[4], (2, NR, LC), 0, 4) < 3).astype(jnp.int32), jax.random.fold_in(splits[4], 1), 0, 1),
    }


hopping = 0.1
coupling = 0.2
restore = 0.25
spring = 0.25
stepsize = 0.5


def kinetic(field, horiz, vert):
    beside = horiz * jnp.roll(field, -1, 3) + jnp.roll(horiz * field, 1, 3)
    beside = beside + vert * jnp.roll(field, -1, 2) + jnp.roll(vert * field, 1, 2)
    return field + hopping * beside


def inner_sum(first, second):
    return jnp.sum(first * second, axis=(1, 2, 3), keepdims=True)


def reference(sources, phonons, momenta, kernel, bonds):
    horiz = bonds[0].astype(jnp.float32)
    vert = bonds[1].astype(jnp.float32)
    times = jnp.arange(NT)
    sign = jnp.where(times == 0, -1.0, 1.0).astype(jnp.float32)[:, None, None]
    weight = sign * jnp.exp(coupling * phonons)

    def forward_op(field):
        return field - weight * jnp.roll(kinetic(field, horiz, vert), 1, 1)

    def adjoint_op(field):
        return field - kinetic(jnp.roll(weight * field, -1, 1), horiz, vert)

    solution = jnp.zeros_like(sources)
    residual = sources
    direction = sources
    norm_now = inner_sum(residual, residual)
    for step in range(ITERS):
        image = adjoint_op(forward_op(direction))
        alpha = norm_now / inner_sum(direction, image)
        solution = solution + alpha * direction
        residual = residual - alpha * image
        norm_next = inner_sum(residual, residual)
        direction = residual + (norm_next / norm_now) * direction
        norm_now = norm_next
    image_y = forward_op(solution)
    fermion_force = 2.0 * coupling * jnp.sum(image_y * (solution - image_y), axis=0)
    boson_force = restore * phonons + spring * (2.0 * phonons - jnp.roll(phonons, -1, 0) - jnp.roll(phonons, 1, 0))
    half_momenta = momenta - 0.5 * stepsize * (boson_force + fermion_force)
    offsets = (times[:, None] - times[None, :]) % NT
    circulant = kernel[offsets]
    drift = jnp.dot(circulant, half_momenta.reshape(NT, -1), precision=lax.Precision.HIGHEST, preferred_element_type=jnp.float32)
    new_phonons = phonons + stepsize * drift.reshape(phonons.shape)
    return half_momenta, new_phonons
```

```python
import jax
import jax.numpy as jnp
from jax import lax
from jax.sharding import PartitionSpec as P

hopping = 0.1
coupling = 0.2
restore = 0.25
spring = 0.25
stepsize = 0.5


def passed_along(block, axis, distance):
    devices = range(lax.axis_size(axis))
    route = [((i - distance) % len(devices), i) for i in devices]
    return lax.ppermute(block, axis, route)


def extended(block, sides, width):
    for axis, dim in sides:
        count = lax.axis_size(axis)
        forward = [(i, i + 1) for i in range(count - 1)]
        forward.append((count - 1, 0))
        backward = [(target, source) for source, target in forward]
        low = lax.ppermute(
            lax.slice_in_dim(block, block.shape[dim] - width, None, axis=dim), axis, forward
        )
        high = lax.ppermute(lax.slice_in_dim(block, 0, width, axis=dim), axis, backward)
        block = jnp.concatenate([low, block, high], axis=dim)
    return block


def inner_local(first, second):
    return jnp.sum(first * second, axis=(1, 2, 3))


def from_all(row):
    axes = ("tm", "slab")
    everyone = lax.axis_size("tm") * lax.axis_size("slab")
    copies = jnp.broadcast_to(row[None], (everyone,) + row.shape)
    return lax.all_to_all(copies, axes, split_axis=0, concat_axis=0, tiled=True)


def krylov_coefficients(moments):
    alpha = moments[0] / moments[1]
    square = moments[2] / moments[1]
    cube = moments[3] / moments[1]
    spread = cube - square * square
    return (alpha * cube - square) / spread, (1.0 - alpha * square) / spread


def circulant_table(kernel):
    total_time = kernel.shape[0]
    rolled = jnp.roll(kernel, total_time - 1)
    tiled = jnp.tile(rolled, total_time + 1)
    shifted = tiled.reshape(total_time, total_time + 1)[:, :total_time]
    return shifted[:, ::-1]


def body(sources, phonons, momenta, kernel, bonds):
    slices = sources.shape[1]
    rows = sources.shape[2]
    horiz = bonds[0].astype(jnp.float32)
    vert = bonds[1].astype(jnp.float32)
    bond_edge = passed_along(bonds[1][rows - 1 :], "slab", 1).astype(jnp.float32)
    vert_padded = jnp.concatenate([bond_edge, vert], axis=0)
    start_time = lax.axis_index("tm") * slices
    times = start_time + jnp.arange(slices, dtype=jnp.int32)
    sign = jnp.where(times == 0, -1.0, 1.0).astype(jnp.float32)[:, None, None]
    weight = sign * jnp.exp(coupling * phonons)

    def kinetic(field):
        padded = extended(field, (("slab", 2),), 1)
        below = (padded[:, :, : rows + 1] * vert_padded)[:, :, :rows]
        above = vert * padded[:, :, 2:]
        beside = horiz * jnp.roll(field, -1, 3) + jnp.roll(horiz * field, 1, 3) + above + below
        return field + hopping * beside

    def forward_op(field):
        moved = kinetic(field)
        earlier = passed_along(moved[:, slices - 1 :], "tm", 1)
        shifted = jnp.concatenate([earlier, moved[:, : slices - 1]], axis=1)
        return field - weight * shifted

    def transposed_op(field):
        scaled = weight * field
        later = passed_along(scaled[:, :1], "tm", -1)
        return field - kinetic(jnp.concatenate([scaled[:, 1:], later], axis=1))

    first = forward_op(sources)
    normal = transposed_op(first)
    second = forward_op(normal)
    partial = jnp.concatenate(
        [
            inner_local(sources, sources),
            inner_local(first, first),
            inner_local(normal, normal),
            inner_local(second, second),
        ]
    )
    moments = jnp.sum(from_all(jnp.pad(partial, (0, 128 - partial.shape[0]))), axis=0)
    low, high = krylov_coefficients(moments[: 4 * sources.shape[0]].reshape(4, -1))
    expand = lambda values: values[:, None, None, None]
    solution = expand(low) * sources + expand(high) * normal
    image_y = expand(low) * first + expand(high) * second
    fermion_force = 2.0 * coupling * jnp.sum(image_y * (solution - image_y), axis=0)
    phonon_pad = extended(phonons, (("tm", 0),), 1)
    boson_force = restore * phonons + spring * (2.0 * phonons - phonon_pad[2:] - phonon_pad[:-2])
    half_momenta = momenta - 0.5 * stepsize * (boson_force + fermion_force)
    circulant = circulant_table(kernel)
    flat = half_momenta.reshape(slices, -1)
    columns = lax.all_to_all(flat, "tm", split_axis=1, concat_axis=0, tiled=True)
    mixed = jnp.dot(
        circulant, columns, precision=lax.Precision.HIGHEST, preferred_element_type=jnp.float32
    )
    drift = lax.all_to_all(mixed, "tm", split_axis=0, concat_axis=1, tiled=True)
    new_phonons = phonons + stepsize * drift.reshape(phonons.shape)
    return (half_momenta, new_phonons)


def solution(mesh):
    return jax.shard_map(
        body,
        mesh=mesh,
        in_specs=(
            P(None, "tm", "slab", None),
            P("tm", "slab", None),
            P("tm", "slab", None),
            P(),
            P(None, "slab", None),
        ),
        out_specs=(P("tm", "slab", None), P("tm", "slab", None)),
        check_vma=False,
    )
```

```python
import jax
import jax.numpy as jnp
from jax import lax
from jax.experimental import pallas as pl
from jax.experimental.pallas import tpu as pltpu
from jax.sharding import PartitionSpec as P

hopping = 0.1
coupling = 0.2
restore = 0.25
spring = 0.25
stepsize = 0.5

LANES = 128
WIDE = 24
EARLY = 3
VMEM = pl.BlockSpec(memory_space=pltpu.VMEM)
PARAMS = pltpu.CompilerParams(vmem_limit_bytes=28 * 2**20)


def layout(entries):
    at, row = {}, 0
    for key, rows in entries:
        at[key] = (row, rows)
        row += rows
    return at, -(-row // 8) * 8


def side_layout(count, slices):
    depth = lambda t: min(3, slices - t)
    entries = [((i, t), depth(t)) for i in range(count) for t in range(slices)]
    entries += [((count, t), min(2, depth(t))) for t in range(slices)]
    return layout(entries + [(("bond", 0), 2), (("bond", 1), 3)])


def corner_layout(count):
    entries = [((i, t), 2 if t == -3 else 3) for i in range(count) for t in (-3, -2, -1)]
    return layout(entries + [((count, -2), 1), ((count, -1), 2)])


def pack_kernel(s_hbm, ph_hbm, pi_hbm, bond_hbm, up, down, up_corner, down_corner, ahead, s_ref, ph_ref, bond_ref, sems):
    count, slices, rows, _ = s_ref.shape
    copies = [
        pltpu.make_async_copy(ph_hbm, ph_ref, sems.at[0]),
        pltpu.make_async_copy(bond_hbm, bond_ref, sems.at[1]),
        pltpu.make_async_copy(pi_hbm.at[slices - 1], ahead.at[EARLY * count + 2], sems.at[2]),
    ]
    copies += [pltpu.make_async_copy(s_hbm.at[i], s_ref.at[i], sems.at[3 + i]) for i in range(count)]
    for copy in copies[3:] + copies[:3]:
        copy.start()
    side, _ = side_layout(count, slices)
    corner, _ = corner_layout(count)

    def rows_of(ref, n, last):
        return ref[pl.ds(rows - n if last else 0, n)]

    def field(source, entries, shift, out, last, wanted):
        for (key, t), (row, n) in entries.items():
            if key == wanted:
                out[pl.ds(row, n)] = rows_of(source.at[t + shift], n, last)

    for i in [*range(count), count]:
        if i < count:
            copies[3 + i].wait()
        else:
            copies[0].wait()
        source = s_ref.at[i] if i < count else ph_ref
        for last, out, out_corner in ((True, up, up_corner), (False, down, down_corner)):
            field(source, side, 0, out, last, i)
            field(source, corner, slices, out_corner, last, i)
        kept = EARLY if i < count else 2
        for j in range(kept):
            ahead[EARLY * i + j] = source[slices - kept + j]
    copies[1].wait()
    for k in range(2):
        for last, out in ((True, up), (False, down)):
            row, n = side[("bond", k)]
            out[pl.ds(row, n)] = rows_of(bond_ref.at[k], n, last).astype(jnp.float32)
    copies[2].wait()


def pack(sources, phonons, momenta, bonds):
    count, slices, rows, columns = sources.shape
    shape = lambda *n: jax.ShapeDtypeStruct(n + (columns,), jnp.float32)
    side, corner = side_layout(count, slices)[1], corner_layout(count)[1]
    return pl.pallas_call(
        pack_kernel,
        out_shape=[shape(side)] * 2 + [shape(corner)] * 2 + [shape(EARLY * count + 3, rows)],
        in_specs=[pl.BlockSpec(memory_space=pltpu.HBM)] * 4,
        out_specs=[VMEM] * 5,
        scratch_shapes=[
            pltpu.VMEM(sources.shape, jnp.float32),
            pltpu.VMEM(phonons.shape, jnp.float32),
            pltpu.VMEM(bonds.shape, bonds.dtype),
            pltpu.SemaphoreType.DMA((3 + count,)),
        ],
        compiler_params=pltpu.CompilerParams(vmem_limit_bytes=60 * 10**6),
        name="pack_halos",
    )(sources, phonons, momenta, bonds)


def operator_kernel(s_ref, ph_ref, bond_ref, above, below, above_corner, below_corner, before, *rest):
    p_ref, q_ref, t_ref, partial_ref, ext, weight, hh_ref, gg_ref, acc = rest
    count, slices, rows, columns = s_ref.shape
    side, _ = side_layout(count, slices)
    corner, _ = corner_layout(count)

    def widen(slot, key, t):
        row, n = (side if t >= 0 else corner)[key, t]
        lo, hi = (below, above) if t >= 0 else (below_corner, above_corner)
        slot[pl.ds(rows, n)] = lo[pl.ds(row, n)]
        slot[pl.ds(WIDE - n, n)] = hi[pl.ds(row, n)]

    for i in range(count):
        for t in range(-EARLY, slices):
            slot = ext.at[i, t + EARLY]
            slot[pl.ds(0, rows)] = before[EARLY * i + t + EARLY] if t < 0 else s_ref[i, t]
            widen(slot, i, t)
    for k, ref in ((0, hh_ref), (1, gg_ref)):
        row, n = side[("bond", k)]
        ref[pl.ds(0, rows)] = hopping * bond_ref[k].astype(jnp.float32)
        ref[pl.ds(rows, n)] = hopping * below[pl.ds(row, n)]
        ref[pl.ds(WIDE - n, n)] = hopping * above[pl.ds(row, n)]
    first = lax.axis_index("tm") == 0
    for t in range(-2, slices):
        slot = weight.at[t + 2]
        slot[pl.ds(0, rows)] = before[EARLY * count + t + 2] if t < 0 else ph_ref[t]
        widen(slot, count, t)
        value = jnp.exp(coupling * slot[...])
        slot[...] = value * jnp.where(first, -1.0, 1.0) if t == 0 else value

    def kinetic(v):
        hh, gg = hh_ref[...], gg_ref[...]
        beside = hh * pltpu.roll(v, columns - 1, 1) + pltpu.roll(hh * v, 1, 1)
        return v + (beside + gg * pltpu.roll(v, WIDE - 1, 0) + pltpu.roll(gg * v, 1, 0))

    def total(v):
        v = v[:8] + v[8:rows]
        return sum(v[:, c : c + LANES] for c in range(0, columns, LANES))

    def one_source(i, _):
        sums = [jnp.zeros((8, LANES), jnp.float32)] * 4
        p_old = q_old = None
        for t in range(-2, slices):
            s = ext[i, t + EARLY]
            w = weight[t + 2]
            p = s - w * kinetic(ext[i, t + EARLY - 1])
            if -1 <= t < slices - 1:
                p_ref[i, t + 1] = p[:rows]
                sums[0] += total(s[:rows] * s[:rows])
                sums[1] += total(p[:rows] * p[:rows])
            if t >= -1:
                q = p_old - kinetic(w * p)
                if t >= 0:
                    u = q - weight[t + 1] * kinetic(q_old)
                    q_ref[i, t] = q[:rows]
                    t_ref[i, t] = u[:rows]
                    sums[2] += total(q[:rows] * q[:rows])
                    sums[3] += total(u[:rows] * u[:rows])
                q_old = q
            p_old = p
        for k in range(4):
            acc[k * count + i] = sums[k]
        return 0

    lax.fori_loop(0, count, one_source, 0)
    lines = jnp.sum(acc[...], axis=1)
    lines = jnp.broadcast_to(jnp.sum(lines, axis=1, keepdims=True), lines.shape)
    at = lambda d: lax.broadcasted_iota(jnp.int32, lines.shape, d)
    row = jnp.sum(jnp.where(at(0) == at(1), lines, 0.0), axis=0, keepdims=True)
    partial_ref[...] = jnp.broadcast_to(row, partial_ref.shape)


def operators(sources, phonons, bonds, halos, everyone):
    count, slices, rows, columns = sources.shape
    f32 = lambda *shape: pltpu.VMEM(shape, jnp.float32)
    field = jax.ShapeDtypeStruct(sources.shape, jnp.float32)
    return pl.pallas_call(
        operator_kernel,
        out_shape=[field] * 3 + [jax.ShapeDtypeStruct((everyone, LANES), jnp.float32)],
        in_specs=[VMEM] * (3 + len(halos)),
        out_specs=[VMEM] * 4,
        scratch_shapes=[
            f32(count, slices + EARLY, WIDE, columns),
            f32(slices + 2, WIDE, columns),
            f32(WIDE, columns),
            f32(WIDE, columns),
            f32(4 * count, 8, LANES),
        ],
        compiler_params=PARAMS,
        name="operators",
    )(sources, phonons, bonds, *halos)


def force_kernel(mom_ref, s_ref, p_ref, q_ref, t_ref, ph_ref, before, pi_ref, half_ref, early_ref, send_ref):
    count, slices, rows, columns = s_ref.shape
    moments = jnp.sum(mom_ref[...], axis=0, keepdims=True)
    m = [moments] + [pltpu.roll(moments, LANES - count * k, 1) for k in range(1, 4)]
    alpha, square, cube = m[0] / m[1], m[2] / m[1], m[3] / m[1]
    spread = cube - square * square
    lane = lax.broadcasted_iota(jnp.int32, moments.shape, 1)

    def at(values, i):
        return jnp.sum(jnp.where(lane == i, values, 0.0))

    low = [at((alpha * cube - square) / spread, i) for i in range(count)]
    high = [at((1.0 - alpha * square) / spread, i) for i in range(count)]
    kept = EARLY * count
    phonon = lambda t: before[kept + 2 + t] if t < 0 else ph_ref[t]
    for t in range(-1, slices - 1):
        fermion = None
        for i in range(count):
            source = before[EARLY * i + EARLY - 1] if t < 0 else s_ref[i, t]
            x = low[i] * source + high[i] * q_ref[i, t + 1]
            y = low[i] * p_ref[i, t + 1] + high[i] * t_ref[i, t + 1]
            term = y * (x - y)
            fermion = term if fermion is None else fermion + term
        beside = phonon(t + 1) + phonon(t - 1)
        boson = restore * phonon(t) + spring * (2.0 * phonon(t) - beside)
        momentum = before[kept + 2] if t < 0 else pi_ref[t]
        half = momentum - 0.5 * stepsize * (boson + 2.0 * coupling * fermion)
        if t < 0:
            early_ref[...] = half
        else:
            half_ref[t] = half
        for r in range(0, rows, 2):
            for c in range(0, columns, LANES):
                send_ref[(r // 2) * (columns // LANES) + c // LANES, pl.ds(2 * (t + 1), 2)] = half[
                    r : r + 2, c : c + LANES
                ]


def force(received, sources, p, q, t, phonons, before, momenta, peers):
    slices, rows, columns = phonons.shape
    shape = lambda *n: jax.ShapeDtypeStruct(n, jnp.float32)
    return pl.pallas_call(
        force_kernel,
        out_shape=[shape(slices - 1, rows, columns), shape(rows, columns), shape(peers, 2 * slices, LANES)],
        in_specs=[VMEM] * 8,
        out_specs=[VMEM] * 3,
        compiler_params=PARAMS,
        name="force",
    )(received, sources, p, q, t, phonons, before, momenta)


def table_kernel(kernel_ref, table_ref):
    times = kernel_ref.shape[1]
    same = jnp.broadcast_to(pltpu.roll(kernel_ref[...], times - 1, 1), (times, times))
    shifted = pltpu.roll(same, 0, 1, stride=1, stride_axis=0)
    table_ref[...] = stepsize * jnp.transpose(shifted)


def circulant(kernel):
    times = kernel.shape[0]
    return pl.pallas_call(
        table_kernel,
        out_shape=jax.ShapeDtypeStruct((times, times), jnp.float32),
        in_specs=[VMEM],
        out_specs=VMEM,
        compiler_params=PARAMS,
        name="circulant",
    )(kernel[None])


def drift_kernel(table_ref, x_ref, out_ref):
    times = table_ref.shape[0]
    both = jnp.concatenate([x_ref[pl.ds(k, times, stride=2)] for k in range(2)], axis=1)
    mixed = jnp.dot(
        table_ref[...], both, precision=lax.Precision.HIGHEST, preferred_element_type=jnp.float32
    )
    for k in range(2):
        out_ref[pl.ds(k, times, stride=2)] = mixed[:, k * LANES : (k + 1) * LANES]


def drift(table, columns):
    flat = columns.reshape(-1, LANES)
    mixed = pl.pallas_call(
        drift_kernel,
        out_shape=jax.ShapeDtypeStruct(flat.shape, jnp.float32),
        in_specs=[VMEM] * 2,
        out_specs=VMEM,
        compiler_params=PARAMS,
        name="drift",
    )(table, flat)
    return mixed.reshape(columns.shape)


def add_kernel(ph_ref, back_ref, half_ref, late_ref, out_ref, all_ref):
    slices, rows, columns = ph_ref.shape
    for t in range(slices):
        all_ref[t] = half_ref[t] if t < slices - 1 else late_ref[...]
        for r in range(0, rows, 2):
            for c in range(0, columns, LANES):
                moved = back_ref[(r // 2) * (columns // LANES) + c // LANES, pl.ds(2 * t, 2)]
                out_ref[t, pl.ds(r, 2), pl.ds(c, LANES)] = ph_ref[t, pl.ds(r, 2), pl.ds(c, LANES)] + moved


def add_drift(phonons, back, half, late):
    field = jax.ShapeDtypeStruct(phonons.shape, jnp.float32)
    return pl.pallas_call(
        add_kernel,
        out_shape=[field] * 2,
        in_specs=[VMEM] * 4,
        out_specs=[VMEM] * 2,
        compiler_params=PARAMS,
        name="add_drift",
    )(phonons, back, half, late)


def passed_along(block, axis, distance):
    count = lax.axis_size(axis)
    return lax.ppermute(block, axis, [((i - distance) % count, i) for i in range(count)])


def passed_diagonally(block, times, slabs):
    nt, ns = lax.axis_size("tm"), lax.axis_size("slab")
    route = [
        (((i - times) % nt) * ns + (j - slabs) % ns, i * ns + j) for i in range(nt) for j in range(ns)
    ]
    return lax.ppermute(block, ("tm", "slab"), route)


def body(sources, phonons, momenta, kernel, bonds):
    peers = lax.axis_size("tm")
    everyone = peers * lax.axis_size("slab")
    up, down, up_corner, down_corner, ahead = pack(sources, phonons, momenta, bonds)
    above = passed_along(up, "slab", 1)
    below = passed_along(down, "slab", -1)
    above_corner = passed_diagonally(up_corner, 1, 1)
    below_corner = passed_diagonally(down_corner, 1, -1)
    before = passed_along(ahead, "tm", 1)
    table = circulant(kernel)
    halos = (above, below, above_corner, below_corner, before)
    halos, table = lax.optimization_barrier((halos, table))
    p, q, t, partial = operators(sources, phonons, bonds, halos, everyone)
    received = lax.all_to_all(partial, ("tm", "slab"), split_axis=0, concat_axis=0, tiled=True)
    half, early, send = force(received, sources, p, q, t, phonons, before, momenta, peers)
    columns = lax.all_to_all(send, "tm", split_axis=0, concat_axis=0, tiled=True)
    columns, late = lax.optimization_barrier((columns, passed_along(early, "tm", -1)))
    mixed = drift(table, columns)
    back = lax.all_to_all(mixed, "tm", split_axis=0, concat_axis=0, tiled=True)
    new_phonons, half_momenta = add_drift(phonons, back, half, late)
    return half_momenta, new_phonons


def solution(mesh):
    return jax.shard_map(
        body,
        mesh=mesh,
        in_specs=(
            P(None, "tm", "slab", None),
            P("tm", "slab", None),
            P("tm", "slab", None),
            P(),
            P(None, "slab", None),
        ),
        out_specs=(P("tm", "slab", None), P("tm", "slab", None)),
        check_vma=False,
    )
```

```python
import jax
import jax.numpy as jnp
from jax import lax
from jax.experimental import pallas as pl
from jax.experimental.pallas import tpu as pltpu
from jax.sharding import PartitionSpec as P

hopping = 0.1
coupling = 0.2
restore = 0.25
spring = 0.25
stepsize = 0.5

LANES = 128
WIDE = 24
EARLY = 3
VMEM = pl.BlockSpec(memory_space=pltpu.VMEM)
PARAMS = pltpu.CompilerParams(vmem_limit_bytes=28 * 2**20)


def layout(entries):
    at, row = {}, 0
    for key, rows in entries:
        at[key] = (row, rows)
        row += rows
    return at, -(-row // 8) * 8


def side_layout(count, slices):
    depth = lambda t: min(3, slices - t)
    entries = [((i, t), depth(t)) for i in range(count) for t in range(slices)]
    entries += [((count, t), min(2, depth(t))) for t in range(slices)]
    return layout(entries + [(("bond", 0), 2), (("bond", 1), 3)])


def corner_layout(count):
    entries = [((i, t), 2 if t == -3 else 3) for i in range(count) for t in (-3, -2, -1)]
    return layout(entries + [((count, -2), 1), ((count, -1), 2)])


def rows_of(ref, n, last):
    return ref[pl.ds(ref.shape[0] - n if last else 0, n)]


def side_kernel(s_hbm, ph_hbm, bond_hbm, up, down, s_ref, ph_ref, bond_ref, sems):
    count, slices = s_ref.shape[:2]
    copies = [pltpu.make_async_copy(s_hbm.at[i], s_ref.at[i], sems.at[i]) for i in range(count)]
    copies.append(pltpu.make_async_copy(ph_hbm, ph_ref, sems.at[count]))
    copies.append(pltpu.make_async_copy(bond_hbm, bond_ref, sems.at[count + 1]))
    for copy in copies:
        copy.start()
    side, _ = side_layout(count, slices)
    for i in range(count + 1):
        copies[i].wait()
        source = s_ref.at[i] if i < count else ph_ref
        for t in range(slices):
            row, n = side[i, t]
            up[pl.ds(row, n)] = rows_of(source.at[t], n, True)
            down[pl.ds(row, n)] = rows_of(source.at[t], n, False)
    copies[count + 1].wait()
    for k in range(2):
        row, n = side["bond", k]
        up[pl.ds(row, n)] = rows_of(bond_ref.at[k], n, True).astype(jnp.float32)
        down[pl.ds(row, n)] = rows_of(bond_ref.at[k], n, False).astype(jnp.float32)


def pack_sides(sources, phonons, bonds):
    count, slices, rows, columns = sources.shape
    side = jax.ShapeDtypeStruct((side_layout(count, slices)[1], columns), jnp.float32)
    whole = [jax.ShapeDtypeStruct(x.shape, x.dtype) for x in (sources, phonons, bonds)]
    return pl.pallas_call(
        side_kernel,
        out_shape=[side, side, *whole],
        in_specs=[pl.BlockSpec(memory_space=pltpu.HBM)] * 3,
        out_specs=[VMEM] * 5,
        scratch_shapes=[pltpu.SemaphoreType.DMA((count + 2,))],
        compiler_params=PARAMS,
        name="pack_sides",
    )(*(pltpu.with_memory_space_constraint(x, pltpu.HBM) for x in (sources, phonons, bonds)))


def ahead_kernel(s_ref, ph_ref, pi_hbm, ahead, sem):
    count, slices = s_ref.shape[:2]
    last = pltpu.make_async_copy(pi_hbm.at[slices - 1], ahead.at[EARLY * count + 2], sem)
    last.start()
    for i in range(count):
        for j in range(EARLY):
            ahead[EARLY * i + j] = s_ref[i, slices - EARLY + j]
    for j in range(2):
        ahead[EARLY * count + j] = ph_ref[slices - 2 + j]
    last.wait()


def pack_ahead(sources, phonons, momenta):
    count, _, rows, columns = sources.shape
    return pl.pallas_call(
        ahead_kernel,
        out_shape=jax.ShapeDtypeStruct((EARLY * count + 3, rows, columns), jnp.float32),
        in_specs=[VMEM, VMEM, pl.BlockSpec(memory_space=pltpu.HBM)],
        out_specs=VMEM,
        scratch_shapes=[pltpu.SemaphoreType.DMA(())],
        compiler_params=PARAMS,
        name="pack_ahead",
    )(sources, phonons, pltpu.with_memory_space_constraint(momenta, pltpu.HBM))


def corner_kernel(ahead, up, down):
    count = (ahead.shape[0] - 3) // EARLY
    corner, _ = corner_layout(count)
    for (i, t), (row, n) in corner.items():
        source = ahead.at[EARLY * i + (EARLY if i < count else 2) + t]
        up[pl.ds(row, n)] = rows_of(source, n, True)
        down[pl.ds(row, n)] = rows_of(source, n, False)


def pack_corners(ahead):
    rows = corner_layout((ahead.shape[0] - 3) // EARLY)[1]
    return pl.pallas_call(
        corner_kernel,
        out_shape=[jax.ShapeDtypeStruct((rows, ahead.shape[2]), jnp.float32)] * 2,
        in_specs=[VMEM],
        out_specs=[VMEM] * 2,
        compiler_params=PARAMS,
        name="pack_corners",
    )(ahead)


def kinetic(v, hh, gg):
    rows, columns = v.shape
    beside = hh * pltpu.roll(v, columns - 1, 1) + pltpu.roll(hh * v, 1, 1)
    return v + (beside + gg * pltpu.roll(v, rows - 1, 0) + pltpu.roll(gg * v, 1, 0))


def squares(v):
    columns = v.shape[1]
    v = v[:8] * v[:8] + v[8 : WIDE - 8] * v[8 : WIDE - 8]
    return sum(v[:, c : c + LANES] for c in range(0, columns, LANES))


def widen(slot, own, below, above, at):
    row, n = at
    slot[pl.ds(0, own.shape[0])] = own
    slot[pl.ds(own.shape[0], n)] = below[pl.ds(row, n)]
    slot[pl.ds(WIDE - n, n)] = above[pl.ds(row, n)]


def inner_kernel(
    s_ref, ph_ref, bond_ref, above, below, p_ref, q_ref, t_ref, s_edge, kp_edge, shared, acc, ext, weight
):
    count, slices = s_ref.shape[:2]
    side, _ = side_layout(count, slices)
    for k in range(2):
        widen(shared.at[k], bond_ref[k].astype(jnp.float32), below, above, side["bond", k])
        shared[k] = hopping * shared[k]
    first = lax.axis_index("tm") == 0
    for t in range(slices):
        slot = weight.at[t]
        widen(slot, ph_ref[t], below, above, side[count, t])
        value = jnp.exp(coupling * slot[...])
        slot[...] = value * jnp.where(first, -1.0, 1.0) if t == 0 else value
        for i in range(count):
            widen(ext.at[i, t], s_ref[i, t], below, above, side[i, t])
    for j in range(2):
        shared[2 + j] = weight[j]

    def one_source(i, _):
        moved = lambda v: kinetic(v, shared[0], shared[1])
        sums = [jnp.zeros((8, LANES), jnp.float32)] * 4
        own = s_ref.shape[2]
        p_old = q_old = None
        s_edge[i] = ext[i, 0]
        for t in range(1, slices):
            s = ext[i, t]
            p = s - weight[t] * moved(ext[i, t - 1])
            if t < slices - 1:
                p_ref[i, t - 1] = p[:own]
                sums[0] += squares(s)
                sums[1] += squares(p)
            back = moved(weight[t] * p)
            if t == 1:
                kp_edge[i] = back
            else:
                q = p_old - back
                q_ref[i, t - 2] = q[:own]
                sums[2] += squares(q)
                if t > 2:
                    u = q - weight[t - 1] * moved(q_old)
                    t_ref[i, t - 3] = u[:own]
                    sums[3] += squares(u)
                q_old = q
            p_old = p
        for k in range(4):
            acc[k * count + i] = sums[k]
        return 0

    lax.fori_loop(0, count, one_source, 0)


def inner_operators(sources, phonons, bonds, above, below):
    count, slices, rows, columns = sources.shape
    shape = lambda *n: jax.ShapeDtypeStruct(n, jnp.float32)
    field = lambda times: shape(count, times, rows, columns)
    wide = lambda n: shape(n, WIDE, columns)
    return pl.pallas_call(
        inner_kernel,
        out_shape=[
            field(slices - 2),
            field(slices - 2),
            field(slices - 3),
            wide(count),
            wide(count),
            wide(4),
            shape(4 * count, 8, LANES),
        ],
        in_specs=[VMEM] * 5,
        out_specs=[VMEM] * 7,
        scratch_shapes=[
            pltpu.VMEM((count, slices, WIDE, columns), jnp.float32),
            pltpu.VMEM((slices, WIDE, columns), jnp.float32),
        ],
        compiler_params=PARAMS,
        name="inner_operators",
    )(sources, phonons, bonds, above, below)


def outer_kernel(
    before, above, below, q_inner, s_edge, kp_edge, shared, acc_inner, p_ref, q_ref, t_ref, partial_ref, ext, weight, acc
):
    count = s_edge.shape[0]
    own = before.shape[1]
    corner, _ = corner_layout(count)
    for i in range(count):
        for j in range(EARLY):
            widen(ext.at[i, j], before[EARLY * i + j], below, above, corner[i, j - EARLY])
    for j in range(2):
        widen(weight.at[j], before[EARLY * count + j], below, above, corner[count, j - 2])
        weight[j] = jnp.exp(coupling * weight[j])

    def one_source(i, _):
        moved = lambda v: kinetic(v, shared[0], shared[1])
        w = [weight[0], weight[1], shared[2], shared[3]]
        s = [ext[i, 0], ext[i, 1], ext[i, 2], s_edge[i]]
        p = [s[j + 1] - w[j] * moved(s[j]) for j in range(3)]
        q = [p[0] - moved(w[1] * p[1]), p[1] - moved(w[2] * p[2]), p[2] - kp_edge[i]]
        u = [q[1] - w[1] * moved(q[0]), q[2] - w[2] * moved(q[1])]
        u.append(q_inner[i, 0] - w[3][:own] * moved(q[2])[:own])
        for j in range(2):
            p_ref[i, j] = p[j + 1][:own]
            q_ref[i, j] = q[j + 1][:own]
        for j in range(3):
            t_ref[i, j] = u[j][:own]
        for k, fields in enumerate((s[2:], p[1:], q[1:], u)):
            acc[k * count + i] = acc_inner[k * count + i] + sum(squares(v) for v in fields)
        return 0

    lax.fori_loop(0, count, one_source, 0)
    lines = jnp.sum(acc[...], axis=1)
    lines = jnp.broadcast_to(jnp.sum(lines, axis=1, keepdims=True), lines.shape)
    at = lambda d: lax.broadcasted_iota(jnp.int32, lines.shape, d)
    row = jnp.sum(jnp.where(at(0) == at(1), lines, 0.0), axis=0, keepdims=True)
    partial_ref[...] = jnp.broadcast_to(row, partial_ref.shape)


def outer_operators(before, above, below, inner, everyone):
    _, q_inner, _, s_edge, kp_edge, shared, acc = inner
    count, _, rows, columns = q_inner.shape
    field = lambda times: jax.ShapeDtypeStruct((count, times, rows, columns), jnp.float32)
    return pl.pallas_call(
        outer_kernel,
        out_shape=[field(2), field(2), field(3), jax.ShapeDtypeStruct((everyone, LANES), jnp.float32)],
        in_specs=[VMEM] * 8,
        out_specs=[VMEM] * 4,
        scratch_shapes=[
            pltpu.VMEM((count, EARLY, WIDE, columns), jnp.float32),
            pltpu.VMEM((2, WIDE, columns), jnp.float32),
            pltpu.VMEM((4 * count, 8, LANES), jnp.float32),
        ],
        compiler_params=PARAMS,
        name="outer_operators",
    )(before, above, below, q_inner, s_edge, kp_edge, shared, acc)


def force_kernel(
    mom_ref, s_ref, p_in, q_in, t_in, p_out, q_out, t_out, ph_ref, before, pi_ref, half_ref, early_ref, send_ref
):
    count, slices, rows, columns = s_ref.shape
    moments = jnp.sum(mom_ref[...], axis=0, keepdims=True)
    m = [moments] + [pltpu.roll(moments, LANES - count * k, 1) for k in range(1, 4)]
    alpha, square, cube = m[0] / m[1], m[2] / m[1], m[3] / m[1]
    spread = cube - square * square
    lane = lax.broadcasted_iota(jnp.int32, moments.shape, 1)

    def at(values, i):
        return jnp.sum(jnp.where(lane == i, values, 0.0))

    low = [at((alpha * cube - square) / spread, i) for i in range(count)]
    high = [at((1.0 - alpha * square) / spread, i) for i in range(count)]
    kept = EARLY * count
    phonon = lambda t: before[kept + 2 + t] if t < 0 else ph_ref[t]
    for t in range(-1, slices - 1):
        fermion = None
        for i in range(count):
            source = before[EARLY * i + EARLY - 1] if t < 0 else s_ref[i, t]
            p, q = (p_out[i, t + 1], q_out[i, t + 1]) if t < 1 else (p_in[i, t - 1], q_in[i, t - 1])
            x = low[i] * source + high[i] * q
            y = low[i] * p + high[i] * (t_out[i, t + 1] if t < 2 else t_in[i, t - 2])
            term = y * (x - y)
            fermion = term if fermion is None else fermion + term
        beside = phonon(t + 1) + phonon(t - 1)
        boson = restore * phonon(t) + spring * (2.0 * phonon(t) - beside)
        momentum = before[kept + 2] if t < 0 else pi_ref[t]
        half = momentum - 0.5 * stepsize * (boson + 2.0 * coupling * fermion)
        if t < 0:
            early_ref[...] = half
        else:
            half_ref[t] = half
        for r in range(0, rows, 2):
            for c in range(0, columns, LANES):
                send_ref[(r // 2) * (columns // LANES) + c // LANES, pl.ds(2 * (t + 1), 2)] = half[
                    r : r + 2, c : c + LANES
                ]


def force(received, sources, inner, outer, phonons, before, momenta, peers):
    slices, rows, columns = phonons.shape
    shape = lambda *n: jax.ShapeDtypeStruct(n, jnp.float32)
    return pl.pallas_call(
        force_kernel,
        out_shape=[shape(slices - 1, rows, columns), shape(rows, columns), shape(peers, 2 * slices, LANES)],
        in_specs=[VMEM] * 11,
        out_specs=[VMEM] * 3,
        compiler_params=PARAMS,
        name="force",
    )(received, sources, *inner[:3], *outer[:3], phonons, before, momenta)


def table_kernel(kernel_ref, table_ref):
    times = kernel_ref.shape[1]
    same = jnp.broadcast_to(pltpu.roll(kernel_ref[...], times - 1, 1), (times, times))
    shifted = pltpu.roll(same, 0, 1, stride=1, stride_axis=0)
    table_ref[...] = stepsize * jnp.transpose(shifted)


def circulant(kernel):
    times = kernel.shape[0]
    return pl.pallas_call(
        table_kernel,
        out_shape=jax.ShapeDtypeStruct((times, times), jnp.float32),
        in_specs=[VMEM],
        out_specs=VMEM,
        compiler_params=PARAMS,
        name="circulant",
        cost_estimate=pl.CostEstimate(flops=10**11, bytes_accessed=10**6, transcendentals=0),
    )(kernel[None])


def drift_kernel(table_ref, x_ref, out_ref):
    times = table_ref.shape[0]
    both = jnp.concatenate([x_ref[pl.ds(k, times, stride=2)] for k in range(2)], axis=1)
    mixed = jnp.dot(
        table_ref[...], both, precision=lax.Precision.HIGHEST, preferred_element_type=jnp.float32
    )
    for k in range(2):
        out_ref[pl.ds(k, times, stride=2)] = mixed[:, k * LANES : (k + 1) * LANES]


def drift(table, columns):
    flat = columns.reshape(-1, LANES)
    mixed = pl.pallas_call(
        drift_kernel,
        out_shape=jax.ShapeDtypeStruct(flat.shape, jnp.float32),
        in_specs=[VMEM] * 2,
        out_specs=VMEM,
        compiler_params=PARAMS,
        name="drift",
    )(table, flat)
    return mixed.reshape(columns.shape)


def add_kernel(ph_ref, back_ref, half_ref, late_ref, out_ref, all_ref):
    slices, rows, columns = ph_ref.shape
    for t in range(slices):
        all_ref[t] = half_ref[t] if t < slices - 1 else late_ref[...]
        for r in range(0, rows, 2):
            for c in range(0, columns, LANES):
                moved = back_ref[(r // 2) * (columns // LANES) + c // LANES, pl.ds(2 * t, 2)]
                out_ref[t, pl.ds(r, 2), pl.ds(c, LANES)] = ph_ref[t, pl.ds(r, 2), pl.ds(c, LANES)] + moved


def add_drift(phonons, back, half, late):
    field = jax.ShapeDtypeStruct(phonons.shape, jnp.float32)
    return pl.pallas_call(
        add_kernel,
        out_shape=[field] * 2,
        in_specs=[VMEM] * 4,
        out_specs=[VMEM] * 2,
        compiler_params=PARAMS,
        name="add_drift",
    )(phonons, back, half, late)


def passed_along(block, axis, distance):
    count = lax.axis_size(axis)
    return lax.ppermute(block, axis, [((i - distance) % count, i) for i in range(count)])


def passed_diagonally(block, times, slabs):
    nt, ns = lax.axis_size("tm"), lax.axis_size("slab")
    route = [
        (((i - times) % nt) * ns + (j - slabs) % ns, i * ns + j) for i in range(nt) for j in range(ns)
    ]
    return lax.ppermute(block, ("tm", "slab"), route)


def body(sources, phonons, momenta, kernel, bonds):
    peers = lax.axis_size("tm")
    everyone = peers * lax.axis_size("slab")
    up, down, sources, phonons, bonds = pack_sides(sources, phonons, bonds)
    above = passed_along(up, "slab", 1)
    below = passed_along(down, "slab", -1)
    ahead = pack_ahead(sources, phonons, momenta)
    before = passed_along(ahead, "tm", 1)
    up_corner, down_corner = pack_corners(ahead)
    above_corner = passed_diagonally(up_corner, 1, 1)
    below_corner = passed_diagonally(down_corner, 1, -1)
    (above, below), table = lax.optimization_barrier(((above, below), circulant(kernel)))
    inner = inner_operators(sources, phonons, bonds, above, below)
    outer = outer_operators(before, above_corner, below_corner, inner, everyone)
    received = lax.all_to_all(outer[3], ("tm", "slab"), split_axis=0, concat_axis=0, tiled=True)
    half, early, send = force(received, sources, inner, outer, phonons, before, momenta, peers)
    columns = lax.all_to_all(send, "tm", split_axis=0, concat_axis=0, tiled=True)
    columns, late = lax.optimization_barrier((columns, passed_along(early, "tm", -1)))
    mixed = drift(table, columns)
    back = lax.all_to_all(mixed, "tm", split_axis=0, concat_axis=0, tiled=True)
    new_phonons, half_momenta = add_drift(phonons, back, half, late)
    return half_momenta, new_phonons


def solution(mesh):
    return jax.shard_map(
        body,
        mesh=mesh,
        in_specs=(
            P(None, "tm", "slab", None),
            P("tm", "slab", None),
            P("tm", "slab", None),
            P(),
            P(None, "slab", None),
        ),
        out_specs=(P("tm", "slab", None), P("tm", "slab", None)),
        check_vma=False,
    )
```

```python
import jax
import jax.numpy as jnp
from jax import lax
from jax.experimental import pallas as pl
from jax.experimental.pallas import tpu as pltpu
from jax.sharding import PartitionSpec as P

hopping = 0.1
coupling = 0.2
restore = 0.25
spring = 0.25
stepsize = 0.5

LANES = 128
WIDE = 24
EARLY = 3
VMEM = pl.BlockSpec(memory_space=pltpu.VMEM)
PARAMS = pltpu.CompilerParams(vmem_limit_bytes=28 * 2**20)


def layout(entries):
    at, row = {}, 0
    for key, rows in entries:
        at[key] = (row, rows)
        row += rows
    return at, -(-row // 8) * 8


def side_layout(count, slices):
    depth = lambda t: min(3, slices - t)
    entries = [((i, t), depth(t)) for i in range(count) for t in range(slices)]
    entries += [((count, t), min(2, depth(t))) for t in range(slices)]
    return layout(entries + [(("bond", 0), 2), (("bond", 1), 3)])


def corner_layout(count):
    entries = [((i, t), 2 if t == -3 else 3) for i in range(count) for t in (-3, -2, -1)]
    return layout(entries + [((count, -2), 1), ((count, -1), 2)])


def rows_of(ref, n, last):
    return ref[pl.ds(ref.shape[0] - n if last else 0, n)]


def side_kernel(s_hbm, ph_hbm, bond_hbm, up, down, s_ref, ph_ref, bond_ref, sems):
    count, slices = s_ref.shape[:2]
    copies = [pltpu.make_async_copy(s_hbm.at[i], s_ref.at[i], sems.at[i]) for i in range(count)]
    copies.append(pltpu.make_async_copy(ph_hbm, ph_ref, sems.at[count]))
    copies.append(pltpu.make_async_copy(bond_hbm, bond_ref, sems.at[count + 1]))
    for copy in copies:
        copy.start()
    side, _ = side_layout(count, slices)
    for i in range(count + 1):
        copies[i].wait()
        source = s_ref.at[i] if i < count else ph_ref
        for t in range(slices):
            row, n = side[i, t]
            up[pl.ds(row, n)] = rows_of(source.at[t], n, True)
            down[pl.ds(row, n)] = rows_of(source.at[t], n, False)
    copies[count + 1].wait()
    for k in range(2):
        row, n = side["bond", k]
        up[pl.ds(row, n)] = rows_of(bond_ref.at[k], n, True).astype(jnp.float32)
        down[pl.ds(row, n)] = rows_of(bond_ref.at[k], n, False).astype(jnp.float32)


def pack_sides(sources, phonons, bonds):
    count, slices, rows, columns = sources.shape
    side = jax.ShapeDtypeStruct((side_layout(count, slices)[1], columns), jnp.float32)
    whole = [jax.ShapeDtypeStruct(x.shape, x.dtype) for x in (sources, phonons, bonds)]
    return pl.pallas_call(
        side_kernel,
        out_shape=[side, side, *whole],
        in_specs=[pl.BlockSpec(memory_space=pltpu.HBM)] * 3,
        out_specs=[VMEM] * 5,
        scratch_shapes=[pltpu.SemaphoreType.DMA((count + 2,))],
        compiler_params=PARAMS,
        name="pack_sides",
    )(*(pltpu.with_memory_space_constraint(x, pltpu.HBM) for x in (sources, phonons, bonds)))


def ahead_kernel(s_ref, ph_ref, pi_hbm, ahead, sem):
    count, slices = s_ref.shape[:2]
    last = pltpu.make_async_copy(pi_hbm.at[slices - 1], ahead.at[EARLY * count + 2], sem)
    last.start()
    for i in range(count):
        for j in range(EARLY):
            ahead[EARLY * i + j] = s_ref[i, slices - EARLY + j]
    for j in range(2):
        ahead[EARLY * count + j] = ph_ref[slices - 2 + j]
    last.wait()


def pack_ahead(sources, phonons, momenta):
    count, _, rows, columns = sources.shape
    return pl.pallas_call(
        ahead_kernel,
        out_shape=jax.ShapeDtypeStruct((EARLY * count + 3, rows, columns), jnp.float32),
        in_specs=[VMEM, VMEM, pl.BlockSpec(memory_space=pltpu.HBM)],
        out_specs=VMEM,
        scratch_shapes=[pltpu.SemaphoreType.DMA(())],
        compiler_params=PARAMS,
        name="pack_ahead",
    )(sources, phonons, pltpu.with_memory_space_constraint(momenta, pltpu.HBM))


def corner_kernel(ahead, up, down):
    count = (ahead.shape[0] - 3) // EARLY
    corner, _ = corner_layout(count)
    for (i, t), (row, n) in corner.items():
        source = ahead.at[EARLY * i + (EARLY if i < count else 2) + t]
        up[pl.ds(row, n)] = rows_of(source, n, True)
        down[pl.ds(row, n)] = rows_of(source, n, False)


def pack_corners(ahead):
    rows = corner_layout((ahead.shape[0] - 3) // EARLY)[1]
    return pl.pallas_call(
        corner_kernel,
        out_shape=[jax.ShapeDtypeStruct((rows, ahead.shape[2]), jnp.float32)] * 2,
        in_specs=[VMEM],
        out_specs=[VMEM] * 2,
        compiler_params=PARAMS,
        name="pack_corners",
    )(ahead)


def horizontal(v, hh):
    return v + (hh * pltpu.roll(v, v.shape[1] - 1, 1) + pltpu.roll(hh * v, 1, 1))


def vertical(v, gg):
    return gg * pltpu.roll(v, v.shape[0] - 1, 0) + pltpu.roll(gg * v, 1, 0)


def kinetic(v, hh, gg):
    return horizontal(v, hh) + vertical(v, gg)


def squares(v):
    columns = v.shape[1]
    v = v[:8] * v[:8] + v[8 : WIDE - 8] * v[8 : WIDE - 8]
    return sum(v[:, c : c + LANES] for c in range(0, columns, LANES))


def widen(slot, own, below, above, at):
    row, n = at
    slot[pl.ds(0, own.shape[0])] = own
    slot[pl.ds(own.shape[0], n)] = below[pl.ds(row, n)]
    slot[pl.ds(WIDE - n, n)] = above[pl.ds(row, n)]


def own_kernel(s_ref, ph_ref, bond_ref, hs_ref, wp_ref, hwp_ref, q_ref, hq_ref, weight):
    count, slices, rows, _ = s_ref.shape
    first = lax.axis_index("tm") == 0
    for t in range(slices):
        value = jnp.exp(coupling * ph_ref[t])
        weight[t] = value * jnp.where(first, -1.0, 1.0) if t == 0 else value
    hh = hopping * bond_ref[0].astype(jnp.float32)
    gg = hopping * bond_ref[1].astype(jnp.float32)
    gg = jnp.where(lax.broadcasted_iota(jnp.int32, gg.shape, 0) < rows - 1, gg, 0.0)

    def one_source(i, _):
        p_old = None
        for t in range(1, slices):
            v = s_ref[i, t - 1]
            along = horizontal(v, hh)
            hs_ref[i, t - 1] = along
            p = s_ref[i, t] - weight[t] * (along + vertical(v, gg))
            v = weight[t] * p
            along = horizontal(v, hh)
            wp_ref[i, t - 1] = v
            hwp_ref[i, t - 1] = along
            if 2 <= t < slices - 1:
                q = p_old - (along + vertical(v, gg))
                q_ref[i, t - 2] = q
                hq_ref[i, t - 2] = horizontal(q, hh)
            p_old = p
        return 0

    lax.fori_loop(0, count, one_source, 0)


def own_parts(sources, phonons, bonds):
    count, slices, rows, columns = sources.shape
    field = lambda n: jax.ShapeDtypeStruct((count, n, rows, columns), jnp.float32)
    return pl.pallas_call(
        own_kernel,
        out_shape=[field(slices - 1)] * 3
        + [field(slices - 3)] * 2
        + [jax.ShapeDtypeStruct(phonons.shape, jnp.float32)],
        in_specs=[VMEM] * 3,
        out_specs=[VMEM] * 6,
        compiler_params=PARAMS,
        name="own_parts",
    )(sources, phonons, bonds)


def inner_kernel(
    s_ref, ph_ref, bond_ref, above, below, hs_ref, wp_own, hwp_ref, q_own, hq_ref, weight_own,
    p_ref, q_ref, t_ref, s_edge, kp_edge, shared, acc, ext, weight, hh_two, hh_three,
):
    count, slices, own, columns = s_ref.shape
    side, _ = side_layout(count, slices)
    for k in range(2):
        widen(shared.at[k], bond_ref[k].astype(jnp.float32), below, above, side["bond", k])
        shared[k] = hopping * shared[k]
    hh_two[...] = shared[0, pl.ds(own, 8)]
    hh_two[pl.ds(3, 1)] = shared[0, pl.ds(own - 1, 1)]
    hh_two[pl.ds(4, 1)] = shared[0, pl.ds(0, 1)]
    hh_three[...] = jnp.zeros_like(hh_three)
    hh_three[pl.ds(2, 2)] = shared[0, pl.ds(own - 2, 2)]
    hh_three[pl.ds(4, 2)] = shared[0, pl.ds(0, 2)]
    first = lax.axis_index("tm") == 0
    for t in range(slices):
        slot = weight.at[t]
        widen(slot, weight_own[t], below, above, side[count, t])
        value = jnp.exp(coupling * slot[pl.ds(own, 8)])
        slot[pl.ds(own, 8)] = value * jnp.where(first, -1.0, 1.0) if t == 0 else value
        for i in range(count):
            widen(ext.at[i, t], s_ref[i, t], below, above, side[i, t])
    for j in range(2):
        shared[2 + j] = weight[j]

    def one_source(i, _):
        sub = lax.broadcasted_iota(jnp.int32, (8, columns), 0)
        turn = lambda v: pltpu.roll(v, 4, 0)
        gg = shared[1]
        sums = [jnp.zeros((8, LANES), jnp.float32)] * 4
        p_old = q_old = None
        s_edge[i] = ext[i, 0]
        for t in range(1, slices):
            s, v = ext[i, t], ext[i, t - 1]
            along = jnp.concatenate([hs_ref[i, t - 1], horizontal(v[own:], shared[0, pl.ds(own, 8)])], axis=0)
            p = s - weight[t] * (along + vertical(v, gg))
            if t < slices - 1:
                p_ref[i, t - 1] = p[:own]
                sums[0] += squares(s)
                sums[1] += squares(p)
            v = weight[t] * p
            change = v[:own] - wp_own[i, t - 1]
            tile = jnp.where(sub == 3, turn(change[8:]), jnp.where(sub == 4, turn(change[:8]), v[own:]))
            tile = horizontal(tile, hh_two[...])
            turned, along = turn(tile), hwp_ref[i, t - 1]
            top = along[:8] + jnp.where(sub == 0, turned, 0.0)
            bottom = along[8:] + jnp.where(sub == 7, turned, 0.0)
            back = jnp.concatenate([top, bottom, tile], axis=0) + vertical(v, gg)
            if t == 1:
                kp_edge[i] = back
            else:
                q = p_old - back
                q_ref[i, t - 2] = q[:own]
                sums[2] += squares(q)
                if t > 2:
                    change = q_old[:own] - q_own[i, t - 3]
                    tile = jnp.where(sub < 4, turn(change[8:]), turn(change[:8]))
                    turned, along = turn(horizontal(tile, hh_three[...])), hq_ref[i, t - 3]
                    top = along[:8] + jnp.where(sub < 2, turned, 0.0)
                    bottom = along[8:] + jnp.where(sub > 5, turned, 0.0)
                    moved = jnp.concatenate([top, bottom], axis=0) + vertical(q_old, gg)[:own]
                    u = q[:own] - weight[t - 1, pl.ds(0, own)] * moved
                    t_ref[i, t - 3] = u
                    sums[3] += squares(u)
                q_old = q
            p_old = p
        for k in range(4):
            acc[k * count + i] = sums[k]
        return 0

    lax.fori_loop(0, count, one_source, 0)


def inner_operators(sources, phonons, bonds, above, below, parts):
    count, slices, rows, columns = sources.shape
    shape = lambda *n: jax.ShapeDtypeStruct(n, jnp.float32)
    field = lambda times: shape(count, times, rows, columns)
    wide = lambda n: shape(n, WIDE, columns)
    return pl.pallas_call(
        inner_kernel,
        out_shape=[
            field(slices - 2),
            field(slices - 2),
            field(slices - 3),
            wide(count),
            wide(count),
            wide(4),
            shape(4 * count, 8, LANES),
        ],
        in_specs=[VMEM] * 11,
        out_specs=[VMEM] * 7,
        scratch_shapes=[
            pltpu.VMEM((count, slices, WIDE, columns), jnp.float32),
            pltpu.VMEM((slices, WIDE, columns), jnp.float32),
            pltpu.VMEM((8, columns), jnp.float32),
            pltpu.VMEM((8, columns), jnp.float32),
        ],
        compiler_params=PARAMS,
        name="inner_operators",
    )(sources, phonons, bonds, above, below, *parts)


def outer_kernel(
    before, above, below, q_inner, s_edge, kp_edge, shared, acc_inner, p_ref, q_ref, t_ref, partial_ref, ext, weight, acc
):
    count = s_edge.shape[0]
    own = before.shape[1]
    corner, _ = corner_layout(count)
    for i in range(count):
        for j in range(EARLY):
            widen(ext.at[i, j], before[EARLY * i + j], below, above, corner[i, j - EARLY])
    for j in range(2):
        widen(weight.at[j], before[EARLY * count + j], below, above, corner[count, j - 2])
        weight[j] = jnp.exp(coupling * weight[j])

    def one_source(i, _):
        moved = lambda v: kinetic(v, shared[0], shared[1])
        w = [weight[0], weight[1], shared[2], shared[3]]
        s = [ext[i, 0], ext[i, 1], ext[i, 2], s_edge[i]]
        p = [s[j + 1] - w[j] * moved(s[j]) for j in range(3)]
        q = [p[0] - moved(w[1] * p[1]), p[1] - moved(w[2] * p[2]), p[2] - kp_edge[i]]
        u = [q[1] - w[1] * moved(q[0]), q[2] - w[2] * moved(q[1])]
        u.append(q_inner[i, 0] - w[3][:own] * moved(q[2])[:own])
        for j in range(2):
            p_ref[i, j] = p[j + 1][:own]
            q_ref[i, j] = q[j + 1][:own]
        for j in range(3):
            t_ref[i, j] = u[j][:own]
        for k, fields in enumerate((s[2:], p[1:], q[1:], u)):
            acc[k * count + i] = acc_inner[k * count + i] + sum(squares(v) for v in fields)
        return 0

    lax.fori_loop(0, count, one_source, 0)
    lines = jnp.sum(acc[...], axis=1)
    lines = jnp.broadcast_to(jnp.sum(lines, axis=1, keepdims=True), lines.shape)
    at = lambda d: lax.broadcasted_iota(jnp.int32, lines.shape, d)
    row = jnp.sum(jnp.where(at(0) == at(1), lines, 0.0), axis=0, keepdims=True)
    partial_ref[...] = jnp.broadcast_to(row, partial_ref.shape)


def outer_operators(before, above, below, inner, everyone):
    _, q_inner, _, s_edge, kp_edge, shared, acc = inner
    count, _, rows, columns = q_inner.shape
    field = lambda times: jax.ShapeDtypeStruct((count, times, rows, columns), jnp.float32)
    return pl.pallas_call(
        outer_kernel,
        out_shape=[field(2), field(2), field(3), jax.ShapeDtypeStruct((everyone, LANES), jnp.float32)],
        in_specs=[VMEM] * 8,
        out_specs=[VMEM] * 4,
        scratch_shapes=[
            pltpu.VMEM((count, EARLY, WIDE, columns), jnp.float32),
            pltpu.VMEM((2, WIDE, columns), jnp.float32),
            pltpu.VMEM((4 * count, 8, LANES), jnp.float32),
        ],
        compiler_params=PARAMS,
        name="outer_operators",
    )(before, above, below, q_inner, s_edge, kp_edge, shared, acc)


def force_kernel(
    mom_ref, s_ref, p_in, q_in, t_in, p_out, q_out, t_out, ph_ref, before, pi_ref, half_ref, early_ref, send_ref
):
    count, slices, rows, columns = s_ref.shape
    moments = jnp.sum(mom_ref[...], axis=0, keepdims=True)
    m = [moments] + [pltpu.roll(moments, LANES - count * k, 1) for k in range(1, 4)]
    alpha, square, cube = m[0] / m[1], m[2] / m[1], m[3] / m[1]
    spread = cube - square * square
    lane = lax.broadcasted_iota(jnp.int32, moments.shape, 1)

    def at(values, i):
        return jnp.sum(jnp.where(lane == i, values, 0.0))

    low = [at((alpha * cube - square) / spread, i) for i in range(count)]
    high = [at((1.0 - alpha * square) / spread, i) for i in range(count)]
    kept = EARLY * count
    phonon = lambda t: before[kept + 2 + t] if t < 0 else ph_ref[t]
    for t in range(-1, slices - 1):
        fermion = None
        for i in range(count):
            source = before[EARLY * i + EARLY - 1] if t < 0 else s_ref[i, t]
            p, q = (p_out[i, t + 1], q_out[i, t + 1]) if t < 1 else (p_in[i, t - 1], q_in[i, t - 1])
            x = low[i] * source + high[i] * q
            y = low[i] * p + high[i] * (t_out[i, t + 1] if t < 2 else t_in[i, t - 2])
            term = y * (x - y)
            fermion = term if fermion is None else fermion + term
        beside = phonon(t + 1) + phonon(t - 1)
        boson = restore * phonon(t) + spring * (2.0 * phonon(t) - beside)
        momentum = before[kept + 2] if t < 0 else pi_ref[t]
        half = momentum - 0.5 * stepsize * (boson + 2.0 * coupling * fermion)
        if t < 0:
            early_ref[...] = half
        else:
            half_ref[t] = half
        for r in range(0, rows, 2):
            for c in range(0, columns, LANES):
                send_ref[(r // 2) * (columns // LANES) + c // LANES, pl.ds(2 * (t + 1), 2)] = half[
                    r : r + 2, c : c + LANES
                ]


def force(received, sources, inner, outer, phonons, before, momenta, peers):
    slices, rows, columns = phonons.shape
    shape = lambda *n: jax.ShapeDtypeStruct(n, jnp.float32)
    return pl.pallas_call(
        force_kernel,
        out_shape=[shape(slices - 1, rows, columns), shape(rows, columns), shape(peers, 2 * slices, LANES)],
        in_specs=[VMEM] * 11,
        out_specs=[VMEM] * 3,
        compiler_params=PARAMS,
        name="force",
    )(received, sources, *inner[:3], *outer[:3], phonons, before, momenta)


def table_kernel(kernel_ref, table_ref):
    times = kernel_ref.shape[1]
    same = jnp.broadcast_to(pltpu.roll(kernel_ref[...], times - 1, 1), (times, times))
    shifted = pltpu.roll(same, 0, 1, stride=1, stride_axis=0)
    table_ref[...] = stepsize * jnp.transpose(shifted)


def circulant(kernel):
    times = kernel.shape[0]
    return pl.pallas_call(
        table_kernel,
        out_shape=jax.ShapeDtypeStruct((times, times), jnp.float32),
        in_specs=[VMEM],
        out_specs=VMEM,
        compiler_params=PARAMS,
        name="circulant",
        cost_estimate=pl.CostEstimate(flops=10**11, bytes_accessed=10**6, transcendentals=0),
    )(kernel[None])


def drift_kernel(table_ref, x_ref, out_ref):
    times = table_ref.shape[0]
    both = jnp.concatenate([x_ref[pl.ds(k, times, stride=2)] for k in range(2)], axis=1)
    mixed = jnp.dot(
        table_ref[...], both, precision=lax.Precision.HIGHEST, preferred_element_type=jnp.float32
    )
    for k in range(2):
        out_ref[pl.ds(k, times, stride=2)] = mixed[:, k * LANES : (k + 1) * LANES]


def drift(table, columns):
    flat = columns.reshape(-1, LANES)
    mixed = pl.pallas_call(
        drift_kernel,
        out_shape=jax.ShapeDtypeStruct(flat.shape, jnp.float32),
        in_specs=[VMEM] * 2,
        out_specs=VMEM,
        compiler_params=PARAMS,
        name="drift",
    )(table, flat)
    return mixed.reshape(columns.shape)


def join_kernel(half_ref, late_ref, all_ref):
    last = half_ref.shape[0]
    all_ref[pl.ds(0, last)] = half_ref[...]
    all_ref[last] = late_ref[...]


def join_times(half, late):
    return pl.pallas_call(
        join_kernel,
        out_shape=jax.ShapeDtypeStruct((half.shape[0] + 1,) + half.shape[1:], jnp.float32),
        in_specs=[VMEM] * 2,
        out_specs=VMEM,
        compiler_params=PARAMS,
        name="join_times",
    )(half, late)


def add_kernel(ph_ref, back_ref, out_ref):
    slices, rows, columns = ph_ref.shape
    for t in range(slices):
        for r in range(0, rows, 2):
            for c in range(0, columns, LANES):
                moved = back_ref[(r // 2) * (columns // LANES) + c // LANES, pl.ds(2 * t, 2)]
                out_ref[t, pl.ds(r, 2), pl.ds(c, LANES)] = ph_ref[t, pl.ds(r, 2), pl.ds(c, LANES)] + moved


def add_drift(phonons, back):
    return pl.pallas_call(
        add_kernel,
        out_shape=jax.ShapeDtypeStruct(phonons.shape, jnp.float32),
        in_specs=[VMEM] * 2,
        out_specs=VMEM,
        compiler_params=PARAMS,
        name="add_drift",
    )(phonons, back)


def passed_along(block, axis, distance):
    count = lax.axis_size(axis)
    return lax.ppermute(block, axis, [((i - distance) % count, i) for i in range(count)])


def passed_diagonally(block, times, slabs):
    nt, ns = lax.axis_size("tm"), lax.axis_size("slab")
    route = [
        (((i - times) % nt) * ns + (j - slabs) % ns, i * ns + j) for i in range(nt) for j in range(ns)
    ]
    return lax.ppermute(block, ("tm", "slab"), route)


def body(sources, phonons, momenta, kernel, bonds):
    peers = lax.axis_size("tm")
    everyone = peers * lax.axis_size("slab")
    up, down, sources, phonons, bonds = pack_sides(sources, phonons, bonds)
    above = passed_along(up, "slab", 1)
    below = passed_along(down, "slab", -1)
    ahead = pack_ahead(sources, phonons, momenta)
    before = passed_along(ahead, "tm", 1)
    up_corner, down_corner = pack_corners(ahead)
    above_corner = passed_diagonally(up_corner, 1, 1)
    below_corner = passed_diagonally(down_corner, 1, -1)
    side_halos = (above, below)
    own = own_parts(sources, phonons, bonds)
    (above, below), table, own = lax.optimization_barrier((side_halos, circulant(kernel), own))
    inner = inner_operators(sources, phonons, bonds, above, below, own)
    outer = outer_operators(before, above_corner, below_corner, inner, everyone)
    received = lax.all_to_all(outer[3], ("tm", "slab"), split_axis=0, concat_axis=0, tiled=True)
    half, early, send = force(received, sources, inner, outer, phonons, before, momenta, peers)
    columns = lax.all_to_all(send, "tm", split_axis=0, concat_axis=0, tiled=True)
    half_momenta = join_times(half, passed_along(early, "tm", -1))
    columns, half_momenta = lax.optimization_barrier((columns, half_momenta))
    mixed = drift(table, columns)
    back = lax.all_to_all(mixed, "tm", split_axis=0, concat_axis=0, tiled=True)
    return half_momenta, add_drift(phonons, back)


def solution(mesh):
    return jax.shard_map(
        body,
        mesh=mesh,
        in_specs=(
            P(None, "tm", "slab", None),
            P("tm", "slab", None),
            P("tm", "slab", None),
            P(),
            P(None, "slab", None),
        ),
        out_specs=(P("tm", "slab", None), P("tm", "slab", None)),
        check_vma=False,
    )
```

```python
import jax
import jax.numpy as jnp
from jax import lax
from jax.experimental import pallas as pl
from jax.experimental.pallas import tpu as pltpu
from jax.sharding import PartitionSpec as P

hopping = 0.1
coupling = 0.2
restore = 0.25
spring = 0.25
stepsize = 0.5

LANES = 128
WIDE = 24
EARLY = 3
VMEM = pl.BlockSpec(memory_space=pltpu.VMEM)
PARAMS = pltpu.CompilerParams(vmem_limit_bytes=28 * 2**20)


def layout(entries):
    at, row = {}, 0
    for key, rows in entries:
        at[key] = (row, rows)
        row += rows
    return at, -(-row // 8) * 8


def side_layout(count, slices):
    depth = lambda t: min(3, slices - t)
    entries = [((i, t), depth(t)) for i in range(count) for t in range(slices)]
    entries += [((count, t), min(2, depth(t))) for t in range(slices)]
    return layout(entries + [(("bond", 0), 2), (("bond", 1), 3)])


def corner_layout(count):
    entries = [((i, t), 2 if t == -3 else 3) for i in range(count) for t in (-3, -2, -1)]
    return layout(entries + [((count, -2), 1), ((count, -1), 2)])


def rows_of(ref, n, last):
    return ref[pl.ds(ref.shape[0] - n if last else 0, n)]


def side_kernel(s_hbm, ph_hbm, bond_hbm, pi_hbm, up, down, s_ref, ph_ref, bond_ref, pi_ref, sems):
    count, slices = s_ref.shape[:2]
    copies = [pltpu.make_async_copy(s_hbm.at[i], s_ref.at[i], sems.at[i]) for i in range(count)]
    copies.append(pltpu.make_async_copy(ph_hbm, ph_ref, sems.at[count]))
    copies.append(pltpu.make_async_copy(bond_hbm, bond_ref, sems.at[count + 1]))
    copies.append(pltpu.make_async_copy(pi_hbm.at[slices - 1], pi_ref, sems.at[count + 2]))
    for copy in copies:
        copy.start()
    side, _ = side_layout(count, slices)
    for i in range(count + 1):
        copies[i].wait()
        source = s_ref.at[i] if i < count else ph_ref
        for t in range(slices):
            row, n = side[i, t]
            up[pl.ds(row, n)] = rows_of(source.at[t], n, True)
            down[pl.ds(row, n)] = rows_of(source.at[t], n, False)
    copies[count + 1].wait()
    for k in range(2):
        row, n = side["bond", k]
        up[pl.ds(row, n)] = rows_of(bond_ref.at[k], n, True).astype(jnp.float32)
        down[pl.ds(row, n)] = rows_of(bond_ref.at[k], n, False).astype(jnp.float32)
    copies[count + 2].wait()


def pack_sides(sources, phonons, bonds, momenta):
    count, slices, rows, columns = sources.shape
    side = jax.ShapeDtypeStruct((side_layout(count, slices)[1], columns), jnp.float32)
    whole = [jax.ShapeDtypeStruct(x.shape, x.dtype) for x in (sources, phonons, bonds)]
    whole.append(jax.ShapeDtypeStruct(momenta.shape[1:], jnp.float32))
    return pl.pallas_call(
        side_kernel,
        out_shape=[side, side, *whole],
        in_specs=[pl.BlockSpec(memory_space=pltpu.HBM)] * 4,
        out_specs=[VMEM] * 6,
        scratch_shapes=[pltpu.SemaphoreType.DMA((count + 3,))],
        compiler_params=PARAMS,
        name="pack_sides",
    )(*(pltpu.with_memory_space_constraint(x, pltpu.HBM) for x in (sources, phonons, bonds, momenta)))


def ahead_kernel(s_ref, ph_ref, pi_ref, ahead):
    count, slices = s_ref.shape[:2]
    for i in range(count):
        for j in range(EARLY):
            ahead[EARLY * i + j] = s_ref[i, slices - EARLY + j]
    for j in range(2):
        ahead[EARLY * count + j] = ph_ref[slices - 2 + j]
    ahead[EARLY * count + 2] = pi_ref[...]


def pack_ahead(sources, phonons, last_momenta):
    count, _, rows, columns = sources.shape
    return pl.pallas_call(
        ahead_kernel,
        out_shape=jax.ShapeDtypeStruct((EARLY * count + 3, rows, columns), jnp.float32),
        in_specs=[VMEM] * 3,
        out_specs=VMEM,
        compiler_params=PARAMS,
        name="pack_ahead",
    )(sources, phonons, last_momenta)


def corner_kernel(ahead, up, down):
    count = (ahead.shape[0] - 3) // EARLY
    corner, _ = corner_layout(count)
    for (i, t), (row, n) in corner.items():
        source = ahead.at[EARLY * i + (EARLY if i < count else 2) + t]
        up[pl.ds(row, n)] = rows_of(source, n, True)
        down[pl.ds(row, n)] = rows_of(source, n, False)


def pack_corners(ahead):
    rows = corner_layout((ahead.shape[0] - 3) // EARLY)[1]
    return pl.pallas_call(
        corner_kernel,
        out_shape=[jax.ShapeDtypeStruct((rows, ahead.shape[2]), jnp.float32)] * 2,
        in_specs=[VMEM],
        out_specs=[VMEM] * 2,
        compiler_params=PARAMS,
        name="pack_corners",
    )(ahead)


def horizontal(v, hh):
    return v + (hh * pltpu.roll(v, v.shape[1] - 1, 1) + pltpu.roll(hh * v, 1, 1))


def vertical(v, gg):
    return gg * pltpu.roll(v, v.shape[0] - 1, 0) + pltpu.roll(gg * v, 1, 0)


def kinetic(v, hh, gg):
    return horizontal(v, hh) + vertical(v, gg)


def squares(v):
    columns = v.shape[1]
    v = v[:8] * v[:8] + v[8 : WIDE - 8] * v[8 : WIDE - 8]
    return sum(v[:, c : c + LANES] for c in range(0, columns, LANES))


def widen(slot, own, below, above, at):
    row, n = at
    slot[pl.ds(0, own.shape[0])] = own
    slot[pl.ds(own.shape[0], n)] = below[pl.ds(row, n)]
    slot[pl.ds(WIDE - n, n)] = above[pl.ds(row, n)]


def own_kernel(s_ref, ph_ref, bond_ref, hs_ref, wp_ref, hwp_ref, q_ref, hq_ref, weight):
    count, slices, rows, _ = s_ref.shape
    first = lax.axis_index("tm") == 0
    for t in range(slices):
        value = jnp.exp(coupling * ph_ref[t])
        weight[t] = value * jnp.where(first, -1.0, 1.0) if t == 0 else value
    hh = hopping * bond_ref[0].astype(jnp.float32)
    gg = hopping * bond_ref[1].astype(jnp.float32)
    gg = jnp.where(lax.broadcasted_iota(jnp.int32, gg.shape, 0) < rows - 1, gg, 0.0)

    def one_source(i, _):
        p_old = None
        for t in range(1, slices):
            v = s_ref[i, t - 1]
            along = horizontal(v, hh)
            hs_ref[i, t - 1] = along
            p = s_ref[i, t] - weight[t] * (along + vertical(v, gg))
            v = weight[t] * p
            along = horizontal(v, hh)
            wp_ref[i, t - 1] = v
            hwp_ref[i, t - 1] = along
            if 2 <= t < slices - 1:
                q = p_old - (along + vertical(v, gg))
                q_ref[i, t - 2] = q
                hq_ref[i, t - 2] = horizontal(q, hh)
            p_old = p
        return 0

    lax.fori_loop(0, count, one_source, 0)


def own_parts(sources, phonons, bonds):
    count, slices, rows, columns = sources.shape
    field = lambda n: jax.ShapeDtypeStruct((count, n, rows, columns), jnp.float32)
    return pl.pallas_call(
        own_kernel,
        out_shape=[field(slices - 1)] * 3
        + [field(slices - 3)] * 2
        + [jax.ShapeDtypeStruct(phonons.shape, jnp.float32)],
        in_specs=[VMEM] * 3,
        out_specs=[VMEM] * 6,
        compiler_params=PARAMS,
        name="own_parts",
    )(sources, phonons, bonds)


def inner_kernel(
    s_ref, ph_ref, bond_ref, above, below, hs_ref, wp_own, hwp_ref, q_own, hq_ref, weight_own,
    p_ref, q_ref, t_ref, s_edge, kp_edge, shared, acc, ext, weight, hh_two, hh_three,
):
    count, slices, own, columns = s_ref.shape
    side, _ = side_layout(count, slices)
    for k in range(2):
        widen(shared.at[k], bond_ref[k].astype(jnp.float32), below, above, side["bond", k])
        shared[k] = hopping * shared[k]
    hh_two[...] = shared[0, pl.ds(own, 8)]
    hh_two[pl.ds(3, 1)] = shared[0, pl.ds(own - 1, 1)]
    hh_two[pl.ds(4, 1)] = shared[0, pl.ds(0, 1)]
    hh_three[...] = jnp.zeros_like(hh_three)
    hh_three[pl.ds(2, 2)] = shared[0, pl.ds(own - 2, 2)]
    hh_three[pl.ds(4, 2)] = shared[0, pl.ds(0, 2)]
    first = lax.axis_index("tm") == 0
    for t in range(slices):
        slot = weight.at[t]
        widen(slot, weight_own[t], below, above, side[count, t])
        value = jnp.exp(coupling * slot[pl.ds(own, 8)])
        slot[pl.ds(own, 8)] = value * jnp.where(first, -1.0, 1.0) if t == 0 else value
        for i in range(count):
            widen(ext.at[i, t], s_ref[i, t], below, above, side[i, t])
    for j in range(2):
        shared[2 + j] = weight[j]

    def one_source(i, _):
        sub = lax.broadcasted_iota(jnp.int32, (8, columns), 0)
        turn = lambda v: pltpu.roll(v, 4, 0)
        gg = shared[1]
        sums = [jnp.zeros((8, LANES), jnp.float32)] * 4
        p_old = q_old = None
        s_edge[i] = ext[i, 0]
        for t in range(1, slices):
            s, v = ext[i, t], ext[i, t - 1]
            along = jnp.concatenate([hs_ref[i, t - 1], horizontal(v[own:], shared[0, pl.ds(own, 8)])], axis=0)
            p = s - weight[t] * (along + vertical(v, gg))
            if t < slices - 1:
                p_ref[i, t - 1] = p[:own]
                sums[0] += squares(s)
                sums[1] += squares(p)
            v = weight[t] * p
            change = v[:own] - wp_own[i, t - 1]
            tile = jnp.where(sub == 3, turn(change[8:]), jnp.where(sub == 4, turn(change[:8]), v[own:]))
            tile = horizontal(tile, hh_two[...])
            turned, along = turn(tile), hwp_ref[i, t - 1]
            top = along[:8] + jnp.where(sub == 0, turned, 0.0)
            bottom = along[8:] + jnp.where(sub == 7, turned, 0.0)
            back = jnp.concatenate([top, bottom, tile], axis=0) + vertical(v, gg)
            if t == 1:
                kp_edge[i] = back
            else:
                q = p_old - back
                q_ref[i, t - 2] = q[:own]
                sums[2] += squares(q)
                if t > 2:
                    change = q_old[:own] - q_own[i, t - 3]
                    tile = jnp.where(sub < 4, turn(change[8:]), turn(change[:8]))
                    turned, along = turn(horizontal(tile, hh_three[...])), hq_ref[i, t - 3]
                    top = along[:8] + jnp.where(sub < 2, turned, 0.0)
                    bottom = along[8:] + jnp.where(sub > 5, turned, 0.0)
                    moved = jnp.concatenate([top, bottom], axis=0) + vertical(q_old, gg)[:own]
                    u = q[:own] - weight[t - 1, pl.ds(0, own)] * moved
                    t_ref[i, t - 3] = u
                    sums[3] += squares(u)
                q_old = q
            p_old = p
        for k in range(4):
            acc[k * count + i] = sums[k]
        return 0

    lax.fori_loop(0, count, one_source, 0)


def inner_operators(sources, phonons, bonds, above, below, parts):
    count, slices, rows, columns = sources.shape
    shape = lambda *n: jax.ShapeDtypeStruct(n, jnp.float32)
    field = lambda times: shape(count, times, rows, columns)
    wide = lambda n: shape(n, WIDE, columns)
    return pl.pallas_call(
        inner_kernel,
        out_shape=[
            field(slices - 2),
            field(slices - 2),
            field(slices - 3),
            wide(count),
            wide(count),
            wide(4),
            shape(4 * count, 8, LANES),
        ],
        in_specs=[VMEM] * 11,
        out_specs=[VMEM] * 7,
        scratch_shapes=[
            pltpu.VMEM((count, slices, WIDE, columns), jnp.float32),
            pltpu.VMEM((slices, WIDE, columns), jnp.float32),
            pltpu.VMEM((8, columns), jnp.float32),
            pltpu.VMEM((8, columns), jnp.float32),
        ],
        compiler_params=PARAMS,
        name="inner_operators",
    )(sources, phonons, bonds, above, below, *parts)


def outer_kernel(
    before, above, below, q_inner, s_edge, kp_edge, shared, acc_inner, p_ref, q_ref, t_ref, partial_ref, ext, weight, acc
):
    count = s_edge.shape[0]
    own = before.shape[1]
    corner, _ = corner_layout(count)
    for i in range(count):
        for j in range(EARLY):
            widen(ext.at[i, j], before[EARLY * i + j], below, above, corner[i, j - EARLY])
    for j in range(2):
        widen(weight.at[j], before[EARLY * count + j], below, above, corner[count, j - 2])
        weight[j] = jnp.exp(coupling * weight[j])

    def one_source(i, _):
        moved = lambda v: kinetic(v, shared[0], shared[1])
        w = [weight[0], weight[1], shared[2], shared[3]]
        s = [ext[i, 0], ext[i, 1], ext[i, 2], s_edge[i]]
        p = [s[j + 1] - w[j] * moved(s[j]) for j in range(3)]
        q = [p[0] - moved(w[1] * p[1]), p[1] - moved(w[2] * p[2]), p[2] - kp_edge[i]]
        u = [q[1] - w[1] * moved(q[0]), q[2] - w[2] * moved(q[1])]
        u.append(q_inner[i, 0] - w[3][:own] * moved(q[2])[:own])
        for j in range(2):
            p_ref[i, j] = p[j + 1][:own]
            q_ref[i, j] = q[j + 1][:own]
        for j in range(3):
            t_ref[i, j] = u[j][:own]
        for k, fields in enumerate((s[2:], p[1:], q[1:], u)):
            acc[k * count + i] = acc_inner[k * count + i] + sum(squares(v) for v in fields)
        return 0

    lax.fori_loop(0, count, one_source, 0)
    lines = jnp.sum(acc[...], axis=1)
    lines = jnp.broadcast_to(jnp.sum(lines, axis=1, keepdims=True), lines.shape)
    at = lambda d: lax.broadcasted_iota(jnp.int32, lines.shape, d)
    row = jnp.sum(jnp.where(at(0) == at(1), lines, 0.0), axis=0, keepdims=True)
    partial_ref[...] = jnp.broadcast_to(row, partial_ref.shape)


def outer_operators(before, above, below, inner, everyone):
    _, q_inner, _, s_edge, kp_edge, shared, acc = inner
    count, _, rows, columns = q_inner.shape
    field = lambda times: jax.ShapeDtypeStruct((count, times, rows, columns), jnp.float32)
    return pl.pallas_call(
        outer_kernel,
        out_shape=[field(2), field(2), field(3), jax.ShapeDtypeStruct((everyone, LANES), jnp.float32)],
        in_specs=[VMEM] * 8,
        out_specs=[VMEM] * 4,
        scratch_shapes=[
            pltpu.VMEM((count, EARLY, WIDE, columns), jnp.float32),
            pltpu.VMEM((2, WIDE, columns), jnp.float32),
            pltpu.VMEM((4 * count, 8, LANES), jnp.float32),
        ],
        compiler_params=PARAMS,
        name="outer_operators",
    )(before, above, below, q_inner, s_edge, kp_edge, shared, acc)


def force_kernel(
    mom_ref, s_ref, p_in, q_in, t_in, p_out, q_out, t_out, ph_ref, before, pi_ref, half_ref, early_ref, send_hbm,
    send_ref, sems,
):
    count, slices, rows, columns = s_ref.shape
    moments = jnp.sum(mom_ref[...], axis=0, keepdims=True)
    m = [moments] + [pltpu.roll(moments, LANES - count * k, 1) for k in range(1, 4)]
    alpha, square, cube = m[0] / m[1], m[2] / m[1], m[3] / m[1]
    spread = cube - square * square
    lane = lax.broadcasted_iota(jnp.int32, moments.shape, 1)

    def at(values, i):
        return jnp.sum(jnp.where(lane == i, values, 0.0))

    low = [at((alpha * cube - square) / spread, i) for i in range(count)]
    high = [at((1.0 - alpha * square) / spread, i) for i in range(count)]
    kept = EARLY * count
    phonon = lambda t: before[kept + 2 + t] if t < 0 else ph_ref[t]
    copies = []
    for t in range(-1, slices - 1):
        fermion = None
        for i in range(count):
            source = before[EARLY * i + EARLY - 1] if t < 0 else s_ref[i, t]
            p, q = (p_out[i, t + 1], q_out[i, t + 1]) if t < 1 else (p_in[i, t - 1], q_in[i, t - 1])
            x = low[i] * source + high[i] * q
            y = low[i] * p + high[i] * (t_out[i, t + 1] if t < 2 else t_in[i, t - 2])
            term = y * (x - y)
            fermion = term if fermion is None else fermion + term
        beside = phonon(t + 1) + phonon(t - 1)
        boson = restore * phonon(t) + spring * (2.0 * phonon(t) - beside)
        momentum = before[kept + 2] if t < 0 else pi_ref[t]
        half = momentum - 0.5 * stepsize * (boson + 2.0 * coupling * fermion)
        if t < 0:
            early_ref[...] = half
        else:
            half_ref[t] = half
        for r in range(0, rows, 2):
            for c in range(0, columns, LANES):
                send_ref[(r // 2) * (columns // LANES) + c // LANES, pl.ds(2 * (t + 1), 2)] = half[
                    r : r + 2, c : c + LANES
                ]
        if t % 4 == 2:
            tile = pl.ds(8 * (t // 4), 8)
            copy = pltpu.make_async_copy(send_ref.at[:, tile], send_hbm.at[:, tile], sems.at[t // 4])
            copy.start()
            copies.append(copy)
    for copy in copies:
        copy.wait()


def force(received, sources, inner, outer, phonons, before, momenta, peers):
    slices, rows, columns = phonons.shape
    shape = lambda *n: jax.ShapeDtypeStruct(n, jnp.float32)
    return pl.pallas_call(
        force_kernel,
        out_shape=[shape(slices - 1, rows, columns), shape(rows, columns), shape(peers, 2 * slices, LANES)],
        in_specs=[VMEM] * 11,
        out_specs=[VMEM, VMEM, pl.BlockSpec(memory_space=pltpu.HBM)],
        scratch_shapes=[
            pltpu.VMEM((peers, 2 * slices, LANES), jnp.float32),
            pltpu.SemaphoreType.DMA((slices // 4,)),
        ],
        compiler_params=PARAMS,
        name="force",
    )(received, sources, *inner[:3], *outer[:3], phonons, before, momenta)


def table_kernel(kernel_ref, table_ref):
    times = kernel_ref.shape[1]
    same = jnp.broadcast_to(pltpu.roll(kernel_ref[...], times - 1, 1), (times, times))
    shifted = pltpu.roll(same, 0, 1, stride=1, stride_axis=0)
    table_ref[...] = stepsize * jnp.transpose(shifted)


def circulant(kernel):
    times = kernel.shape[0]
    return pl.pallas_call(
        table_kernel,
        out_shape=jax.ShapeDtypeStruct((times, times), jnp.float32),
        in_specs=[VMEM],
        out_specs=VMEM,
        compiler_params=PARAMS,
        name="circulant",
        cost_estimate=pl.CostEstimate(flops=10**11, bytes_accessed=10**6, transcendentals=0),
    )(kernel[None])


def drift_kernel(table_ref, x_ref, out_ref):
    times = table_ref.shape[0]
    both = jnp.concatenate([x_ref[pl.ds(k, times, stride=2)] for k in range(2)], axis=1)
    mixed = jnp.dot(
        table_ref[...], both, precision=lax.Precision.HIGHEST, preferred_element_type=jnp.float32
    )
    for k in range(2):
        out_ref[pl.ds(k, times, stride=2)] = mixed[:, k * LANES : (k + 1) * LANES]


def drift(table, columns):
    flat = columns.reshape(-1, LANES)
    mixed = pl.pallas_call(
        drift_kernel,
        out_shape=jax.ShapeDtypeStruct(flat.shape, jnp.float32),
        in_specs=[VMEM] * 2,
        out_specs=VMEM,
        compiler_params=PARAMS,
        name="drift",
    )(table, flat)
    return mixed.reshape(columns.shape)


def join_kernel(half_ref, late_ref, all_ref):
    last = half_ref.shape[0]
    all_ref[pl.ds(0, last)] = half_ref[...]
    all_ref[last] = late_ref[...]


def join_times(half, late):
    return pl.pallas_call(
        join_kernel,
        out_shape=jax.ShapeDtypeStruct((half.shape[0] + 1,) + half.shape[1:], jnp.float32),
        in_specs=[VMEM] * 2,
        out_specs=VMEM,
        compiler_params=PARAMS,
        name="join_times",
    )(half, late)


def add_kernel(ph_ref, back_ref, out_hbm, out_ref, sems):
    slices, rows, columns = ph_ref.shape
    copies = []
    for t in range(slices):
        for r in range(0, rows, 2):
            for c in range(0, columns, LANES):
                moved = back_ref[(r // 2) * (columns // LANES) + c // LANES, pl.ds(2 * t, 2)]
                out_ref[t, pl.ds(r, 2), pl.ds(c, LANES)] = ph_ref[t, pl.ds(r, 2), pl.ds(c, LANES)] + moved
        copies.append(pltpu.make_async_copy(out_ref.at[t], out_hbm.at[t], sems.at[t]))
        copies[t].start()
    for copy in copies:
        copy.wait()


def add_drift(phonons, back):
    return pl.pallas_call(
        add_kernel,
        out_shape=jax.ShapeDtypeStruct(phonons.shape, jnp.float32),
        in_specs=[VMEM] * 2,
        out_specs=pl.BlockSpec(memory_space=pltpu.HBM),
        scratch_shapes=[
            pltpu.VMEM(phonons.shape, jnp.float32),
            pltpu.SemaphoreType.DMA((phonons.shape[0],)),
        ],
        compiler_params=PARAMS,
        name="add_drift",
    )(phonons, back)


def passed_along(block, axis, distance):
    count = lax.axis_size(axis)
    return lax.ppermute(block, axis, [((i - distance) % count, i) for i in range(count)])


def passed_diagonally(block, times, slabs):
    nt, ns = lax.axis_size("tm"), lax.axis_size("slab")
    route = [
        (((i - times) % nt) * ns + (j - slabs) % ns, i * ns + j) for i in range(nt) for j in range(ns)
    ]
    return lax.ppermute(block, ("tm", "slab"), route)


def body(sources, phonons, momenta, kernel, bonds):
    peers = lax.axis_size("tm")
    everyone = peers * lax.axis_size("slab")
    up, down, sources, phonons, bonds, last_momenta = pack_sides(sources, phonons, bonds, momenta)
    above = passed_along(up, "slab", 1)
    below = passed_along(down, "slab", -1)
    ahead = pack_ahead(sources, phonons, last_momenta)
    before = passed_along(ahead, "tm", 1)
    up_corner, down_corner = pack_corners(ahead)
    above_corner = passed_diagonally(up_corner, 1, 1)
    below_corner = passed_diagonally(down_corner, 1, -1)
    side_halos = (above, below)
    own = own_parts(sources, phonons, bonds)
    (above, below), table, own = lax.optimization_barrier((side_halos, circulant(kernel), own))
    inner = inner_operators(sources, phonons, bonds, above, below, own)
    outer = outer_operators(before, above_corner, below_corner, inner, everyone)
    received = lax.all_to_all(outer[3], ("tm", "slab"), split_axis=0, concat_axis=0, tiled=True)
    half, early, send = force(received, sources, inner, outer, phonons, before, momenta, peers)
    columns = lax.all_to_all(send, "tm", split_axis=0, concat_axis=0, tiled=True)
    half_momenta = join_times(half, passed_along(early, "tm", -1))
    columns, half_momenta = lax.optimization_barrier((columns, half_momenta))
    mixed = drift(table, columns)
    back = lax.all_to_all(mixed, "tm", split_axis=0, concat_axis=0, tiled=True)
    return half_momenta, add_drift(phonons, back)


def solution(mesh):
    return jax.shard_map(
        body,
        mesh=mesh,
        in_specs=(
            P(None, "tm", "slab", None),
            P("tm", "slab", None),
            P("tm", "slab", None),
            P(),
            P(None, "slab", None),
        ),
        out_specs=(P("tm", "slab", None), P("tm", "slab", None)),
        check_vma=False,
    )
```

```python
import jax
import jax.numpy as jnp
from jax import lax
from jax.experimental import pallas as pl
from jax.experimental.pallas import tpu as pltpu
from jax.sharding import PartitionSpec as P

hopping = 0.1
coupling = 0.2
restore = 0.25
spring = 0.25
stepsize = 0.5

LANES = 128
WIDE = 24
EARLY = 3
VMEM = pl.BlockSpec(memory_space=pltpu.VMEM)
PARAMS = pltpu.CompilerParams(vmem_limit_bytes=28 * 2**20)


def layout(entries):
    at, row = {}, 0
    for key, rows in entries:
        at[key] = (row, rows)
        row += rows
    return at, -(-row // 8) * 8


def side_layout(count, slices):
    depth = lambda t: min(3, slices - t)
    entries = [((i, t), depth(t)) for i in range(count) for t in range(slices)]
    entries += [((count, t), min(2, depth(t))) for t in range(slices)]
    return layout(entries + [(("bond", 0), 2), (("bond", 1), 3)])


def corner_layout(count):
    entries = [((i, t), 2 if t == -3 else 3) for i in range(count) for t in (-3, -2, -1)]
    return layout(entries + [((count, -2), 1), ((count, -1), 2)])


def rows_of(ref, n, last):
    return ref[pl.ds(ref.shape[0] - n if last else 0, n)]


def side_kernel(s_hbm, ph_hbm, bond_hbm, pi_hbm, up, down, s_ref, ph_ref, bond_ref, pi_ref, sems):
    count, slices = s_ref.shape[:2]
    copies = [pltpu.make_async_copy(s_hbm.at[i], s_ref.at[i], sems.at[i]) for i in range(count)]
    copies.append(pltpu.make_async_copy(ph_hbm, ph_ref, sems.at[count]))
    copies.append(pltpu.make_async_copy(bond_hbm, bond_ref, sems.at[count + 1]))
    copies.append(pltpu.make_async_copy(pi_hbm.at[slices - 1], pi_ref, sems.at[count + 2]))
    for copy in copies:
        copy.start()
    side, _ = side_layout(count, slices)
    for i in range(count + 1):
        copies[i].wait()
        source = s_ref.at[i] if i < count else ph_ref
        for t in range(slices):
            row, n = side[i, t]
            up[pl.ds(row, n)] = rows_of(source.at[t], n, True)
            down[pl.ds(row, n)] = rows_of(source.at[t], n, False)
    copies[count + 1].wait()
    for k in range(2):
        row, n = side["bond", k]
        up[pl.ds(row, n)] = rows_of(bond_ref.at[k], n, True).astype(jnp.float32)
        down[pl.ds(row, n)] = rows_of(bond_ref.at[k], n, False).astype(jnp.float32)
    copies[count + 2].wait()


def pack_sides(sources, phonons, bonds, momenta):
    count, slices, rows, columns = sources.shape
    side = jax.ShapeDtypeStruct((side_layout(count, slices)[1], columns), jnp.float32)
    whole = [jax.ShapeDtypeStruct(x.shape, x.dtype) for x in (sources, phonons, bonds)]
    whole.append(jax.ShapeDtypeStruct(momenta.shape[1:], jnp.float32))
    return pl.pallas_call(
        side_kernel,
        out_shape=[side, side, *whole],
        in_specs=[pl.BlockSpec(memory_space=pltpu.HBM)] * 4,
        out_specs=[VMEM] * 6,
        scratch_shapes=[pltpu.SemaphoreType.DMA((count + 3,))],
        compiler_params=PARAMS,
        name="pack_sides",
    )(*(pltpu.with_memory_space_constraint(x, pltpu.HBM) for x in (sources, phonons, bonds, momenta)))


def ahead_kernel(s_ref, ph_ref, pi_ref, ahead):
    count, slices = s_ref.shape[:2]
    for i in range(count):
        for j in range(EARLY):
            ahead[EARLY * i + j] = s_ref[i, slices - EARLY + j]
    for j in range(2):
        ahead[EARLY * count + j] = ph_ref[slices - 2 + j]
    ahead[EARLY * count + 2] = pi_ref[...]


def pack_ahead(sources, phonons, last_momenta):
    count, _, rows, columns = sources.shape
    return pl.pallas_call(
        ahead_kernel,
        out_shape=jax.ShapeDtypeStruct((EARLY * count + 3, rows, columns), jnp.float32),
        in_specs=[VMEM] * 3,
        out_specs=VMEM,
        compiler_params=PARAMS,
        name="pack_ahead",
    )(sources, phonons, last_momenta)


def corner_kernel(ahead, up, down):
    count = (ahead.shape[0] - 3) // EARLY
    corner, _ = corner_layout(count)
    for (i, t), (row, n) in corner.items():
        source = ahead.at[EARLY * i + (EARLY if i < count else 2) + t]
        up[pl.ds(row, n)] = rows_of(source, n, True)
        down[pl.ds(row, n)] = rows_of(source, n, False)


def pack_corners(ahead):
    rows = corner_layout((ahead.shape[0] - 3) // EARLY)[1]
    return pl.pallas_call(
        corner_kernel,
        out_shape=[jax.ShapeDtypeStruct((rows, ahead.shape[2]), jnp.float32)] * 2,
        in_specs=[VMEM],
        out_specs=[VMEM] * 2,
        compiler_params=PARAMS,
        name="pack_corners",
    )(ahead)


def horizontal(v, hh):
    return v + (hh * pltpu.roll(v, v.shape[1] - 1, 1) + pltpu.roll(hh * v, 1, 1))


def vertical(v, gg):
    return gg * pltpu.roll(v, v.shape[0] - 1, 0) + pltpu.roll(gg * v, 1, 0)


def kinetic(v, hh, gg):
    return horizontal(v, hh) + vertical(v, gg)


def squares(v):
    columns = v.shape[1]
    v = v[:8] * v[:8] + v[8 : WIDE - 8] * v[8 : WIDE - 8]
    return sum(v[:, c : c + LANES] for c in range(0, columns, LANES))


def widen(slot, own, below, above, at):
    row, n = at
    slot[pl.ds(0, own.shape[0])] = own
    slot[pl.ds(own.shape[0], n)] = below[pl.ds(row, n)]
    slot[pl.ds(WIDE - n, n)] = above[pl.ds(row, n)]


def own_kernel(s_ref, ph_ref, bond_ref, hs_ref, wp_ref, hwp_ref, q_ref, hq_ref, weight):
    count, slices, rows, _ = s_ref.shape
    first = lax.axis_index("tm") == 0
    for t in range(slices):
        value = jnp.exp(coupling * ph_ref[t])
        weight[t] = value * jnp.where(first, -1.0, 1.0) if t == 0 else value
    hh = hopping * bond_ref[0].astype(jnp.float32)
    gg = hopping * bond_ref[1].astype(jnp.float32)
    gg = jnp.where(lax.broadcasted_iota(jnp.int32, gg.shape, 0) < rows - 1, gg, 0.0)

    def one_source(i, _):
        p_old = None
        for t in range(1, slices):
            v = s_ref[i, t - 1]
            along = horizontal(v, hh)
            hs_ref[i, t - 1] = along
            p = s_ref[i, t] - weight[t] * (along + vertical(v, gg))
            v = weight[t] * p
            along = horizontal(v, hh)
            wp_ref[i, t - 1] = v
            hwp_ref[i, t - 1] = along
            if 2 <= t < slices - 1:
                q = p_old - (along + vertical(v, gg))
                q_ref[i, t - 2] = q
                hq_ref[i, t - 2] = horizontal(q, hh)
            p_old = p
        return 0

    lax.fori_loop(0, count, one_source, 0)


def own_parts(sources, phonons, bonds):
    count, slices, rows, columns = sources.shape
    field = lambda n: jax.ShapeDtypeStruct((count, n, rows, columns), jnp.float32)
    return pl.pallas_call(
        own_kernel,
        out_shape=[field(slices - 1)] * 3
        + [field(slices - 3)] * 2
        + [jax.ShapeDtypeStruct(phonons.shape, jnp.float32)],
        in_specs=[VMEM] * 3,
        out_specs=[VMEM] * 6,
        compiler_params=PARAMS,
        name="own_parts",
    )(sources, phonons, bonds)


def build_tiles(hh_two, hh_three, hh, own):
    hh_two[...] = hh[pl.ds(own, 8)]
    hh_two[pl.ds(3, 1)] = hh[pl.ds(own - 1, 1)]
    hh_two[pl.ds(4, 1)] = hh[pl.ds(0, 1)]
    hh_three[...] = jnp.zeros_like(hh_three)
    hh_three[pl.ds(2, 2)] = hh[pl.ds(own - 2, 2)]
    hh_three[pl.ds(4, 2)] = hh[pl.ds(0, 2)]


def turn(v):
    return pltpu.roll(v, 4, 0)


def place_in(v):
    return lax.broadcasted_iota(jnp.int32, (8, v.shape[1]), 0)


def moved_sources(v, along, hh_halo, gg):
    own = along.shape[0]
    return jnp.concatenate([along, horizontal(v[own:], hh_halo)], axis=0) + vertical(v, gg)


def moved_weighted(v, v_own, along, hh_two, gg):
    own, sub = along.shape[0], place_in(v)
    change = v[:own] - v_own
    tile = jnp.where(sub == 3, turn(change[8:]), jnp.where(sub == 4, turn(change[:8]), v[own:]))
    tile = horizontal(tile, hh_two)
    turned = turn(tile)
    top = along[:8] + jnp.where(sub == 0, turned, 0.0)
    bottom = along[8:] + jnp.where(sub == 7, turned, 0.0)
    return jnp.concatenate([top, bottom, tile], axis=0) + vertical(v, gg)


def moved_normal(q, q_own, along, hh_three, gg):
    own, sub = along.shape[0], place_in(q)
    change = q[:own] - q_own
    tile = jnp.where(sub < 4, turn(change[8:]), turn(change[:8]))
    turned = turn(horizontal(tile, hh_three))
    top = along[:8] + jnp.where(sub < 2, turned, 0.0)
    bottom = along[8:] + jnp.where(sub > 5, turned, 0.0)
    return jnp.concatenate([top, bottom], axis=0) + vertical(q, gg)[:own]


def inner_kernel(
    s_ref, ph_ref, bond_ref, above, below, hs_ref, wp_own, hwp_ref, q_own, hq_ref, weight_own,
    p_ref, q_ref, t_ref, s_edge, kp_edge, shared, acc, ext, weight, hh_two, hh_three,
):
    count, slices, own, columns = s_ref.shape
    side, _ = side_layout(count, slices)
    for k in range(2):
        widen(shared.at[k], bond_ref[k].astype(jnp.float32), below, above, side["bond", k])
        shared[k] = hopping * shared[k]
    build_tiles(hh_two, hh_three, shared.at[0], own)
    first = lax.axis_index("tm") == 0
    for t in range(slices):
        slot = weight.at[t]
        widen(slot, weight_own[t], below, above, side[count, t])
        value = jnp.exp(coupling * slot[pl.ds(own, 8)])
        slot[pl.ds(own, 8)] = value * jnp.where(first, -1.0, 1.0) if t == 0 else value
        for i in range(count):
            widen(ext.at[i, t], s_ref[i, t], below, above, side[i, t])
    for j in range(2):
        shared[2 + j] = weight[j]

    def one_source(i, _):
        gg = shared[1]
        sums = [jnp.zeros((8, LANES), jnp.float32)] * 4
        p_old = q_old = None
        s_edge[i] = ext[i, 0]
        for t in range(1, slices):
            s = ext[i, t]
            p = s - weight[t] * moved_sources(ext[i, t - 1], hs_ref[i, t - 1], shared[0, pl.ds(own, 8)], gg)
            if t < slices - 1:
                p_ref[i, t - 1] = p[:own]
                sums[0] += squares(s)
                sums[1] += squares(p)
            back = moved_weighted(weight[t] * p, wp_own[i, t - 1], hwp_ref[i, t - 1], hh_two[...], gg)
            if t == 1:
                kp_edge[i] = back
            else:
                q = p_old - back
                q_ref[i, t - 2] = q[:own]
                sums[2] += squares(q)
                if t > 2:
                    moved = moved_normal(q_old, q_own[i, t - 3], hq_ref[i, t - 3], hh_three[...], gg)
                    u = q[:own] - weight[t - 1, pl.ds(0, own)] * moved
                    t_ref[i, t - 3] = u
                    sums[3] += squares(u)
                q_old = q
            p_old = p
        for k in range(4):
            acc[k * count + i] = sums[k]
        return 0

    lax.fori_loop(0, count, one_source, 0)


def inner_operators(sources, phonons, bonds, above, below, parts):
    count, slices, rows, columns = sources.shape
    shape = lambda *n: jax.ShapeDtypeStruct(n, jnp.float32)
    field = lambda times: shape(count, times, rows, columns)
    wide = lambda n: shape(n, WIDE, columns)
    return pl.pallas_call(
        inner_kernel,
        out_shape=[
            field(slices - 2),
            field(slices - 2),
            field(slices - 3),
            wide(count),
            wide(count),
            wide(4),
            shape(4 * count, 8, LANES),
        ],
        in_specs=[VMEM] * 11,
        out_specs=[VMEM] * 7,
        scratch_shapes=[
            pltpu.VMEM((count, slices, WIDE, columns), jnp.float32),
            pltpu.VMEM((slices, WIDE, columns), jnp.float32),
            pltpu.VMEM((8, columns), jnp.float32),
            pltpu.VMEM((8, columns), jnp.float32),
        ],
        compiler_params=PARAMS,
        name="inner_operators",
    )(sources, phonons, bonds, above, below, *parts)


def early_kernel(
    before, s_ref, bond_ref, wp_own, hwp_own, weight_own, hs_ref, wp_ref, hwp_ref, q_ref, hq_ref, weight
):
    count, _, rows, _ = s_ref.shape
    for j in range(2):
        weight[j] = jnp.exp(coupling * before[EARLY * count + j])
    hh = hopping * bond_ref[0].astype(jnp.float32)
    gg = hopping * bond_ref[1].astype(jnp.float32)
    gg = jnp.where(lax.broadcasted_iota(jnp.int32, gg.shape, 0) < rows - 1, gg, 0.0)

    def one_source(i, _):
        s = [before[EARLY * i + j] for j in range(EARLY)] + [s_ref[i, 0]]
        w = [weight[0], weight[1], weight_own[0]]
        p, back = [], []
        for j in range(3):
            along = horizontal(s[j], hh)
            hs_ref[i, j] = along
            p.append(s[j + 1] - w[j] * (along + vertical(s[j], gg)))
        for j in range(1, 3):
            v = w[j] * p[j]
            along = horizontal(v, hh)
            wp_ref[i, j - 1] = v
            hwp_ref[i, j - 1] = along
            back.append(along + vertical(v, gg))
        back.append(hwp_own[i, 0] + vertical(wp_own[i, 0], gg))
        for j in range(3):
            q = p[j] - back[j]
            q_ref[i, j] = q
            hq_ref[i, j] = horizontal(q, hh)
        return 0

    lax.fori_loop(0, count, one_source, 0)


def early_parts(before, sources, bonds, own):
    count, _, rows, columns = sources.shape
    field = lambda n: jax.ShapeDtypeStruct((count, n, rows, columns), jnp.float32)
    return pl.pallas_call(
        early_kernel,
        out_shape=[field(3), field(2), field(2), field(3), field(3)]
        + [jax.ShapeDtypeStruct((2, rows, columns), jnp.float32)],
        in_specs=[VMEM] * 6,
        out_specs=[VMEM] * 6,
        compiler_params=PARAMS,
        name="early_parts",
    )(before, sources, bonds, own[1], own[2], own[5])


def outer_kernel(
    before, above, below, hs_ref, wp_own, hwp_ref, q_own, hq_ref, weight_own, q_inner, s_edge, kp_edge, shared, acc_inner,
    p_ref, q_ref, t_ref, partial_ref, ext, weight, acc, hh_two, hh_three,
):
    count = s_edge.shape[0]
    own = before.shape[1]
    corner, _ = corner_layout(count)
    build_tiles(hh_two, hh_three, shared.at[0], own)
    for i in range(count):
        for j in range(EARLY):
            widen(ext.at[i, j], before[EARLY * i + j], below, above, corner[i, j - EARLY])
    for j in range(2):
        slot = weight.at[j]
        row, n = corner[count, j - 2]
        slot[pl.ds(own, n)] = below[pl.ds(row, n)]
        slot[pl.ds(WIDE - n, n)] = above[pl.ds(row, n)]
        slot[pl.ds(own, 8)] = jnp.exp(coupling * slot[pl.ds(own, 8)])
        slot[pl.ds(0, own)] = weight_own[j]

    def one_source(i, _):
        gg, hh_halo = shared[1], shared[0, pl.ds(own, 8)]
        two, three = hh_two[...], hh_three[...]
        w = [weight[0], weight[1], shared[2], shared[3]]
        s = [ext[i, 0], ext[i, 1], ext[i, 2], s_edge[i]]
        p = [s[j + 1] - w[j] * moved_sources(s[j], hs_ref[i, j], hh_halo, gg) for j in range(3)]
        back = [moved_weighted(w[j] * p[j], wp_own[i, j - 1], hwp_ref[i, j - 1], two, gg) for j in (1, 2)]
        q = [p[0] - back[0], p[1] - back[1], p[2] - kp_edge[i]]
        moved = [moved_normal(q[j], q_own[i, j], hq_ref[i, j], three, gg) for j in range(3)]
        u = [x[:own] - w[j + 1][:own] * moved[j] for j, x in enumerate((q[1], q[2], q_inner[i, 0]))]
        for j in range(2):
            p_ref[i, j] = p[j + 1][:own]
            q_ref[i, j] = q[j + 1][:own]
        for j in range(3):
            t_ref[i, j] = u[j][:own]
        for k, fields in enumerate((s[2:], p[1:], q[1:], u)):
            acc[k * count + i] = acc_inner[k * count + i] + sum(squares(v) for v in fields)
        return 0

    lax.fori_loop(0, count, one_source, 0)
    lines = jnp.sum(acc[...], axis=1)
    lines = jnp.broadcast_to(jnp.sum(lines, axis=1, keepdims=True), lines.shape)
    at = lambda d: lax.broadcasted_iota(jnp.int32, lines.shape, d)
    row = jnp.sum(jnp.where(at(0) == at(1), lines, 0.0), axis=0, keepdims=True)
    partial_ref[...] = jnp.broadcast_to(row, partial_ref.shape)


def outer_operators(before, above, below, early, inner, everyone):
    _, q_inner, _, s_edge, kp_edge, shared, acc = inner
    count, _, rows, columns = q_inner.shape
    field = lambda times: jax.ShapeDtypeStruct((count, times, rows, columns), jnp.float32)
    return pl.pallas_call(
        outer_kernel,
        out_shape=[field(2), field(2), field(3), jax.ShapeDtypeStruct((everyone, LANES), jnp.float32)],
        in_specs=[VMEM] * 14,
        out_specs=[VMEM] * 4,
        scratch_shapes=[
            pltpu.VMEM((count, EARLY, WIDE, columns), jnp.float32),
            pltpu.VMEM((2, WIDE, columns), jnp.float32),
            pltpu.VMEM((4 * count, 8, LANES), jnp.float32),
            pltpu.VMEM((8, columns), jnp.float32),
            pltpu.VMEM((8, columns), jnp.float32),
        ],
        compiler_params=PARAMS,
        name="outer_operators",
    )(before, above, below, *early, q_inner, s_edge, kp_edge, shared, acc)


def force_kernel(
    mom_ref, s_ref, p_in, q_in, t_in, p_out, q_out, t_out, ph_ref, before, pi_ref, half_ref, early_ref, send_hbm,
    send_ref, sems,
):
    count, slices, rows, columns = s_ref.shape
    moments = jnp.sum(mom_ref[...], axis=0, keepdims=True)
    m = [moments] + [pltpu.roll(moments, LANES - count * k, 1) for k in range(1, 4)]
    alpha, square, cube = m[0] / m[1], m[2] / m[1], m[3] / m[1]
    spread = cube - square * square
    rows_of_both = [(alpha * cube - square) / spread] * count + [(1.0 - alpha * square) / spread] * count
    both = jnp.concatenate(rows_of_both, axis=0)
    at = lambda d: lax.broadcasted_iota(jnp.int32, both.shape, d)
    picked = jnp.where(at(1) == lax.rem(at(0), count), both, 0.0)
    picked = jnp.sum(picked, axis=1, keepdims=True)
    low = [picked[i : i + 1] for i in range(count)]
    high = [picked[count + i : count + i + 1] for i in range(count)]
    kept = EARLY * count
    phonon = lambda t: before[kept + 2 + t] if t < 0 else ph_ref[t]
    copies = []
    for t in range(-1, slices - 1):
        fermion = None
        for i in range(count):
            source = before[EARLY * i + EARLY - 1] if t < 0 else s_ref[i, t]
            p, q = (p_out[i, t + 1], q_out[i, t + 1]) if t < 1 else (p_in[i, t - 1], q_in[i, t - 1])
            x = low[i] * source + high[i] * q
            y = low[i] * p + high[i] * (t_out[i, t + 1] if t < 2 else t_in[i, t - 2])
            term = y * (x - y)
            fermion = term if fermion is None else fermion + term
        beside = phonon(t + 1) + phonon(t - 1)
        boson = restore * phonon(t) + spring * (2.0 * phonon(t) - beside)
        momentum = before[kept + 2] if t < 0 else pi_ref[t]
        half = momentum - 0.5 * stepsize * (boson + 2.0 * coupling * fermion)
        if t < 0:
            early_ref[...] = half
        else:
            half_ref[t] = half
        for r in range(0, rows, 2):
            for c in range(0, columns, LANES):
                send_ref[(r // 2) * (columns // LANES) + c // LANES, pl.ds(2 * (t + 1), 2)] = half[
                    r : r + 2, c : c + LANES
                ]
        if t % 4 == 2:
            tile = pl.ds(8 * (t // 4), 8)
            copy = pltpu.make_async_copy(send_ref.at[:, tile], send_hbm.at[:, tile], sems.at[t // 4])
            copy.start()
            copies.append(copy)
    for copy in copies:
        copy.wait()


def force(received, sources, inner, outer, phonons, before, momenta, peers):
    slices, rows, columns = phonons.shape
    shape = lambda *n: jax.ShapeDtypeStruct(n, jnp.float32)
    return pl.pallas_call(
        force_kernel,
        out_shape=[shape(slices - 1, rows, columns), shape(rows, columns), shape(peers, 2 * slices, LANES)],
        in_specs=[VMEM] * 11,
        out_specs=[VMEM, VMEM, pl.BlockSpec(memory_space=pltpu.HBM)],
        scratch_shapes=[
            pltpu.VMEM((peers, 2 * slices, LANES), jnp.float32),
            pltpu.SemaphoreType.DMA((slices // 4,)),
        ],
        compiler_params=PARAMS,
        name="force",
    )(received, sources, *inner[:3], *outer[:3], phonons, before, momenta)


def table_kernel(kernel_ref, table_ref):
    times = kernel_ref.shape[1]
    same = jnp.broadcast_to(pltpu.roll(kernel_ref[...], times - 1, 1), (times, times))
    shifted = pltpu.roll(same, 0, 1, stride=1, stride_axis=0)
    table_ref[...] = stepsize * jnp.transpose(shifted)


def circulant(kernel):
    times = kernel.shape[0]
    return pl.pallas_call(
        table_kernel,
        out_shape=jax.ShapeDtypeStruct((times, times), jnp.float32),
        in_specs=[VMEM],
        out_specs=VMEM,
        compiler_params=PARAMS,
        name="circulant",
        cost_estimate=pl.CostEstimate(flops=10**11, bytes_accessed=10**6, transcendentals=0),
    )(kernel[None])


def drift_kernel(table_ref, x_ref, out_ref):
    times = table_ref.shape[0]
    both = jnp.concatenate([x_ref[pl.ds(k, times, stride=2)] for k in range(2)], axis=1)
    mixed = jnp.dot(
        table_ref[...], both, precision=lax.Precision.HIGHEST, preferred_element_type=jnp.float32
    )
    for k in range(2):
        out_ref[pl.ds(k, times, stride=2)] = mixed[:, k * LANES : (k + 1) * LANES]


def drift(table, columns):
    flat = columns.reshape(-1, LANES)
    mixed = pl.pallas_call(
        drift_kernel,
        out_shape=jax.ShapeDtypeStruct(flat.shape, jnp.float32),
        in_specs=[VMEM] * 2,
        out_specs=VMEM,
        compiler_params=PARAMS,
        name="drift",
    )(table, flat)
    return mixed.reshape(columns.shape)


def join_kernel(half_ref, late_ref, all_ref):
    last = half_ref.shape[0]
    all_ref[pl.ds(0, last)] = half_ref[...]
    all_ref[last] = late_ref[...]


def join_times(half, late):
    return pl.pallas_call(
        join_kernel,
        out_shape=jax.ShapeDtypeStruct((half.shape[0] + 1,) + half.shape[1:], jnp.float32),
        in_specs=[VMEM] * 2,
        out_specs=VMEM,
        compiler_params=PARAMS,
        name="join_times",
    )(half, late)


def add_kernel(ph_ref, back_ref, out_hbm, out_ref, sems):
    slices, rows, columns = ph_ref.shape
    copies = []
    for t in range(slices):
        for r in range(0, rows, 2):
            for c in range(0, columns, LANES):
                moved = back_ref[(r // 2) * (columns // LANES) + c // LANES, pl.ds(2 * t, 2)]
                out_ref[t, pl.ds(r, 2), pl.ds(c, LANES)] = ph_ref[t, pl.ds(r, 2), pl.ds(c, LANES)] + moved
        copies.append(pltpu.make_async_copy(out_ref.at[t], out_hbm.at[t], sems.at[t]))
        copies[t].start()
    for copy in copies:
        copy.wait()


def add_drift(phonons, back):
    return pl.pallas_call(
        add_kernel,
        out_shape=jax.ShapeDtypeStruct(phonons.shape, jnp.float32),
        in_specs=[VMEM] * 2,
        out_specs=pl.BlockSpec(memory_space=pltpu.HBM),
        scratch_shapes=[
            pltpu.VMEM(phonons.shape, jnp.float32),
            pltpu.SemaphoreType.DMA((phonons.shape[0],)),
        ],
        compiler_params=PARAMS,
        name="add_drift",
    )(phonons, back)


def passed_along(block, axis, distance):
    count = lax.axis_size(axis)
    return lax.ppermute(block, axis, [((i - distance) % count, i) for i in range(count)])


def passed_diagonally(block, times, slabs):
    nt, ns = lax.axis_size("tm"), lax.axis_size("slab")
    route = [
        (((i - times) % nt) * ns + (j - slabs) % ns, i * ns + j) for i in range(nt) for j in range(ns)
    ]
    return lax.ppermute(block, ("tm", "slab"), route)


def body(sources, phonons, momenta, kernel, bonds):
    peers = lax.axis_size("tm")
    everyone = peers * lax.axis_size("slab")
    up, down, sources, phonons, bonds, last_momenta = pack_sides(sources, phonons, bonds, momenta)
    above = passed_along(up, "slab", 1)
    below = passed_along(down, "slab", -1)
    ahead = pack_ahead(sources, phonons, last_momenta)
    before = passed_along(ahead, "tm", 1)
    up_corner, down_corner = pack_corners(ahead)
    above_corner = passed_diagonally(up_corner, 1, 1)
    own, down_corner = lax.optimization_barrier((own_parts(sources, phonons, bonds), down_corner))
    below_corner = passed_diagonally(down_corner, 1, -1)
    side_halos = (above, below)
    early = early_parts(before, sources, bonds, own)
    (above, below), table, own, early = lax.optimization_barrier((side_halos, circulant(kernel), own, early))
    inner = inner_operators(sources, phonons, bonds, above, below, own)
    outer = outer_operators(before, above_corner, below_corner, early, inner, everyone)
    received = lax.all_to_all(outer[3], ("tm", "slab"), split_axis=0, concat_axis=0, tiled=True)
    half, half_before, send = force(received, sources, inner, outer, phonons, before, momenta, peers)
    columns = lax.all_to_all(send, "tm", split_axis=0, concat_axis=0, tiled=True)
    half_momenta = join_times(half, passed_along(half_before, "tm", -1))
    columns, half_momenta = lax.optimization_barrier((columns, half_momenta))
    mixed = drift(table, columns)
    back = lax.all_to_all(mixed, "tm", split_axis=0, concat_axis=0, tiled=True)
    return half_momenta, add_drift(phonons, back)


def solution(mesh):
    return jax.shard_map(
        body,
        mesh=mesh,
        in_specs=(
            P(None, "tm", "slab", None),
            P("tm", "slab", None),
            P("tm", "slab", None),
            P(),
            P(None, "slab", None),
        ),
        out_specs=(P("tm", "slab", None), P("tm", "slab", None)),
        check_vma=False,
    )
```

```python
import jax
import jax.numpy as jnp
from jax import lax
from jax.experimental import pallas as pl
from jax.experimental.pallas import tpu as pltpu
from jax.sharding import PartitionSpec as P

hopping = 0.1
coupling = 0.2
restore = 0.25
spring = 0.25
stepsize = 0.5

LANES = 128
WIDE = 24
EARLY = 3
VMEM = pl.BlockSpec(memory_space=pltpu.VMEM)
PARAMS = pltpu.CompilerParams(vmem_limit_bytes=28 * 2**20)


def layout(entries):
    at, row = {}, 0
    for key, rows in entries:
        at[key] = (row, rows)
        row += rows
    return at, -(-row // 8) * 8


def side_layout(count, slices):
    depth = lambda t: min(3, slices - t)
    entries = [((i, t), depth(t)) for i in range(count) for t in range(slices)]
    entries += [((count, t), min(2, depth(t))) for t in range(slices)]
    return layout(entries + [(("bond", 0), 2), (("bond", 1), 3)])


def corner_layout(count):
    entries = [((i, t), 2 if t == -3 else 3) for i in range(count) for t in (-3, -2, -1)]
    return layout(entries + [((count, -2), 1), ((count, -1), 2)])


def rows_of(ref, n, last):
    return ref[pl.ds(ref.shape[0] - n if last else 0, n)]


def side_kernel(s_hbm, ph_hbm, bond_hbm, pi_hbm, up, down, s_ref, ph_ref, bond_ref, pi_ref, sems):
    count, slices = s_ref.shape[:2]
    copies = [pltpu.make_async_copy(s_hbm.at[i], s_ref.at[i], sems.at[i]) for i in range(count)]
    copies.append(pltpu.make_async_copy(ph_hbm, ph_ref, sems.at[count]))
    copies.append(pltpu.make_async_copy(bond_hbm, bond_ref, sems.at[count + 1]))
    copies.append(pltpu.make_async_copy(pi_hbm.at[slices - 1], pi_ref, sems.at[count + 2]))
    for copy in copies:
        copy.start()
    side, _ = side_layout(count, slices)
    for i in range(count + 1):
        copies[i].wait()
        source = s_ref.at[i] if i < count else ph_ref
        for t in range(slices):
            row, n = side[i, t]
            up[pl.ds(row, n)] = rows_of(source.at[t], n, True)
            down[pl.ds(row, n)] = rows_of(source.at[t], n, False)
    copies[count + 1].wait()
    for k in range(2):
        row, n = side["bond", k]
        up[pl.ds(row, n)] = rows_of(bond_ref.at[k], n, True).astype(jnp.float32)
        down[pl.ds(row, n)] = rows_of(bond_ref.at[k], n, False).astype(jnp.float32)
    copies[count + 2].wait()


def pack_sides(sources, phonons, bonds, momenta):
    count, slices, rows, columns = sources.shape
    side = jax.ShapeDtypeStruct((side_layout(count, slices)[1], columns), jnp.float32)
    whole = [jax.ShapeDtypeStruct(x.shape, x.dtype) for x in (sources, phonons, bonds)]
    whole.append(jax.ShapeDtypeStruct(momenta.shape[1:], jnp.float32))
    return pl.pallas_call(
        side_kernel,
        out_shape=[side, side, *whole],
        in_specs=[pl.BlockSpec(memory_space=pltpu.HBM)] * 4,
        out_specs=[VMEM] * 6,
        scratch_shapes=[pltpu.SemaphoreType.DMA((count + 3,))],
        compiler_params=PARAMS,
        name="pack_sides",
    )(*(pltpu.with_memory_space_constraint(x, pltpu.HBM) for x in (sources, phonons, bonds, momenta)))


def ahead_kernel(s_ref, ph_ref, pi_ref, ahead):
    count, slices = s_ref.shape[:2]
    for i in range(count):
        for j in range(EARLY):
            ahead[EARLY * i + j] = s_ref[i, slices - EARLY + j]
    for j in range(2):
        ahead[EARLY * count + j] = ph_ref[slices - 2 + j]
    ahead[EARLY * count + 2] = pi_ref[...]


def pack_ahead(sources, phonons, last_momenta):
    count, _, rows, columns = sources.shape
    return pl.pallas_call(
        ahead_kernel,
        out_shape=jax.ShapeDtypeStruct((EARLY * count + 3, rows, columns), jnp.float32),
        in_specs=[VMEM] * 3,
        out_specs=VMEM,
        compiler_params=PARAMS,
        name="pack_ahead",
    )(sources, phonons, last_momenta)


def corner_kernel(ahead, up, down):
    count = (ahead.shape[0] - 3) // EARLY
    corner, _ = corner_layout(count)
    for (i, t), (row, n) in corner.items():
        source = ahead.at[EARLY * i + (EARLY if i < count else 2) + t]
        up[pl.ds(row, n)] = rows_of(source, n, True)
        down[pl.ds(row, n)] = rows_of(source, n, False)


def pack_corners(ahead):
    rows = corner_layout((ahead.shape[0] - 3) // EARLY)[1]
    return pl.pallas_call(
        corner_kernel,
        out_shape=[jax.ShapeDtypeStruct((rows, ahead.shape[2]), jnp.float32)] * 2,
        in_specs=[VMEM],
        out_specs=[VMEM] * 2,
        compiler_params=PARAMS,
        name="pack_corners",
    )(ahead)


def horizontal(v, hh):
    return v + (hh * pltpu.roll(v, v.shape[1] - 1, 1) + pltpu.roll(hh * v, 1, 1))


def vertical(v, gg):
    return gg * pltpu.roll(v, v.shape[0] - 1, 0) + pltpu.roll(gg * v, 1, 0)


def kinetic(v, hh, gg):
    return horizontal(v, hh) + vertical(v, gg)


def squares(v):
    columns = v.shape[1]
    v = v[:8] * v[:8] + v[8 : WIDE - 8] * v[8 : WIDE - 8]
    return sum(v[:, c : c + LANES] for c in range(0, columns, LANES))


def widen(slot, own, below, above, at):
    row, n = at
    slot[pl.ds(0, own.shape[0])] = own
    slot[pl.ds(own.shape[0], n)] = below[pl.ds(row, n)]
    slot[pl.ds(WIDE - n, n)] = above[pl.ds(row, n)]


def own_kernel(s_ref, ph_ref, bond_ref, hs_ref, wp_ref, hwp_ref, q_ref, hq_ref, weight):
    count, slices, rows, _ = s_ref.shape
    first = lax.axis_index("tm") == 0
    for t in range(slices):
        value = jnp.exp(coupling * ph_ref[t])
        weight[t] = value * jnp.where(first, -1.0, 1.0) if t == 0 else value
    hh = hopping * bond_ref[0].astype(jnp.float32)
    gg = hopping * bond_ref[1].astype(jnp.float32)
    gg = jnp.where(lax.broadcasted_iota(jnp.int32, gg.shape, 0) < rows - 1, gg, 0.0)

    def one_source(i, _):
        p_old = None
        for t in range(1, slices):
            v = s_ref[i, t - 1]
            along = horizontal(v, hh)
            hs_ref[i, t - 1] = along
            p = s_ref[i, t] - weight[t] * (along + vertical(v, gg))
            v = weight[t] * p
            along = horizontal(v, hh)
            wp_ref[i, t - 1] = v
            hwp_ref[i, t - 1] = along
            if 2 <= t < slices - 1:
                q = p_old - (along + vertical(v, gg))
                q_ref[i, t - 2] = q
                hq_ref[i, t - 2] = horizontal(q, hh)
            p_old = p
        return 0

    lax.fori_loop(0, count, one_source, 0)


def own_parts(sources, phonons, bonds):
    count, slices, rows, columns = sources.shape
    field = lambda n: jax.ShapeDtypeStruct((count, n, rows, columns), jnp.float32)
    return pl.pallas_call(
        own_kernel,
        out_shape=[field(slices - 1)] * 3
        + [field(slices - 3)] * 2
        + [jax.ShapeDtypeStruct(phonons.shape, jnp.float32)],
        in_specs=[VMEM] * 3,
        out_specs=[VMEM] * 6,
        compiler_params=PARAMS,
        name="own_parts",
    )(sources, phonons, bonds)


def build_tiles(hh_two, hh_three, hh, own):
    hh_two[...] = hh[pl.ds(own, 8)]
    hh_two[pl.ds(3, 1)] = hh[pl.ds(own - 1, 1)]
    hh_two[pl.ds(4, 1)] = hh[pl.ds(0, 1)]
    hh_three[...] = jnp.zeros_like(hh_three)
    hh_three[pl.ds(2, 2)] = hh[pl.ds(own - 2, 2)]
    hh_three[pl.ds(4, 2)] = hh[pl.ds(0, 2)]


def turn(v):
    return pltpu.roll(v, 4, 0)


def place_in(v):
    return lax.broadcasted_iota(jnp.int32, (8, v.shape[1]), 0)


def moved_sources(v, along, hh_halo, gg):
    own = along.shape[0]
    return jnp.concatenate([along, horizontal(v[own:], hh_halo)], axis=0) + vertical(v, gg)


def moved_weighted(v, v_own, along, hh_two, gg):
    own, sub = along.shape[0], place_in(v)
    change = v[:own] - v_own
    tile = jnp.where(sub == 3, turn(change[8:]), jnp.where(sub == 4, turn(change[:8]), v[own:]))
    tile = horizontal(tile, hh_two)
    turned = turn(tile)
    top = along[:8] + jnp.where(sub == 0, turned, 0.0)
    bottom = along[8:] + jnp.where(sub == 7, turned, 0.0)
    return jnp.concatenate([top, bottom, tile], axis=0) + vertical(v, gg)


def moved_normal(q, q_own, along, hh_three, gg):
    own, sub = along.shape[0], place_in(q)
    change = q[:own] - q_own
    tile = jnp.where(sub < 4, turn(change[8:]), turn(change[:8]))
    turned = turn(horizontal(tile, hh_three))
    top = along[:8] + jnp.where(sub < 2, turned, 0.0)
    bottom = along[8:] + jnp.where(sub > 5, turned, 0.0)
    return jnp.concatenate([top, bottom], axis=0) + vertical(q, gg)[:own]


def inner_kernel(
    s_ref, ph_ref, bond_ref, above, below, hs_ref, wp_own, hwp_ref, q_own, hq_ref, weight_own,
    p_ref, q_ref, t_ref, s_edge, kp_edge, shared, acc, ext, weight, hh_two, hh_three,
):
    count, slices, own, columns = s_ref.shape
    side, _ = side_layout(count, slices)
    for k in range(2):
        widen(shared.at[k], bond_ref[k].astype(jnp.float32), below, above, side["bond", k])
        shared[k] = hopping * shared[k]
    build_tiles(hh_two, hh_three, shared.at[0], own)
    first = lax.axis_index("tm") == 0
    for t in range(slices):
        slot = weight.at[t]
        widen(slot, weight_own[t], below, above, side[count, t])
        value = jnp.exp(coupling * slot[pl.ds(own, 8)])
        slot[pl.ds(own, 8)] = value * jnp.where(first, -1.0, 1.0) if t == 0 else value
        for i in range(count):
            widen(ext.at[i, t], s_ref[i, t], below, above, side[i, t])
    for j in range(2):
        shared[2 + j] = weight[j]

    def one_source(i, _):
        gg = shared[1]
        sums = [jnp.zeros((8, LANES), jnp.float32)] * 4
        p_old = q_old = None
        s_edge[i] = ext[i, 0]
        for t in range(1, slices):
            s = ext[i, t]
            p = s - weight[t] * moved_sources(ext[i, t - 1], hs_ref[i, t - 1], shared[0, pl.ds(own, 8)], gg)
            if t < slices - 1:
                p_ref[i, t - 1] = p[:own]
                sums[0] += squares(s)
                sums[1] += squares(p)
            back = moved_weighted(weight[t] * p, wp_own[i, t - 1], hwp_ref[i, t - 1], hh_two[...], gg)
            if t == 1:
                kp_edge[i] = back
            else:
                q = p_old - back
                q_ref[i, t - 2] = q[:own]
                sums[2] += squares(q)
                if t > 2:
                    moved = moved_normal(q_old, q_own[i, t - 3], hq_ref[i, t - 3], hh_three[...], gg)
                    u = q[:own] - weight[t - 1, pl.ds(0, own)] * moved
                    t_ref[i, t - 3] = u
                    sums[3] += squares(u)
                q_old = q
            p_old = p
        for k in range(4):
            acc[k * count + i] = sums[k]
        return 0

    for i in range(count):
        one_source(i, 0)


def inner_operators(sources, phonons, bonds, above, below, parts):
    count, slices, rows, columns = sources.shape
    shape = lambda *n: jax.ShapeDtypeStruct(n, jnp.float32)
    field = lambda times: shape(count, times, rows, columns)
    wide = lambda n: shape(n, WIDE, columns)
    return pl.pallas_call(
        inner_kernel,
        out_shape=[
            field(slices - 2),
            field(slices - 2),
            field(slices - 3),
            wide(count),
            wide(count),
            wide(4),
            shape(4 * count, 8, LANES),
        ],
        in_specs=[VMEM] * 11,
        out_specs=[VMEM] * 7,
        scratch_shapes=[
            pltpu.VMEM((count, slices, WIDE, columns), jnp.float32),
            pltpu.VMEM((slices, WIDE, columns), jnp.float32),
            pltpu.VMEM((8, columns), jnp.float32),
            pltpu.VMEM((8, columns), jnp.float32),
        ],
        compiler_params=PARAMS,
        name="inner_operators",
    )(sources, phonons, bonds, above, below, *parts)


def early_kernel(
    before, s_ref, bond_ref, wp_own, hwp_own, weight_own, hs_ref, wp_ref, hwp_ref, q_ref, hq_ref, weight
):
    count, _, rows, _ = s_ref.shape
    for j in range(2):
        weight[j] = jnp.exp(coupling * before[EARLY * count + j])
    hh = hopping * bond_ref[0].astype(jnp.float32)
    gg = hopping * bond_ref[1].astype(jnp.float32)
    gg = jnp.where(lax.broadcasted_iota(jnp.int32, gg.shape, 0) < rows - 1, gg, 0.0)

    def one_source(i, _):
        s = [before[EARLY * i + j] for j in range(EARLY)] + [s_ref[i, 0]]
        w = [weight[0], weight[1], weight_own[0]]
        p, back = [], []
        for j in range(3):
            along = horizontal(s[j], hh)
            hs_ref[i, j] = along
            p.append(s[j + 1] - w[j] * (along + vertical(s[j], gg)))
        for j in range(1, 3):
            v = w[j] * p[j]
            along = horizontal(v, hh)
            wp_ref[i, j - 1] = v
            hwp_ref[i, j - 1] = along
            back.append(along + vertical(v, gg))
        back.append(hwp_own[i, 0] + vertical(wp_own[i, 0], gg))
        for j in range(3):
            q = p[j] - back[j]
            q_ref[i, j] = q
            hq_ref[i, j] = horizontal(q, hh)
        return 0

    lax.fori_loop(0, count, one_source, 0)


def early_parts(before, sources, bonds, own):
    count, _, rows, columns = sources.shape
    field = lambda n: jax.ShapeDtypeStruct((count, n, rows, columns), jnp.float32)
    return pl.pallas_call(
        early_kernel,
        out_shape=[field(3), field(2), field(2), field(3), field(3)]
        + [jax.ShapeDtypeStruct((2, rows, columns), jnp.float32)],
        in_specs=[VMEM] * 6,
        out_specs=[VMEM] * 6,
        compiler_params=PARAMS,
        name="early_parts",
    )(before, sources, bonds, own[1], own[2], own[5])


def outer_kernel(
    before, above, below, hs_ref, wp_own, hwp_ref, q_own, hq_ref, weight_own, q_inner, s_edge, kp_edge, shared, acc_inner,
    p_ref, q_ref, t_ref, partial_ref, ext, weight, acc, hh_two, hh_three,
):
    count = s_edge.shape[0]
    own = before.shape[1]
    corner, _ = corner_layout(count)
    build_tiles(hh_two, hh_three, shared.at[0], own)
    for i in range(count):
        for j in range(EARLY):
            widen(ext.at[i, j], before[EARLY * i + j], below, above, corner[i, j - EARLY])
    for j in range(2):
        slot = weight.at[j]
        row, n = corner[count, j - 2]
        slot[pl.ds(own, n)] = below[pl.ds(row, n)]
        slot[pl.ds(WIDE - n, n)] = above[pl.ds(row, n)]
        slot[pl.ds(own, 8)] = jnp.exp(coupling * slot[pl.ds(own, 8)])
        slot[pl.ds(0, own)] = weight_own[j]

    def one_source(i, _):
        gg, hh_halo = shared[1], shared[0, pl.ds(own, 8)]
        two, three = hh_two[...], hh_three[...]
        w = [weight[0], weight[1], shared[2], shared[3]]
        s = [ext[i, 0], ext[i, 1], ext[i, 2], s_edge[i]]
        p = [s[j + 1] - w[j] * moved_sources(s[j], hs_ref[i, j], hh_halo, gg) for j in range(3)]
        back = [moved_weighted(w[j] * p[j], wp_own[i, j - 1], hwp_ref[i, j - 1], two, gg) for j in (1, 2)]
        q = [p[0] - back[0], p[1] - back[1], p[2] - kp_edge[i]]
        moved = [moved_normal(q[j], q_own[i, j], hq_ref[i, j], three, gg) for j in range(3)]
        u = [x[:own] - w[j + 1][:own] * moved[j] for j, x in enumerate((q[1], q[2], q_inner[i, 0]))]
        for j in range(2):
            p_ref[i, j] = p[j + 1][:own]
            q_ref[i, j] = q[j + 1][:own]
        for j in range(3):
            t_ref[i, j] = u[j][:own]
        for k, fields in enumerate((s[2:], p[1:], q[1:], u)):
            acc[k * count + i] = acc_inner[k * count + i] + sum(squares(v) for v in fields)
        return 0

    for i in range(count):
        one_source(i, 0)
    lines = jnp.sum(acc[...], axis=1)
    lines = jnp.broadcast_to(jnp.sum(lines, axis=1, keepdims=True), lines.shape)
    at = lambda d: lax.broadcasted_iota(jnp.int32, lines.shape, d)
    row = jnp.sum(jnp.where(at(0) == at(1), lines, 0.0), axis=0, keepdims=True)
    partial_ref[...] = jnp.broadcast_to(row, partial_ref.shape)


def outer_operators(before, above, below, early, inner, everyone):
    _, q_inner, _, s_edge, kp_edge, shared, acc = inner
    count, _, rows, columns = q_inner.shape
    field = lambda times: jax.ShapeDtypeStruct((count, times, rows, columns), jnp.float32)
    return pl.pallas_call(
        outer_kernel,
        out_shape=[field(2), field(2), field(3), jax.ShapeDtypeStruct((everyone, LANES), jnp.float32)],
        in_specs=[VMEM] * 14,
        out_specs=[VMEM] * 4,
        scratch_shapes=[
            pltpu.VMEM((count, EARLY, WIDE, columns), jnp.float32),
            pltpu.VMEM((2, WIDE, columns), jnp.float32),
            pltpu.VMEM((4 * count, 8, LANES), jnp.float32),
            pltpu.VMEM((8, columns), jnp.float32),
            pltpu.VMEM((8, columns), jnp.float32),
        ],
        compiler_params=PARAMS,
        name="outer_operators",
    )(before, above, below, *early, q_inner, s_edge, kp_edge, shared, acc)


def force_kernel(
    mom_ref, s_ref, p_in, q_in, t_in, p_out, q_out, t_out, ph_ref, before, pi_ref, half_ref, early_ref, send_hbm,
    send_ref, sems,
):
    count, slices, rows, columns = s_ref.shape
    moments = jnp.sum(mom_ref[...], axis=0, keepdims=True)
    m = [moments] + [pltpu.roll(moments, LANES - count * k, 1) for k in range(1, 4)]
    alpha, square, cube = m[0] / m[1], m[2] / m[1], m[3] / m[1]
    spread = cube - square * square
    rows_of_both = [(alpha * cube - square) / spread] * count + [(1.0 - alpha * square) / spread] * count
    both = jnp.concatenate(rows_of_both, axis=0)
    at = lambda d: lax.broadcasted_iota(jnp.int32, both.shape, d)
    picked = jnp.where(at(1) == lax.rem(at(0), count), both, 0.0)
    picked = jnp.sum(picked, axis=1, keepdims=True)
    low = [picked[i : i + 1] for i in range(count)]
    high = [picked[count + i : count + i + 1] for i in range(count)]
    kept = EARLY * count
    phonon = lambda t: before[kept + 2 + t] if t < 0 else ph_ref[t]
    copies = []
    for t in range(-1, slices - 1):
        fermion = None
        for i in range(count):
            source = before[EARLY * i + EARLY - 1] if t < 0 else s_ref[i, t]
            p, q = (p_out[i, t + 1], q_out[i, t + 1]) if t < 1 else (p_in[i, t - 1], q_in[i, t - 1])
            x = low[i] * source + high[i] * q
            y = low[i] * p + high[i] * (t_out[i, t + 1] if t < 2 else t_in[i, t - 2])
            term = y * (x - y)
            fermion = term if fermion is None else fermion + term
        beside = phonon(t + 1) + phonon(t - 1)
        boson = restore * phonon(t) + spring * (2.0 * phonon(t) - beside)
        momentum = before[kept + 2] if t < 0 else pi_ref[t]
        half = momentum - 0.5 * stepsize * (boson + 2.0 * coupling * fermion)
        if t < 0:
            early_ref[...] = half
        else:
            half_ref[t] = half
        for r in range(0, rows, 2):
            for c in range(0, columns, LANES):
                send_ref[(r // 2) * (columns // LANES) + c // LANES, pl.ds(2 * (t + 1), 2)] = half[
                    r : r + 2, c : c + LANES
                ]
        if t % 4 == 2:
            tile = pl.ds(8 * (t // 4), 8)
            copy = pltpu.make_async_copy(send_ref.at[:, tile], send_hbm.at[:, tile], sems.at[t // 4])
            copy.start()
            copies.append(copy)
    for copy in copies:
        copy.wait()


def force(received, sources, inner, outer, phonons, before, momenta, peers):
    slices, rows, columns = phonons.shape
    shape = lambda *n: jax.ShapeDtypeStruct(n, jnp.float32)
    return pl.pallas_call(
        force_kernel,
        out_shape=[shape(slices - 1, rows, columns), shape(rows, columns), shape(peers, 2 * slices, LANES)],
        in_specs=[VMEM] * 11,
        out_specs=[VMEM, VMEM, pl.BlockSpec(memory_space=pltpu.HBM)],
        scratch_shapes=[
            pltpu.VMEM((peers, 2 * slices, LANES), jnp.float32),
            pltpu.SemaphoreType.DMA((slices // 4,)),
        ],
        compiler_params=PARAMS,
        name="force",
    )(received, sources, *inner[:3], *outer[:3], phonons, before, momenta)


def table_kernel(kernel_ref, table_ref):
    times = kernel_ref.shape[1]
    same = jnp.broadcast_to(pltpu.roll(kernel_ref[...], times - 1, 1), (times, times))
    shifted = pltpu.roll(same, 0, 1, stride=1, stride_axis=0)
    table_ref[...] = stepsize * jnp.transpose(shifted)


def circulant(kernel):
    times = kernel.shape[0]
    return pl.pallas_call(
        table_kernel,
        out_shape=jax.ShapeDtypeStruct((times, times), jnp.float32),
        in_specs=[VMEM],
        out_specs=VMEM,
        compiler_params=PARAMS,
        name="circulant",
        cost_estimate=pl.CostEstimate(flops=10**11, bytes_accessed=10**6, transcendentals=0),
    )(kernel[None])


def drift_kernel(table_ref, x_ref, out_ref):
    times = table_ref.shape[0]
    both = jnp.concatenate([x_ref[pl.ds(k, times, stride=2)] for k in range(2)], axis=1)
    mixed = jnp.dot(
        table_ref[...], both, precision=lax.Precision.HIGHEST, preferred_element_type=jnp.float32
    )
    for k in range(2):
        out_ref[pl.ds(k, times, stride=2)] = mixed[:, k * LANES : (k + 1) * LANES]


def drift(table, columns):
    flat = columns.reshape(-1, LANES)
    mixed = pl.pallas_call(
        drift_kernel,
        out_shape=jax.ShapeDtypeStruct(flat.shape, jnp.float32),
        in_specs=[VMEM] * 2,
        out_specs=VMEM,
        compiler_params=PARAMS,
        name="drift",
    )(table, flat)
    return mixed.reshape(columns.shape)


def join_kernel(half_ref, late_ref, all_ref):
    last = half_ref.shape[0]
    all_ref[pl.ds(0, last)] = half_ref[...]
    all_ref[last] = late_ref[...]


def join_times(half, late):
    return pl.pallas_call(
        join_kernel,
        out_shape=jax.ShapeDtypeStruct((half.shape[0] + 1,) + half.shape[1:], jnp.float32),
        in_specs=[VMEM] * 2,
        out_specs=VMEM,
        compiler_params=PARAMS,
        name="join_times",
    )(half, late)


def add_kernel(ph_ref, back_ref, out_hbm, out_ref, sems):
    slices, rows, columns = ph_ref.shape
    copies = []
    for t in range(slices):
        for r in range(0, rows, 2):
            for c in range(0, columns, LANES):
                moved = back_ref[(r // 2) * (columns // LANES) + c // LANES, pl.ds(2 * t, 2)]
                out_ref[t, pl.ds(r, 2), pl.ds(c, LANES)] = ph_ref[t, pl.ds(r, 2), pl.ds(c, LANES)] + moved
        copies.append(pltpu.make_async_copy(out_ref.at[t], out_hbm.at[t], sems.at[t]))
        copies[t].start()
    for copy in copies:
        copy.wait()


def add_drift(phonons, back):
    return pl.pallas_call(
        add_kernel,
        out_shape=jax.ShapeDtypeStruct(phonons.shape, jnp.float32),
        in_specs=[VMEM] * 2,
        out_specs=pl.BlockSpec(memory_space=pltpu.HBM),
        scratch_shapes=[
            pltpu.VMEM(phonons.shape, jnp.float32),
            pltpu.SemaphoreType.DMA((phonons.shape[0],)),
        ],
        compiler_params=PARAMS,
        name="add_drift",
    )(phonons, back)


def passed_along(block, axis, distance):
    count = lax.axis_size(axis)
    return lax.ppermute(block, axis, [((i - distance) % count, i) for i in range(count)])


def passed_diagonally(block, times, slabs):
    nt, ns = lax.axis_size("tm"), lax.axis_size("slab")
    route = [
        (((i - times) % nt) * ns + (j - slabs) % ns, i * ns + j) for i in range(nt) for j in range(ns)
    ]
    return lax.ppermute(block, ("tm", "slab"), route)


def body(sources, phonons, momenta, kernel, bonds):
    peers = lax.axis_size("tm")
    everyone = peers * lax.axis_size("slab")
    up, down, sources, phonons, bonds, last_momenta = pack_sides(sources, phonons, bonds, momenta)
    above = passed_along(up, "slab", 1)
    below = passed_along(down, "slab", -1)
    ahead = pack_ahead(sources, phonons, last_momenta)
    before = passed_along(ahead, "tm", 1)
    up_corner, down_corner = pack_corners(ahead)
    above_corner = passed_diagonally(up_corner, 1, 1)
    own, down_corner = lax.optimization_barrier((own_parts(sources, phonons, bonds), down_corner))
    below_corner = passed_diagonally(down_corner, 1, -1)
    side_halos = (above, below)
    early = early_parts(before, sources, bonds, own)
    (above, below), table, own, early = lax.optimization_barrier((side_halos, circulant(kernel), own, early))
    inner = inner_operators(sources, phonons, bonds, above, below, own)
    outer = outer_operators(before, above_corner, below_corner, early, inner, everyone)
    received = lax.all_to_all(outer[3], ("tm", "slab"), split_axis=0, concat_axis=0, tiled=True)
    half, half_before, send = force(received, sources, inner, outer, phonons, before, momenta, peers)
    columns = lax.all_to_all(send, "tm", split_axis=0, concat_axis=0, tiled=True)
    half_momenta = join_times(half, passed_along(half_before, "tm", -1))
    columns, half_momenta = lax.optimization_barrier((columns, half_momenta))
    mixed = drift(table, columns)
    back = lax.all_to_all(mixed, "tm", split_axis=0, concat_axis=0, tiled=True)
    return half_momenta, add_drift(phonons, back)


def solution(mesh):
    return jax.shard_map(
        body,
        mesh=mesh,
        in_specs=(
            P(None, "tm", "slab", None),
            P("tm", "slab", None),
            P("tm", "slab", None),
            P(),
            P(None, "slab", None),
        ),
        out_specs=(P("tm", "slab", None), P("tm", "slab", None)),
        check_vma=False,
    )
```

```python
import jax
import jax.numpy as jnp
from jax import lax
from jax.experimental import pallas as pl
from jax.experimental.pallas import tpu as pltpu
from jax.sharding import PartitionSpec as P

hopping = 0.1
coupling = 0.2
restore = 0.25
spring = 0.25
stepsize = 0.5

LANES = 128
WIDE = 24
EARLY = 3
VMEM = pl.BlockSpec(memory_space=pltpu.VMEM)
PARAMS = pltpu.CompilerParams(vmem_limit_bytes=28 * 2**20)


def layout(entries):
    at, row = {}, 0
    for key, rows in entries:
        at[key] = (row, rows)
        row += rows
    return at, -(-row // 8) * 8


def side_layout(count, slices):
    depth = lambda t: min(3, slices - t)
    entries = [((i, t), depth(t)) for i in range(count) for t in range(slices)]
    entries += [((count, t), min(2, depth(t))) for t in range(slices)]
    return layout(entries + [(("bond", 0), 2), (("bond", 1), 3)])


def corner_layout(count):
    entries = [((i, t), 2 if t == -3 else 3) for i in range(count) for t in (-3, -2, -1)]
    return layout(entries + [((count, -2), 1), ((count, -1), 2)])


def rows_of(ref, n, last):
    return ref[pl.ds(ref.shape[0] - n if last else 0, n)]


def side_kernel(s_hbm, ph_hbm, bond_hbm, pi_hbm, up, down, s_ref, ph_ref, bond_ref, pi_ref, sems):
    count, slices = s_ref.shape[:2]
    copies = [pltpu.make_async_copy(s_hbm.at[i], s_ref.at[i], sems.at[i]) for i in range(count)]
    copies.append(pltpu.make_async_copy(ph_hbm, ph_ref, sems.at[count]))
    copies.append(pltpu.make_async_copy(bond_hbm, bond_ref, sems.at[count + 1]))
    copies.append(pltpu.make_async_copy(pi_hbm.at[slices - 1], pi_ref, sems.at[count + 2]))
    for copy in copies:
        copy.start()
    side, _ = side_layout(count, slices)
    for i in range(count + 1):
        copies[i].wait()
        source = s_ref.at[i] if i < count else ph_ref
        for t in range(slices):
            row, n = side[i, t]
            up[pl.ds(row, n)] = rows_of(source.at[t], n, True)
            down[pl.ds(row, n)] = rows_of(source.at[t], n, False)
    copies[count + 1].wait()
    for k in range(2):
        row, n = side["bond", k]
        up[pl.ds(row, n)] = rows_of(bond_ref.at[k], n, True).astype(jnp.float32)
        down[pl.ds(row, n)] = rows_of(bond_ref.at[k], n, False).astype(jnp.float32)
    copies[count + 2].wait()


def pack_sides(sources, phonons, bonds, momenta):
    count, slices, rows, columns = sources.shape
    side = jax.ShapeDtypeStruct((side_layout(count, slices)[1], columns), jnp.float32)
    whole = [jax.ShapeDtypeStruct(x.shape, x.dtype) for x in (sources, phonons, bonds)]
    whole.append(jax.ShapeDtypeStruct(momenta.shape[1:], jnp.float32))
    return pl.pallas_call(
        side_kernel,
        out_shape=[side, side, *whole],
        in_specs=[pl.BlockSpec(memory_space=pltpu.HBM)] * 4,
        out_specs=[VMEM] * 6,
        scratch_shapes=[pltpu.SemaphoreType.DMA((count + 3,))],
        compiler_params=PARAMS,
        name="pack_sides",
    )(*(pltpu.with_memory_space_constraint(x, pltpu.HBM) for x in (sources, phonons, bonds, momenta)))


def ahead_kernel(s_ref, ph_ref, pi_ref, ahead):
    count, slices = s_ref.shape[:2]
    for i in range(count):
        for j in range(EARLY):
            ahead[EARLY * i + j] = s_ref[i, slices - EARLY + j]
    for j in range(2):
        ahead[EARLY * count + j] = ph_ref[slices - 2 + j]
    ahead[EARLY * count + 2] = pi_ref[...]


def pack_ahead(sources, phonons, last_momenta):
    count, _, rows, columns = sources.shape
    return pl.pallas_call(
        ahead_kernel,
        out_shape=jax.ShapeDtypeStruct((EARLY * count + 3, rows, columns), jnp.float32),
        in_specs=[VMEM] * 3,
        out_specs=VMEM,
        compiler_params=PARAMS,
        name="pack_ahead",
    )(sources, phonons, last_momenta)


def corner_kernel(ahead, up, down):
    count = (ahead.shape[0] - 3) // EARLY
    corner, _ = corner_layout(count)
    for (i, t), (row, n) in corner.items():
        source = ahead.at[EARLY * i + (EARLY if i < count else 2) + t]
        up[pl.ds(row, n)] = rows_of(source, n, True)
        down[pl.ds(row, n)] = rows_of(source, n, False)


def pack_corners(ahead):
    rows = corner_layout((ahead.shape[0] - 3) // EARLY)[1]
    return pl.pallas_call(
        corner_kernel,
        out_shape=[jax.ShapeDtypeStruct((rows, ahead.shape[2]), jnp.float32)] * 2,
        in_specs=[VMEM],
        out_specs=[VMEM] * 2,
        compiler_params=PARAMS,
        name="pack_corners",
    )(ahead)


def horizontal(v, hh):
    return v + (hh * pltpu.roll(v, v.shape[1] - 1, 1) + pltpu.roll(hh * v, 1, 1))


def vertical(v, gg):
    return gg * pltpu.roll(v, v.shape[0] - 1, 0) + pltpu.roll(gg * v, 1, 0)


def kinetic(v, hh, gg):
    return horizontal(v, hh) + vertical(v, gg)


def squares(v):
    columns = v.shape[1]
    v = v[:8] * v[:8] + v[8 : WIDE - 8] * v[8 : WIDE - 8]
    return sum(v[:, c : c + LANES] for c in range(0, columns, LANES))


def widen(slot, own, below, above, at):
    row, n = at
    slot[pl.ds(0, own.shape[0])] = own
    slot[pl.ds(own.shape[0], n)] = below[pl.ds(row, n)]
    slot[pl.ds(WIDE - n, n)] = above[pl.ds(row, n)]


def own_kernel(s_ref, ph_ref, bond_ref, hs_ref, wp_ref, hwp_ref, q_ref, hq_ref, weight):
    count, slices, rows, _ = s_ref.shape
    first = lax.axis_index("tm") == 0
    for t in range(slices):
        value = jnp.exp(coupling * ph_ref[t])
        weight[t] = value * jnp.where(first, -1.0, 1.0) if t == 0 else value
    hh = hopping * bond_ref[0].astype(jnp.float32)
    gg = hopping * bond_ref[1].astype(jnp.float32)
    gg = jnp.where(lax.broadcasted_iota(jnp.int32, gg.shape, 0) < rows - 1, gg, 0.0)

    def one_source(i, _):
        p_old = None
        for t in range(1, slices):
            v = s_ref[i, t - 1]
            along = horizontal(v, hh)
            hs_ref[i, t - 1] = along
            p = s_ref[i, t] - weight[t] * (along + vertical(v, gg))
            v = weight[t] * p
            along = horizontal(v, hh)
            wp_ref[i, t - 1] = v
            hwp_ref[i, t - 1] = along
            if 2 <= t < slices - 1:
                q = p_old - (along + vertical(v, gg))
                q_ref[i, t - 2] = q
                hq_ref[i, t - 2] = horizontal(q, hh)
            p_old = p
        return 0

    lax.fori_loop(0, count, one_source, 0)


def own_parts(sources, phonons, bonds):
    count, slices, rows, columns = sources.shape
    field = lambda n: jax.ShapeDtypeStruct((count, n, rows, columns), jnp.float32)
    return pl.pallas_call(
        own_kernel,
        out_shape=[field(slices - 1)] * 3
        + [field(slices - 3)] * 2
        + [jax.ShapeDtypeStruct(phonons.shape, jnp.float32)],
        in_specs=[VMEM] * 3,
        out_specs=[VMEM] * 6,
        compiler_params=PARAMS,
        name="own_parts",
    )(sources, phonons, bonds)


def build_tiles(hh_two, hh_three, hh, own):
    hh_two[...] = hh[pl.ds(own, 8)]
    hh_two[pl.ds(3, 1)] = hh[pl.ds(own - 1, 1)]
    hh_two[pl.ds(4, 1)] = hh[pl.ds(0, 1)]
    hh_three[...] = jnp.zeros_like(hh_three)
    hh_three[pl.ds(2, 2)] = hh[pl.ds(own - 2, 2)]
    hh_three[pl.ds(4, 2)] = hh[pl.ds(0, 2)]


def turn(v):
    return pltpu.roll(v, 4, 0)


def place_in(v):
    return lax.broadcasted_iota(jnp.int32, (8, v.shape[1]), 0)


def moved_sources(v, along, hh_halo, gg):
    own = along.shape[0]
    return jnp.concatenate([along, horizontal(v[own:], hh_halo)], axis=0) + vertical(v, gg)


def moved_weighted(v, v_own, along, hh_two, gg):
    own, sub = along.shape[0], place_in(v)
    change = v[:own] - v_own
    tile = jnp.where(sub == 3, turn(change[8:]), jnp.where(sub == 4, turn(change[:8]), v[own:]))
    tile = horizontal(tile, hh_two)
    turned = turn(tile)
    top = along[:8] + jnp.where(sub == 0, turned, 0.0)
    bottom = along[8:] + jnp.where(sub == 7, turned, 0.0)
    return jnp.concatenate([top, bottom, tile], axis=0) + vertical(v, gg)


def moved_normal(q, q_own, along, hh_three, gg):
    own, sub = along.shape[0], place_in(q)
    change = q[:own] - q_own
    tile = jnp.where(sub < 4, turn(change[8:]), turn(change[:8]))
    turned = turn(horizontal(tile, hh_three))
    top = along[:8] + jnp.where(sub < 2, turned, 0.0)
    bottom = along[8:] + jnp.where(sub > 5, turned, 0.0)
    return jnp.concatenate([top, bottom], axis=0) + vertical(q, gg)[:own]


def inner_kernel(
    s_ref, ph_ref, bond_ref, above, below, hs_ref, wp_own, hwp_ref, q_own, hq_ref, weight_own,
    p_ref, q_ref, t_ref, s_edge, kp_edge, shared, acc, ext, weight, hh_two, hh_three,
):
    count, slices, own, columns = s_ref.shape
    side, _ = side_layout(count, slices)
    for k in range(2):
        widen(shared.at[k], bond_ref[k].astype(jnp.float32), below, above, side["bond", k])
        shared[k] = hopping * shared[k]
    build_tiles(hh_two, hh_three, shared.at[0], own)
    first = lax.axis_index("tm") == 0
    for t in range(slices):
        slot = weight.at[t]
        widen(slot, weight_own[t], below, above, side[count, t])
        value = jnp.exp(coupling * slot[pl.ds(own, 8)])
        slot[pl.ds(own, 8)] = value * jnp.where(first, -1.0, 1.0) if t == 0 else value
        for i in range(count):
            widen(ext.at[i, t], s_ref[i, t], below, above, side[i, t])
    for j in range(2):
        shared[2 + j] = weight[j]

    def one_source(i, _):
        gg = shared[1]
        sums = [jnp.zeros((8, LANES), jnp.float32)] * 4
        p_old = q_old = None
        s_edge[i] = ext[i, 0]
        for t in range(1, slices):
            s = ext[i, t]
            p = s - weight[t] * moved_sources(ext[i, t - 1], hs_ref[i, t - 1], shared[0, pl.ds(own, 8)], gg)
            if t < slices - 1:
                p_ref[i, t - 1] = p[:own]
                sums[0] += squares(s)
                sums[1] += squares(p)
            back = moved_weighted(weight[t] * p, wp_own[i, t - 1], hwp_ref[i, t - 1], hh_two[...], gg)
            if t == 1:
                kp_edge[i] = back
            else:
                q = p_old - back
                q_ref[i, t - 2] = q[:own]
                sums[2] += squares(q)
                if t > 2:
                    moved = moved_normal(q_old, q_own[i, t - 3], hq_ref[i, t - 3], hh_three[...], gg)
                    u = q[:own] - weight[t - 1, pl.ds(0, own)] * moved
                    t_ref[i, t - 3] = u
                    sums[3] += squares(u)
                q_old = q
            p_old = p
        for k in range(4):
            acc[k * count + i] = sums[k]
        return 0

    lax.fori_loop(0, count, one_source, 0)


def inner_operators(sources, phonons, bonds, above, below, parts):
    count, slices, rows, columns = sources.shape
    shape = lambda *n: jax.ShapeDtypeStruct(n, jnp.float32)
    field = lambda times: shape(count, times, rows, columns)
    wide = lambda n: shape(n, WIDE, columns)
    return pl.pallas_call(
        inner_kernel,
        out_shape=[
            field(slices - 2),
            field(slices - 2),
            field(slices - 3),
            wide(count),
            wide(count),
            wide(4),
            shape(4 * count, 8, LANES),
        ],
        in_specs=[VMEM] * 11,
        out_specs=[VMEM] * 7,
        scratch_shapes=[
            pltpu.VMEM((count, slices, WIDE, columns), jnp.float32),
            pltpu.VMEM((slices, WIDE, columns), jnp.float32),
            pltpu.VMEM((8, columns), jnp.float32),
            pltpu.VMEM((8, columns), jnp.float32),
        ],
        compiler_params=PARAMS,
        name="inner_operators",
    )(sources, phonons, bonds, above, below, *parts)


def early_kernel(
    before, s_ref, bond_ref, wp_own, hwp_own, weight_own, hs_ref, wp_ref, hwp_ref, q_ref, hq_ref, weight
):
    count, _, rows, _ = s_ref.shape
    for j in range(2):
        weight[j] = jnp.exp(coupling * before[EARLY * count + j])
    hh = hopping * bond_ref[0].astype(jnp.float32)
    gg = hopping * bond_ref[1].astype(jnp.float32)
    gg = jnp.where(lax.broadcasted_iota(jnp.int32, gg.shape, 0) < rows - 1, gg, 0.0)

    def one_source(i, _):
        s = [before[EARLY * i + j] for j in range(EARLY)] + [s_ref[i, 0]]
        w = [weight[0], weight[1], weight_own[0]]
        p, back = [], []
        for j in range(3):
            along = horizontal(s[j], hh)
            hs_ref[i, j] = along
            p.append(s[j + 1] - w[j] * (along + vertical(s[j], gg)))
        for j in range(1, 3):
            v = w[j] * p[j]
            along = horizontal(v, hh)
            wp_ref[i, j - 1] = v
            hwp_ref[i, j - 1] = along
            back.append(along + vertical(v, gg))
        back.append(hwp_own[i, 0] + vertical(wp_own[i, 0], gg))
        for j in range(3):
            q = p[j] - back[j]
            q_ref[i, j] = q
            hq_ref[i, j] = horizontal(q, hh)
        return 0

    lax.fori_loop(0, count, one_source, 0)


def early_parts(before, sources, bonds, own):
    count, _, rows, columns = sources.shape
    field = lambda n: jax.ShapeDtypeStruct((count, n, rows, columns), jnp.float32)
    return pl.pallas_call(
        early_kernel,
        out_shape=[field(3), field(2), field(2), field(3), field(3)]
        + [jax.ShapeDtypeStruct((2, rows, columns), jnp.float32)],
        in_specs=[VMEM] * 6,
        out_specs=[VMEM] * 6,
        compiler_params=PARAMS,
        name="early_parts",
    )(before, sources, bonds, own[1], own[2], own[5])


def outer_kernel(
    before, above, below, hs_ref, wp_own, hwp_ref, q_own, hq_ref, weight_own, q_inner, s_edge, kp_edge, shared, acc_inner,
    p_ref, q_ref, t_ref, partial_ref, ext, weight, acc, hh_two, hh_three,
):
    count = s_edge.shape[0]
    own = before.shape[1]
    corner, _ = corner_layout(count)
    build_tiles(hh_two, hh_three, shared.at[0], own)
    for i in range(count):
        for j in range(EARLY):
            widen(ext.at[i, j], before[EARLY * i + j], below, above, corner[i, j - EARLY])
    for j in range(2):
        slot = weight.at[j]
        row, n = corner[count, j - 2]
        slot[pl.ds(own, n)] = below[pl.ds(row, n)]
        slot[pl.ds(WIDE - n, n)] = above[pl.ds(row, n)]
        slot[pl.ds(own, 8)] = jnp.exp(coupling * slot[pl.ds(own, 8)])
        slot[pl.ds(0, own)] = weight_own[j]

    def one_source(i, _):
        gg, hh_halo = shared[1], shared[0, pl.ds(own, 8)]
        two, three = hh_two[...], hh_three[...]
        w = [weight[0], weight[1], shared[2], shared[3]]
        s = [ext[i, 0], ext[i, 1], ext[i, 2], s_edge[i]]
        p = [s[j + 1] - w[j] * moved_sources(s[j], hs_ref[i, j], hh_halo, gg) for j in range(3)]
        back = [moved_weighted(w[j] * p[j], wp_own[i, j - 1], hwp_ref[i, j - 1], two, gg) for j in (1, 2)]
        q = [p[0] - back[0], p[1] - back[1], p[2] - kp_edge[i]]
        moved = [moved_normal(q[j], q_own[i, j], hq_ref[i, j], three, gg) for j in range(3)]
        u = [x[:own] - w[j + 1][:own] * moved[j] for j, x in enumerate((q[1], q[2], q_inner[i, 0]))]
        for j in range(2):
            p_ref[i, j] = p[j + 1][:own]
            q_ref[i, j] = q[j + 1][:own]
        for j in range(3):
            t_ref[i, j] = u[j][:own]
        for k, fields in enumerate((s[2:], p[1:], q[1:], u)):
            acc[k * count + i] = acc_inner[k * count + i] + sum(squares(v) for v in fields)
        return 0

    lax.fori_loop(0, count, one_source, 0)
    lines = jnp.sum(acc[...], axis=1)
    lines = jnp.broadcast_to(jnp.sum(lines, axis=1, keepdims=True), lines.shape)
    at = lambda d: lax.broadcasted_iota(jnp.int32, lines.shape, d)
    row = jnp.sum(jnp.where(at(0) == at(1), lines, 0.0), axis=0, keepdims=True)
    partial_ref[...] = jnp.broadcast_to(row, partial_ref.shape)


def outer_operators(before, above, below, early, inner, everyone):
    _, q_inner, _, s_edge, kp_edge, shared, acc = inner
    count, _, rows, columns = q_inner.shape
    field = lambda times: jax.ShapeDtypeStruct((count, times, rows, columns), jnp.float32)
    return pl.pallas_call(
        outer_kernel,
        out_shape=[field(2), field(2), field(3), jax.ShapeDtypeStruct((everyone, LANES), jnp.float32)],
        in_specs=[VMEM] * 14,
        out_specs=[VMEM] * 4,
        scratch_shapes=[
            pltpu.VMEM((count, EARLY, WIDE, columns), jnp.float32),
            pltpu.VMEM((2, WIDE, columns), jnp.float32),
            pltpu.VMEM((4 * count, 8, LANES), jnp.float32),
            pltpu.VMEM((8, columns), jnp.float32),
            pltpu.VMEM((8, columns), jnp.float32),
        ],
        compiler_params=PARAMS,
        name="outer_operators",
    )(before, above, below, *early, q_inner, s_edge, kp_edge, shared, acc)


def force_kernel(
    mom_ref, s_ref, p_in, q_in, t_in, p_out, q_out, t_out, ph_ref, before, pi_ref, half_ref, early_ref, send_hbm,
    send_ref, sems,
):
    count, slices, rows, columns = s_ref.shape
    moments = jnp.sum(mom_ref[...], axis=0, keepdims=True)
    m = [moments] + [pltpu.roll(moments, LANES - count * k, 1) for k in range(1, 4)]
    alpha, square, cube = m[0] / m[1], m[2] / m[1], m[3] / m[1]
    spread = cube - square * square
    rows_of_both = [(alpha * cube - square) / spread] * count + [(1.0 - alpha * square) / spread] * count
    both = jnp.concatenate(rows_of_both, axis=0)
    at = lambda d: lax.broadcasted_iota(jnp.int32, both.shape, d)
    picked = jnp.where(at(1) == lax.rem(at(0), count), both, 0.0)
    picked = jnp.sum(picked, axis=1, keepdims=True)
    low = [picked[i : i + 1] for i in range(count)]
    high = [picked[count + i : count + i + 1] for i in range(count)]
    kept = EARLY * count
    phonon = lambda t: before[kept + 2 + t] if t < 0 else ph_ref[t]
    copies = []
    for t in range(-1, slices - 1):
        fermion = None
        for i in range(count):
            source = before[EARLY * i + EARLY - 1] if t < 0 else s_ref[i, t]
            p, q = (p_out[i, t + 1], q_out[i, t + 1]) if t < 1 else (p_in[i, t - 1], q_in[i, t - 1])
            x = low[i] * source + high[i] * q
            y = low[i] * p + high[i] * (t_out[i, t + 1] if t < 2 else t_in[i, t - 2])
            term = y * (x - y)
            fermion = term if fermion is None else fermion + term
        beside = phonon(t + 1) + phonon(t - 1)
        boson = restore * phonon(t) + spring * (2.0 * phonon(t) - beside)
        momentum = before[kept + 2] if t < 0 else pi_ref[t]
        half = momentum - 0.5 * stepsize * (boson + 2.0 * coupling * fermion)
        if t < 0:
            early_ref[...] = half
        else:
            half_ref[t] = half
        for r in range(0, rows, 2):
            for c in range(0, columns, LANES):
                send_ref[(r // 2) * (columns // LANES) + c // LANES, pl.ds(2 * (t + 1), 2)] = half[
                    r : r + 2, c : c + LANES
                ]
        if t % 4 == 2:
            tile = pl.ds(8 * (t // 4), 8)
            copy = pltpu.make_async_copy(send_ref.at[:, tile], send_hbm.at[:, tile], sems.at[t // 4])
            copy.start()
            copies.append(copy)
    for copy in copies:
        copy.wait()


def force(received, sources, inner, outer, phonons, before, momenta, peers):
    slices, rows, columns = phonons.shape
    shape = lambda *n: jax.ShapeDtypeStruct(n, jnp.float32)
    return pl.pallas_call(
        force_kernel,
        out_shape=[shape(slices - 1, rows, columns), shape(rows, columns), shape(peers, 2 * slices, LANES)],
        in_specs=[VMEM] * 11,
        out_specs=[VMEM, VMEM, pl.BlockSpec(memory_space=pltpu.HBM)],
        scratch_shapes=[
            pltpu.VMEM((peers, 2 * slices, LANES), jnp.float32),
            pltpu.SemaphoreType.DMA((slices // 4,)),
        ],
        compiler_params=PARAMS,
        name="force",
    )(received, sources, *inner[:3], *outer[:3], phonons, before, momenta)


def table_kernel(kernel_ref, table_ref):
    times = kernel_ref.shape[1]
    same = jnp.broadcast_to(pltpu.roll(kernel_ref[...], times - 1, 1), (times, times))
    shifted = pltpu.roll(same, 0, 1, stride=1, stride_axis=0)
    table_ref[...] = stepsize * jnp.transpose(shifted)


def circulant(kernel):
    times = kernel.shape[0]
    return pl.pallas_call(
        table_kernel,
        out_shape=jax.ShapeDtypeStruct((times, times), jnp.float32),
        in_specs=[VMEM],
        out_specs=VMEM,
        compiler_params=PARAMS,
        name="circulant",
        cost_estimate=pl.CostEstimate(flops=10**11, bytes_accessed=10**6, transcendentals=0),
    )(kernel[None])


def drift_kernel(table_ref, x_ref, out_ref):
    times = table_ref.shape[0]
    both = jnp.concatenate([x_ref[pl.ds(k, times, stride=2)] for k in range(2)], axis=1)
    mixed = jnp.dot(
        table_ref[...], both, precision=lax.Precision.HIGHEST, preferred_element_type=jnp.float32
    )
    for k in range(2):
        out_ref[pl.ds(k, times, stride=2)] = mixed[:, k * LANES : (k + 1) * LANES]


def drift(table, columns):
    flat = columns.reshape(-1, LANES)
    mixed = pl.pallas_call(
        drift_kernel,
        out_shape=jax.ShapeDtypeStruct(flat.shape, jnp.float32),
        in_specs=[VMEM] * 2,
        out_specs=VMEM,
        compiler_params=PARAMS,
        name="drift",
    )(table, flat)
    return mixed.reshape(columns.shape)


def join_kernel(half_ref, late_ref, all_ref):
    last = half_ref.shape[0]
    all_ref[pl.ds(0, last)] = half_ref[...]
    all_ref[last] = late_ref[...]


def join_times(half, late):
    return pl.pallas_call(
        join_kernel,
        out_shape=jax.ShapeDtypeStruct((half.shape[0] + 1,) + half.shape[1:], jnp.float32),
        in_specs=[VMEM] * 2,
        out_specs=VMEM,
        compiler_params=PARAMS,
        name="join_times",
    )(half, late)


def add_kernel(ph_ref, back_ref, out_hbm, out_ref, sems):
    slices, rows, columns = ph_ref.shape
    copies = []
    for t in range(slices):
        for r in range(0, rows, 2):
            for c in range(0, columns, LANES):
                moved = back_ref[(r // 2) * (columns // LANES) + c // LANES, pl.ds(2 * t, 2)]
                out_ref[t, pl.ds(r, 2), pl.ds(c, LANES)] = ph_ref[t, pl.ds(r, 2), pl.ds(c, LANES)] + moved
        copies.append(pltpu.make_async_copy(out_ref.at[t], out_hbm.at[t], sems.at[t]))
        copies[t].start()
    for copy in copies:
        copy.wait()


def add_drift(phonons, back):
    return pl.pallas_call(
        add_kernel,
        out_shape=jax.ShapeDtypeStruct(phonons.shape, jnp.float32),
        in_specs=[VMEM] * 2,
        out_specs=pl.BlockSpec(memory_space=pltpu.HBM),
        scratch_shapes=[
            pltpu.VMEM(phonons.shape, jnp.float32),
            pltpu.SemaphoreType.DMA((phonons.shape[0],)),
        ],
        compiler_params=PARAMS,
        name="add_drift",
    )(phonons, back)


def passed_along(block, axis, distance):
    count = lax.axis_size(axis)
    return lax.ppermute(block, axis, [((i - distance) % count, i) for i in range(count)])


def passed_diagonally(block, times, slabs):
    nt, ns = lax.axis_size("tm"), lax.axis_size("slab")
    route = [
        (((i - times) % nt) * ns + (j - slabs) % ns, i * ns + j) for i in range(nt) for j in range(ns)
    ]
    return lax.ppermute(block, ("tm", "slab"), route)


def body(sources, phonons, momenta, kernel, bonds):
    peers = lax.axis_size("tm")
    everyone = peers * lax.axis_size("slab")
    up, down, sources, phonons, bonds, last_momenta = pack_sides(sources, phonons, bonds, momenta)
    above = passed_along(up, "slab", 1)
    below = passed_along(down, "slab", -1)
    ahead = pack_ahead(sources, phonons, last_momenta)
    before = passed_along(ahead, "tm", 1)
    own, corner_slices = lax.optimization_barrier((own_parts(sources, phonons, bonds), ahead))
    up_corner, down_corner = pack_corners(corner_slices)
    above_corner = passed_diagonally(up_corner, 1, 1)
    below_corner = passed_diagonally(down_corner, 1, -1)
    side_halos = (above, below)
    early = early_parts(before, sources, bonds, own)
    (above, below), table, own, early = lax.optimization_barrier((side_halos, circulant(kernel), own, early))
    inner = inner_operators(sources, phonons, bonds, above, below, own)
    outer = outer_operators(before, above_corner, below_corner, early, inner, everyone)
    received = lax.all_to_all(outer[3], ("tm", "slab"), split_axis=0, concat_axis=0, tiled=True)
    half, half_before, send = force(received, sources, inner, outer, phonons, before, momenta, peers)
    columns = lax.all_to_all(send, "tm", split_axis=0, concat_axis=0, tiled=True)
    half_momenta = join_times(half, passed_along(half_before, "tm", -1))
    columns, half_momenta = lax.optimization_barrier((columns, half_momenta))
    mixed = drift(table, columns)
    back = lax.all_to_all(mixed, "tm", split_axis=0, concat_axis=0, tiled=True)
    return half_momenta, add_drift(phonons, back)


def solution(mesh):
    return jax.shard_map(
        body,
        mesh=mesh,
        in_specs=(
            P(None, "tm", "slab", None),
            P("tm", "slab", None),
            P("tm", "slab", None),
            P(),
            P(None, "slab", None),
        ),
        out_specs=(P("tm", "slab", None), P("tm", "slab", None)),
        check_vma=False,
    )
```

```python
import jax
import jax.numpy as jnp
from jax import lax
from jax.experimental import pallas as pl
from jax.experimental.pallas import tpu as pltpu
from jax.sharding import PartitionSpec as P

hopping = 0.1
coupling = 0.2
restore = 0.25
spring = 0.25
stepsize = 0.5

LANES = 128
WIDE = 24
EARLY = 3
VMEM = pl.BlockSpec(memory_space=pltpu.VMEM)
PARAMS = pltpu.CompilerParams(vmem_limit_bytes=28 * 2**20)


def layout(entries):
    at, row = {}, 0
    for key, rows in entries:
        at[key] = (row, rows)
        row += rows
    return at, -(-row // 8) * 8


def side_layout(count, slices):
    depth = lambda t: min(3, slices - t)
    entries = [((i, t), depth(t)) for i in range(count) for t in range(slices)]
    entries += [((count, t), min(2, depth(t))) for t in range(slices)]
    return layout(entries + [(("bond", 0), 2), (("bond", 1), 3)])


def corner_layout(count):
    entries = [((i, t), 2 if t == -3 else 3) for i in range(count) for t in (-3, -2, -1)]
    return layout(entries + [((count, -2), 1), ((count, -1), 2)])


def rows_of(ref, n, last):
    return ref[pl.ds(ref.shape[0] - n if last else 0, n)]


def side_kernel(s_hbm, ph_hbm, bond_hbm, pi_hbm, up, down, s_ref, ph_ref, bond_ref, pi_ref, sems):
    count, slices = s_ref.shape[:2]
    copies = [pltpu.make_async_copy(s_hbm.at[i], s_ref.at[i], sems.at[i]) for i in range(count)]
    copies.append(pltpu.make_async_copy(ph_hbm, ph_ref, sems.at[count]))
    copies.append(pltpu.make_async_copy(bond_hbm, bond_ref, sems.at[count + 1]))
    copies.append(pltpu.make_async_copy(pi_hbm.at[slices - 1], pi_ref, sems.at[count + 2]))
    for copy in copies:
        copy.start()
    side, _ = side_layout(count, slices)
    for i in range(count + 1):
        copies[i].wait()
        source = s_ref.at[i] if i < count else ph_ref
        for t in range(slices):
            row, n = side[i, t]
            up[pl.ds(row, n)] = rows_of(source.at[t], n, True)
            down[pl.ds(row, n)] = rows_of(source.at[t], n, False)
    copies[count + 1].wait()
    for k in range(2):
        row, n = side["bond", k]
        up[pl.ds(row, n)] = rows_of(bond_ref.at[k], n, True).astype(jnp.float32)
        down[pl.ds(row, n)] = rows_of(bond_ref.at[k], n, False).astype(jnp.float32)
    copies[count + 2].wait()


def pack_sides(sources, phonons, bonds, momenta):
    count, slices, rows, columns = sources.shape
    side = jax.ShapeDtypeStruct((side_layout(count, slices)[1], columns), jnp.float32)
    whole = [jax.ShapeDtypeStruct(x.shape, x.dtype) for x in (sources, phonons, bonds)]
    whole.append(jax.ShapeDtypeStruct(momenta.shape[1:], jnp.float32))
    return pl.pallas_call(
        side_kernel,
        out_shape=[side, side, *whole],
        in_specs=[pl.BlockSpec(memory_space=pltpu.HBM)] * 4,
        out_specs=[VMEM] * 6,
        scratch_shapes=[pltpu.SemaphoreType.DMA((count + 3,))],
        compiler_params=PARAMS,
        name="pack_sides",
    )(*(pltpu.with_memory_space_constraint(x, pltpu.HBM) for x in (sources, phonons, bonds, momenta)))


def ahead_kernel(s_ref, ph_ref, pi_ref, ahead):
    count, slices = s_ref.shape[:2]
    for i in range(count):
        for j in range(EARLY):
            ahead[EARLY * i + j] = s_ref[i, slices - EARLY + j]
    for j in range(2):
        ahead[EARLY * count + j] = ph_ref[slices - 2 + j]
    ahead[EARLY * count + 2] = pi_ref[...]


def pack_ahead(sources, phonons, last_momenta):
    count, _, rows, columns = sources.shape
    return pl.pallas_call(
        ahead_kernel,
        out_shape=jax.ShapeDtypeStruct((EARLY * count + 3, rows, columns), jnp.float32),
        in_specs=[VMEM] * 3,
        out_specs=VMEM,
        compiler_params=PARAMS,
        name="pack_ahead",
    )(sources, phonons, last_momenta)


def corner_kernel(ahead, up, down):
    count = (ahead.shape[0] - 3) // EARLY
    corner, _ = corner_layout(count)
    for (i, t), (row, n) in corner.items():
        source = ahead.at[EARLY * i + (EARLY if i < count else 2) + t]
        up[pl.ds(row, n)] = rows_of(source, n, True)
        down[pl.ds(row, n)] = rows_of(source, n, False)


def pack_corners(ahead):
    rows = corner_layout((ahead.shape[0] - 3) // EARLY)[1]
    return pl.pallas_call(
        corner_kernel,
        out_shape=[jax.ShapeDtypeStruct((rows, ahead.shape[2]), jnp.float32)] * 2,
        in_specs=[VMEM],
        out_specs=[VMEM] * 2,
        compiler_params=PARAMS,
        name="pack_corners",
    )(ahead)


def horizontal(v, hh):
    return v + (hh * pltpu.roll(v, v.shape[1] - 1, 1) + pltpu.roll(hh * v, 1, 1))


def vertical(v, gg):
    return gg * pltpu.roll(v, v.shape[0] - 1, 0) + pltpu.roll(gg * v, 1, 0)


def kinetic(v, hh, gg):
    return horizontal(v, hh) + vertical(v, gg)


def squares(v):
    columns = v.shape[1]
    v = v[:8] * v[:8] + v[8 : WIDE - 8] * v[8 : WIDE - 8]
    return sum(v[:, c : c + LANES] for c in range(0, columns, LANES))


def widen(slot, own, below, above, at):
    row, n = at
    slot[pl.ds(0, own.shape[0])] = own
    slot[pl.ds(own.shape[0], n)] = below[pl.ds(row, n)]
    slot[pl.ds(WIDE - n, n)] = above[pl.ds(row, n)]


def own_kernel(s_ref, ph_ref, bond_ref, hs_ref, wp_ref, hwp_ref, q_ref, hq_ref, weight):
    count, slices, rows, _ = s_ref.shape
    first = lax.axis_index("tm") == 0
    for t in range(slices):
        value = jnp.exp(coupling * ph_ref[t])
        weight[t] = value * jnp.where(first, -1.0, 1.0) if t == 0 else value
    hh = hopping * bond_ref[0].astype(jnp.float32)
    gg = hopping * bond_ref[1].astype(jnp.float32)
    gg = jnp.where(lax.broadcasted_iota(jnp.int32, gg.shape, 0) < rows - 1, gg, 0.0)

    def one_source(i, _):
        p_old = None
        for t in range(1, slices):
            v = s_ref[i, t - 1]
            along = horizontal(v, hh)
            hs_ref[i, t - 1] = along
            p = s_ref[i, t] - weight[t] * (along + vertical(v, gg))
            v = weight[t] * p
            along = horizontal(v, hh)
            wp_ref[i, t - 1] = v
            hwp_ref[i, t - 1] = along
            if 2 <= t < slices - 1:
                q = p_old - (along + vertical(v, gg))
                q_ref[i, t - 2] = q
                hq_ref[i, t - 2] = horizontal(q, hh)
            p_old = p
        return 0

    lax.fori_loop(0, count, one_source, 0)


def own_parts(sources, phonons, bonds):
    count, slices, rows, columns = sources.shape
    field = lambda n: jax.ShapeDtypeStruct((count, n, rows, columns), jnp.float32)
    return pl.pallas_call(
        own_kernel,
        out_shape=[field(slices - 1)] * 3
        + [field(slices - 3)] * 2
        + [jax.ShapeDtypeStruct(phonons.shape, jnp.float32)],
        in_specs=[VMEM] * 3,
        out_specs=[VMEM] * 6,
        compiler_params=PARAMS,
        name="own_parts",
    )(sources, phonons, bonds)


def build_tiles(hh_two, hh_three, hh, own):
    hh_two[...] = hh[pl.ds(own, 8)]
    hh_two[pl.ds(3, 1)] = hh[pl.ds(own - 1, 1)]
    hh_two[pl.ds(4, 1)] = hh[pl.ds(0, 1)]
    hh_three[...] = jnp.zeros_like(hh_three)
    hh_three[pl.ds(2, 2)] = hh[pl.ds(own - 2, 2)]
    hh_three[pl.ds(4, 2)] = hh[pl.ds(0, 2)]


def turn(v):
    return pltpu.roll(v, 4, 0)


def place_in(v):
    return lax.broadcasted_iota(jnp.int32, (8, v.shape[1]), 0)


def moved_sources(v, along, hh_halo, gg):
    own = along.shape[0]
    return jnp.concatenate([along, horizontal(v[own:], hh_halo)], axis=0) + vertical(v, gg)


def moved_weighted(v, v_own, along, hh_two, gg):
    own, sub = along.shape[0], place_in(v)
    change = v[:own] - v_own
    tile = jnp.where(sub == 3, turn(change[8:]), jnp.where(sub == 4, turn(change[:8]), v[own:]))
    tile = horizontal(tile, hh_two)
    turned = turn(tile)
    top = along[:8] + jnp.where(sub == 0, turned, 0.0)
    bottom = along[8:] + jnp.where(sub == 7, turned, 0.0)
    return jnp.concatenate([top, bottom, tile], axis=0) + vertical(v, gg)


def moved_normal(q, q_own, along, hh_three, gg):
    own, sub = along.shape[0], place_in(q)
    change = q[:own] - q_own
    tile = jnp.where(sub < 4, turn(change[8:]), turn(change[:8]))
    turned = turn(horizontal(tile, hh_three))
    top = along[:8] + jnp.where(sub < 2, turned, 0.0)
    bottom = along[8:] + jnp.where(sub > 5, turned, 0.0)
    return jnp.concatenate([top, bottom], axis=0) + vertical(q, gg)[:own]


def inner_kernel(
    s_ref, ph_ref, bond_ref, above, below, hs_ref, wp_own, hwp_ref, q_own, hq_ref, weight_own,
    p_ref, q_ref, t_ref, s_edge, kp_edge, shared, acc, ext, weight, hh_two, hh_three,
):
    count, slices, own, columns = s_ref.shape
    side, _ = side_layout(count, slices)
    for k in range(2):
        widen(shared.at[k], bond_ref[k].astype(jnp.float32), below, above, side["bond", k])
        shared[k] = hopping * shared[k]
    build_tiles(hh_two, hh_three, shared.at[0], own)
    first = lax.axis_index("tm") == 0
    for t in range(slices):
        slot = weight.at[t]
        widen(slot, weight_own[t], below, above, side[count, t])
        value = jnp.exp(coupling * slot[pl.ds(own, 8)])
        slot[pl.ds(own, 8)] = value * jnp.where(first, -1.0, 1.0) if t == 0 else value
        for i in range(count):
            widen(ext.at[i, t], s_ref[i, t], below, above, side[i, t])
    for j in range(2):
        shared[2 + j] = weight[j]

    def one_source(i, _):
        gg = shared[1]
        sums = [jnp.zeros((8, LANES), jnp.float32)] * 4
        p_old = q_old = None
        s_edge[i] = ext[i, 0]
        for t in range(1, slices):
            s = ext[i, t]
            p = s - weight[t] * moved_sources(ext[i, t - 1], hs_ref[i, t - 1], shared[0, pl.ds(own, 8)], gg)
            if t < slices - 1:
                p_ref[i, t - 1] = p[:own]
                sums[0] += squares(s)
                sums[1] += squares(p)
            back = moved_weighted(weight[t] * p, wp_own[i, t - 1], hwp_ref[i, t - 1], hh_two[...], gg)
            if t == 1:
                kp_edge[i] = back
            else:
                q = p_old - back
                q_ref[i, t - 2] = q[:own]
                sums[2] += squares(q)
                if t > 2:
                    moved = moved_normal(q_old, q_own[i, t - 3], hq_ref[i, t - 3], hh_three[...], gg)
                    u = q[:own] - weight[t - 1, pl.ds(0, own)] * moved
                    t_ref[i, t - 3] = u
                    sums[3] += squares(u)
                q_old = q
            p_old = p
        for k in range(4):
            acc[k * count + i] = sums[k]
        return 0

    for i in range(count):
        one_source(i, 0)


def inner_operators(sources, phonons, bonds, above, below, parts):
    count, slices, rows, columns = sources.shape
    shape = lambda *n: jax.ShapeDtypeStruct(n, jnp.float32)
    field = lambda times: shape(count, times, rows, columns)
    wide = lambda n: shape(n, WIDE, columns)
    return pl.pallas_call(
        inner_kernel,
        out_shape=[
            field(slices - 2),
            field(slices - 2),
            field(slices - 3),
            wide(count),
            wide(count),
            wide(4),
            shape(4 * count, 8, LANES),
        ],
        in_specs=[VMEM] * 11,
        out_specs=[VMEM] * 7,
        scratch_shapes=[
            pltpu.VMEM((count, slices, WIDE, columns), jnp.float32),
            pltpu.VMEM((slices, WIDE, columns), jnp.float32),
            pltpu.VMEM((8, columns), jnp.float32),
            pltpu.VMEM((8, columns), jnp.float32),
        ],
        compiler_params=PARAMS,
        name="inner_operators",
    )(sources, phonons, bonds, above, below, *parts)


def early_kernel(
    before, s_ref, bond_ref, wp_own, hwp_own, weight_own, hs_ref, wp_ref, hwp_ref, q_ref, hq_ref, weight
):
    count, _, rows, _ = s_ref.shape
    for j in range(2):
        weight[j] = jnp.exp(coupling * before[EARLY * count + j])
    hh = hopping * bond_ref[0].astype(jnp.float32)
    gg = hopping * bond_ref[1].astype(jnp.float32)
    gg = jnp.where(lax.broadcasted_iota(jnp.int32, gg.shape, 0) < rows - 1, gg, 0.0)

    def one_source(i, _):
        s = [before[EARLY * i + j] for j in range(EARLY)] + [s_ref[i, 0]]
        w = [weight[0], weight[1], weight_own[0]]
        p, back = [], []
        for j in range(3):
            along = horizontal(s[j], hh)
            hs_ref[i, j] = along
            p.append(s[j + 1] - w[j] * (along + vertical(s[j], gg)))
        for j in range(1, 3):
            v = w[j] * p[j]
            along = horizontal(v, hh)
            wp_ref[i, j - 1] = v
            hwp_ref[i, j - 1] = along
            back.append(along + vertical(v, gg))
        back.append(hwp_own[i, 0] + vertical(wp_own[i, 0], gg))
        for j in range(3):
            q = p[j] - back[j]
            q_ref[i, j] = q
            hq_ref[i, j] = horizontal(q, hh)
        return 0

    lax.fori_loop(0, count, one_source, 0)


def early_parts(before, sources, bonds, own):
    count, _, rows, columns = sources.shape
    field = lambda n: jax.ShapeDtypeStruct((count, n, rows, columns), jnp.float32)
    return pl.pallas_call(
        early_kernel,
        out_shape=[field(3), field(2), field(2), field(3), field(3)]
        + [jax.ShapeDtypeStruct((2, rows, columns), jnp.float32)],
        in_specs=[VMEM] * 6,
        out_specs=[VMEM] * 6,
        compiler_params=PARAMS,
        name="early_parts",
    )(before, sources, bonds, own[1], own[2], own[5])


def outer_kernel(
    before, above, below, hs_ref, wp_own, hwp_ref, q_own, hq_ref, weight_own, q_inner, s_edge, kp_edge, shared, acc_inner,
    p_ref, q_ref, t_ref, partial_ref, ext, weight, acc, hh_two, hh_three,
):
    count = s_edge.shape[0]
    own = before.shape[1]
    corner, _ = corner_layout(count)
    build_tiles(hh_two, hh_three, shared.at[0], own)
    for i in range(count):
        for j in range(EARLY):
            widen(ext.at[i, j], before[EARLY * i + j], below, above, corner[i, j - EARLY])
    for j in range(2):
        slot = weight.at[j]
        row, n = corner[count, j - 2]
        slot[pl.ds(own, n)] = below[pl.ds(row, n)]
        slot[pl.ds(WIDE - n, n)] = above[pl.ds(row, n)]
        slot[pl.ds(own, 8)] = jnp.exp(coupling * slot[pl.ds(own, 8)])
        slot[pl.ds(0, own)] = weight_own[j]

    def one_source(i, _):
        gg, hh_halo = shared[1], shared[0, pl.ds(own, 8)]
        two, three = hh_two[...], hh_three[...]
        w = [weight[0], weight[1], shared[2], shared[3]]
        s = [ext[i, 0], ext[i, 1], ext[i, 2], s_edge[i]]
        p = [s[j + 1] - w[j] * moved_sources(s[j], hs_ref[i, j], hh_halo, gg) for j in range(3)]
        back = [moved_weighted(w[j] * p[j], wp_own[i, j - 1], hwp_ref[i, j - 1], two, gg) for j in (1, 2)]
        q = [p[0] - back[0], p[1] - back[1], p[2] - kp_edge[i]]
        moved = [moved_normal(q[j], q_own[i, j], hq_ref[i, j], three, gg) for j in range(3)]
        u = [x[:own] - w[j + 1][:own] * moved[j] for j, x in enumerate((q[1], q[2], q_inner[i, 0]))]
        for j in range(2):
            p_ref[i, j] = p[j + 1][:own]
            q_ref[i, j] = q[j + 1][:own]
        for j in range(3):
            t_ref[i, j] = u[j][:own]
        for k, fields in enumerate((s[2:], p[1:], q[1:], u)):
            acc[k * count + i] = acc_inner[k * count + i] + sum(squares(v) for v in fields)
        return 0

    for i in range(count):
        one_source(i, 0)
    lines = jnp.sum(acc[...], axis=1)
    lines = jnp.broadcast_to(jnp.sum(lines, axis=1, keepdims=True), lines.shape)
    at = lambda d: lax.broadcasted_iota(jnp.int32, lines.shape, d)
    row = jnp.sum(jnp.where(at(0) == at(1), lines, 0.0), axis=0, keepdims=True)
    partial_ref[...] = jnp.broadcast_to(row, partial_ref.shape)


def outer_operators(before, above, below, early, inner, everyone):
    _, q_inner, _, s_edge, kp_edge, shared, acc = inner
    count, _, rows, columns = q_inner.shape
    field = lambda times: jax.ShapeDtypeStruct((count, times, rows, columns), jnp.float32)
    return pl.pallas_call(
        outer_kernel,
        out_shape=[field(2), field(2), field(3), jax.ShapeDtypeStruct((everyone, LANES), jnp.float32)],
        in_specs=[VMEM] * 14,
        out_specs=[VMEM] * 4,
        scratch_shapes=[
            pltpu.VMEM((count, EARLY, WIDE, columns), jnp.float32),
            pltpu.VMEM((2, WIDE, columns), jnp.float32),
            pltpu.VMEM((4 * count, 8, LANES), jnp.float32),
            pltpu.VMEM((8, columns), jnp.float32),
            pltpu.VMEM((8, columns), jnp.float32),
        ],
        compiler_params=PARAMS,
        name="outer_operators",
    )(before, above, below, *early, q_inner, s_edge, kp_edge, shared, acc)


def force_kernel(
    mom_ref, s_ref, p_in, q_in, t_in, p_out, q_out, t_out, ph_ref, before, pi_ref, half_ref, early_ref, send_hbm,
    send_ref, sems,
):
    count, slices, rows, columns = s_ref.shape
    moments = jnp.sum(mom_ref[...], axis=0, keepdims=True)
    m = [moments] + [pltpu.roll(moments, LANES - count * k, 1) for k in range(1, 4)]
    alpha, square, cube = m[0] / m[1], m[2] / m[1], m[3] / m[1]
    spread = cube - square * square
    rows_of_both = [(alpha * cube - square) / spread] * count + [(1.0 - alpha * square) / spread] * count
    both = jnp.concatenate(rows_of_both, axis=0)
    at = lambda d: lax.broadcasted_iota(jnp.int32, both.shape, d)
    picked = jnp.where(at(1) == lax.rem(at(0), count), both, 0.0)
    picked = jnp.sum(picked, axis=1, keepdims=True)
    low = [picked[i : i + 1] for i in range(count)]
    high = [picked[count + i : count + i + 1] for i in range(count)]
    kept = EARLY * count
    phonon = lambda t: before[kept + 2 + t] if t < 0 else ph_ref[t]
    copies = []
    for t in range(-1, slices - 1):
        fermion = None
        for i in range(count):
            source = before[EARLY * i + EARLY - 1] if t < 0 else s_ref[i, t]
            p, q = (p_out[i, t + 1], q_out[i, t + 1]) if t < 1 else (p_in[i, t - 1], q_in[i, t - 1])
            x = low[i] * source + high[i] * q
            y = low[i] * p + high[i] * (t_out[i, t + 1] if t < 2 else t_in[i, t - 2])
            term = y * (x - y)
            fermion = term if fermion is None else fermion + term
        beside = phonon(t + 1) + phonon(t - 1)
        boson = restore * phonon(t) + spring * (2.0 * phonon(t) - beside)
        momentum = before[kept + 2] if t < 0 else pi_ref[t]
        half = momentum - 0.5 * stepsize * (boson + 2.0 * coupling * fermion)
        if t < 0:
            early_ref[...] = half
        else:
            half_ref[t] = half
        for r in range(0, rows, 2):
            for c in range(0, columns, LANES):
                send_ref[(r // 2) * (columns // LANES) + c // LANES, pl.ds(2 * (t + 1), 2)] = half[
                    r : r + 2, c : c + LANES
                ]
        if t % 4 == 2:
            tile = pl.ds(8 * (t // 4), 8)
            copy = pltpu.make_async_copy(send_ref.at[:, tile], send_hbm.at[:, tile], sems.at[t // 4])
            copy.start()
            copies.append(copy)
    for copy in copies:
        copy.wait()


def force(received, sources, inner, outer, phonons, before, momenta, peers):
    slices, rows, columns = phonons.shape
    shape = lambda *n: jax.ShapeDtypeStruct(n, jnp.float32)
    return pl.pallas_call(
        force_kernel,
        out_shape=[shape(slices - 1, rows, columns), shape(rows, columns), shape(peers, 2 * slices, LANES)],
        in_specs=[VMEM] * 11,
        out_specs=[VMEM, VMEM, pl.BlockSpec(memory_space=pltpu.HBM)],
        scratch_shapes=[
            pltpu.VMEM((peers, 2 * slices, LANES), jnp.float32),
            pltpu.SemaphoreType.DMA((slices // 4,)),
        ],
        compiler_params=PARAMS,
        name="force",
    )(received, sources, *inner[:3], *outer[:3], phonons, before, momenta)


def table_kernel(kernel_ref, table_ref):
    times = kernel_ref.shape[1]
    same = jnp.broadcast_to(pltpu.roll(kernel_ref[...], times - 1, 1), (times, times))
    shifted = pltpu.roll(same, 0, 1, stride=1, stride_axis=0)
    table_ref[...] = stepsize * jnp.transpose(shifted)


def circulant(kernel):
    times = kernel.shape[0]
    return pl.pallas_call(
        table_kernel,
        out_shape=jax.ShapeDtypeStruct((times, times), jnp.float32),
        in_specs=[VMEM],
        out_specs=VMEM,
        compiler_params=PARAMS,
        name="circulant",
        cost_estimate=pl.CostEstimate(flops=10**11, bytes_accessed=10**6, transcendentals=0),
    )(kernel[None])


def drift_kernel(table_ref, x_ref, out_ref):
    times = table_ref.shape[0]
    both = jnp.concatenate([x_ref[pl.ds(k, times, stride=2)] for k in range(2)], axis=1)
    mixed = jnp.dot(
        table_ref[...], both, precision=lax.Precision.HIGHEST, preferred_element_type=jnp.float32
    )
    for k in range(2):
        out_ref[pl.ds(k, times, stride=2)] = mixed[:, k * LANES : (k + 1) * LANES]


def drift(table, columns):
    flat = columns.reshape(-1, LANES)
    mixed = pl.pallas_call(
        drift_kernel,
        out_shape=jax.ShapeDtypeStruct(flat.shape, jnp.float32),
        in_specs=[VMEM] * 2,
        out_specs=VMEM,
        compiler_params=PARAMS,
        name="drift",
    )(table, flat)
    return mixed.reshape(columns.shape)


def join_kernel(half_ref, late_ref, all_ref):
    last = half_ref.shape[0]
    all_ref[pl.ds(0, last)] = half_ref[...]
    all_ref[last] = late_ref[...]


def join_times(half, late):
    return pl.pallas_call(
        join_kernel,
        out_shape=jax.ShapeDtypeStruct((half.shape[0] + 1,) + half.shape[1:], jnp.float32),
        in_specs=[VMEM] * 2,
        out_specs=VMEM,
        compiler_params=PARAMS,
        name="join_times",
    )(half, late)


def add_kernel(ph_ref, back_ref, out_hbm, out_ref, sems):
    slices, rows, columns = ph_ref.shape
    copies = []
    for t in range(slices):
        for r in range(0, rows, 2):
            for c in range(0, columns, LANES):
                moved = back_ref[(r // 2) * (columns // LANES) + c // LANES, pl.ds(2 * t, 2)]
                out_ref[t, pl.ds(r, 2), pl.ds(c, LANES)] = ph_ref[t, pl.ds(r, 2), pl.ds(c, LANES)] + moved
        copies.append(pltpu.make_async_copy(out_ref.at[t], out_hbm.at[t], sems.at[t]))
        copies[t].start()
    for copy in copies:
        copy.wait()


def add_drift(phonons, back):
    return pl.pallas_call(
        add_kernel,
        out_shape=jax.ShapeDtypeStruct(phonons.shape, jnp.float32),
        in_specs=[VMEM] * 2,
        out_specs=pl.BlockSpec(memory_space=pltpu.HBM),
        scratch_shapes=[
            pltpu.VMEM(phonons.shape, jnp.float32),
            pltpu.SemaphoreType.DMA((phonons.shape[0],)),
        ],
        compiler_params=PARAMS,
        name="add_drift",
    )(phonons, back)


def passed_along(block, axis, distance):
    count = lax.axis_size(axis)
    return lax.ppermute(block, axis, [((i - distance) % count, i) for i in range(count)])


def passed_diagonally(block, times, slabs):
    nt, ns = lax.axis_size("tm"), lax.axis_size("slab")
    route = [
        (((i - times) % nt) * ns + (j - slabs) % ns, i * ns + j) for i in range(nt) for j in range(ns)
    ]
    return lax.ppermute(block, ("tm", "slab"), route)


def body(sources, phonons, momenta, kernel, bonds):
    peers = lax.axis_size("tm")
    everyone = peers * lax.axis_size("slab")
    up, down, sources, phonons, bonds, last_momenta = pack_sides(sources, phonons, bonds, momenta)
    above = passed_along(up, "slab", 1)
    below = passed_along(down, "slab", -1)
    ahead = pack_ahead(sources, phonons, last_momenta)
    before = passed_along(ahead, "tm", 1)
    own, corner_slices = lax.optimization_barrier((own_parts(sources, phonons, bonds), ahead))
    up_corner, down_corner = pack_corners(corner_slices)
    above_corner = passed_diagonally(up_corner, 1, 1)
    below_corner = passed_diagonally(down_corner, 1, -1)
    side_halos = (above, below)
    early = early_parts(before, sources, bonds, own)
    (above, below), table, own, early = lax.optimization_barrier((side_halos, circulant(kernel), own, early))
    inner = inner_operators(sources, phonons, bonds, above, below, own)
    outer = outer_operators(before, above_corner, below_corner, early, inner, everyone)
    received = lax.all_to_all(outer[3], ("tm", "slab"), split_axis=0, concat_axis=0, tiled=True)
    half, half_before, send = force(received, sources, inner, outer, phonons, before, momenta, peers)
    columns = lax.all_to_all(send, "tm", split_axis=0, concat_axis=0, tiled=True)
    half_momenta = join_times(half, passed_along(half_before, "tm", -1))
    columns, half_momenta = lax.optimization_barrier((columns, half_momenta))
    mixed = drift(table, columns)
    back = lax.all_to_all(mixed, "tm", split_axis=0, concat_axis=0, tiled=True)
    return half_momenta, add_drift(phonons, back)


def solution(mesh):
    return jax.shard_map(
        body,
        mesh=mesh,
        in_specs=(
            P(None, "tm", "slab", None),
            P("tm", "slab", None),
            P("tm", "slab", None),
            P(),
            P(None, "slab", None),
        ),
        out_specs=(P("tm", "slab", None), P("tm", "slab", None)),
        check_vma=False,
    )
```
